32 devices in a mesh: expert: 8 (over z, y), batch: 4 (over x, core).
Axes of the slice: x: 2, y: 2, z: 4, core: 2. Of those that a mesh axis runs over, the one named last changes fastest.
Arguments:
- tokens: bfloat16 [8192, 1024], P(('expert', 'batch')), may hold values from -6 to 6
- lengths: int32 [32], P(('expert', 'batch')), may hold values from 64 to 256, as said below
- expert_ids: int32 [8192], P(('expert', 'batch')), may hold values from 0 to 7, as said below
- slots: int32 [8192], P(('expert', 'batch')), may hold values from -1 to 31, as said below
- centroids: bfloat16 [8, 1024], replicated, may hold values from -0.125 to 0.125
- sublayer_norm_gain: bfloat16 [2, 8, 1024], P(None, 'expert'), may hold values from 0.5 to 1.5
- sublayer_norm_bias: bfloat16 [2, 8, 1024], P(None, 'expert'), may hold values from -0.59765625 to 0.59765625
- up_weight: bfloat16 [2, 8, 1024, 4096], P(None, 'expert', None, 'batch'), may hold values from -0.1875 to 0.1875
- up_bias: bfloat16 [2, 8, 4096], P(None, 'expert', 'batch'), may hold values from -0.59765625 to 0.59765625
- down_weight: bfloat16 [2, 8, 4096, 1024], P(None, 'expert', 'batch'), may hold values from -0.09375 to 0.09375
- down_bias: bfloat16 [2, 8, 1024], P(None, 'expert'), may hold values from -0.59765625 to 0.59765625
- cotangent: bfloat16 [8192, 1024], P(('expert', 'batch')), may hold values from -6 to 6
Outputs:
- mixed: bfloat16 [8192, 1024], P(('expert', 'batch'))
- tokens_grad: bfloat16 [8192, 1024], P(('expert', 'batch'))
- centroid_grad: float32 [8, 1024], replicated
- gain_grad: float32 [2, 8, 1024], P(None, 'expert')
- shift_grad: float32 [2, 8, 1024], P(None, 'expert')
- up_weight_grad: float32 [2, 8, 1024, 4096], P(None, 'expert', None, 'batch')
- up_bias_grad: float32 [2, 8, 4096], P(None, 'expert', 'batch')
- down_weight_grad: float32 [2, 8, 4096, 1024], P(None, 'expert', 'batch')
- down_bias_grad: float32 [2, 8, 1024], P(None, 'expert')
- gate_mass: float32 [8], replicated
- load: float32 [8], replicated
The draws below stay inside these ranges and needn't reach their ends.
Inputs may be any that keep to these rules, and one draw needn't show every extreme that they name: `lengths`: one device's sequence has length 256 and one has 64. `expert_ids`: every expert is named somewhere. -1 exactly at padded positions; a device's live positions of one expert have distinct slots; some expert receives 32 positions from every device.
All inputs are finite; a program needn't handle non-finite values.
Results may differ from the reference program's by a relative error of at most 0.017.
Values may be sent and summed in bfloat16 or wider, within the bound.
A program may use at most 128 MiB of HBM per device.

```python
import jax
import jax.numpy as jnp
from jax import lax

D = 1024
FF = 4096
SUBLAYERS = 2
TOK_DEV = 256
MIN_LEN = 64
EXPERTS = 8
CAP = 32
TOKENS = 8192
N_BATCH = 4


def routing(key):
    devices = TOKENS // TOK_DEV
    capacity = TOK_DEV // EXPERTS
    rank = jnp.arange(devices, dtype=jnp.int32)
    jitter = jax.random.randint(jax.random.fold_in(key, 2), (devices,), 128, 256)
    lengths = MIN_LEN + (TOK_DEV - MIN_LEN) * rank * jitter // ((devices - 1) * 255)
    lengths = jnp.clip(lengths, MIN_LEN, TOK_DEV)
    lengths = lengths.at[0].set(MIN_LEN).at[devices - 1].set(TOK_DEV).astype(jnp.int32)
    tiers = jax.random.randint(jax.random.fold_in(key, 3), (EXPERTS,), 0, 3)
    favoured = jax.random.randint(jax.random.fold_in(key, 4), (), 0, EXPERTS)
    slot_index = jnp.arange(TOK_DEV, dtype=jnp.int32)
    expert_of_slot = slot_index // capacity
    weighting = tiers[expert_of_slot] * 512 + jnp.where(expert_of_slot == favoured, 4096, 0)
    noise = jax.random.randint(jax.random.fold_in(key, 5), (devices, TOK_DEV), 0, 1024)
    score = (weighting[None, :] + noise) * TOK_DEV + slot_index[None, :]
    slot_order = jnp.argsort(-score, axis=1).astype(jnp.int32)
    mixing = jax.random.randint(jax.random.fold_in(key, 6), (devices, TOK_DEV), 0, 1024) * TOK_DEV + slot_index[None, :]
    padded = (slot_index[None, :] >= lengths[:, None]).astype(jnp.int32)
    token_order = jnp.argsort(padded * (1024 * TOK_DEV) + mixing, axis=1).astype(jnp.int32)
    assigned = jax.vmap(lambda order, places: jnp.zeros((TOK_DEV,), jnp.int32).at[order].set(places))(token_order, slot_order)
    identity = (assigned // capacity).reshape(-1).astype(jnp.int32)
    placing = jnp.where(padded == 1, -1, assigned % capacity).reshape(-1).astype(jnp.int32)
    return (lengths, identity, placing)


def draw_lengths(key, part):
    return routing(key)[0]


def draw_expert_ids(key, part):
    return routing(key)[1]


def draw_slots(key, part):
    return routing(key)[2]


def block_levels(rng, extent, pieces, least, high):
    loudness, own = 1.0, jax.random.fold_in(rng, 6)
    for axis_at, shards_of in pieces:
        draws = jnp.exp(jax.random.uniform(jax.random.fold_in(own, axis_at), (shards_of,), jnp.float32, least / len(pieces), high / len(pieces)))
        loudness = loudness * jnp.repeat(draws, extent[axis_at] // shards_of).reshape([-1 if axis == axis_at else 1 for axis in range(len(extent))])
    return loudness


def normal_values(rng, extent, scale, limit, pieces=(), kind=jnp.bfloat16):
    level = block_levels(rng, extent, pieces, -0.22, 0.18) if pieces else 1.0
    result = jax.random.normal(rng, extent, jnp.float32) * scale * level
    return jnp.minimum(jnp.maximum(result, -limit), limit).astype(kind)


def setup_inputs(seed: int = 0) -> dict:
    streams_of = jax.random.split(jax.random.key(seed), 13)
    tokens = normal_values(streams_of[0], (TOKENS, D), 1.0, 6.0, ((0, 32),))
    lengths = draw_lengths(jax.random.fold_in(streams_of[12], 71), 0)
    expert_ids = draw_expert_ids(jax.random.fold_in(streams_of[12], 71), 0)
    slots = draw_slots(jax.random.fold_in(streams_of[12], 71), 0)
    centroids = normal_values(streams_of[4], (EXPERTS, D), (2 * D) ** -0.5, 0.125)
    sublayer_norm_gain = jnp.clip(1.0 + 0.1 * jax.random.normal(streams_of[5], (SUBLAYERS, EXPERTS, D), jnp.float32), 0.5, 1.5).astype(jnp.bfloat16)
    sublayer_norm_bias = normal_values(streams_of[6], (SUBLAYERS, EXPERTS, D), 0.1, 0.59765625, ((1, 8),))
    up_weight = normal_values(streams_of[7], (SUBLAYERS, EXPERTS, D, FF), D ** -0.5, 0.1875, ((1, 8), (3, 4)))
    up_bias = normal_values(streams_of[8], (SUBLAYERS, EXPERTS, FF), 0.1, 0.59765625, ((1, 8), (2, 4)))
    down_weight = normal_values(streams_of[9], (SUBLAYERS, EXPERTS, FF, D), FF ** -0.5, 0.09375, ((1, 8), (2, 4)))
    down_bias = normal_values(streams_of[10], (SUBLAYERS, EXPERTS, D), 0.1, 0.59765625, ((1, 8),))
    cotangent = normal_values(streams_of[11], (TOKENS, D), 1.0, 6.0, ((0, 32),))
    return dict(tokens=tokens, lengths=lengths, expert_ids=expert_ids, slots=slots, centroids=centroids, sublayer_norm_gain=sublayer_norm_gain, sublayer_norm_bias=sublayer_norm_bias, up_weight=up_weight, up_bias=up_bias, down_weight=down_weight, down_bias=down_bias, cotangent=cotangent)


@jax.custom_vjp
def low(v):
    return lax.optimization_barrier(v.astype(jnp.bfloat16)).astype(jnp.float32)

@jax.custom_vjp
def low_back(v):
    return v

def low_keep(v):
    return (low(v), None)

def low_pass(kept, grad):
    return (grad,)

def back_keep(v):
    return (v, None)

def back_low(kept, grad):
    return (low(grad),)
low.defvjp(low_keep, low_pass)
low_back.defvjp(back_keep, back_low)

def layer_norm(row_data, gain, shift):
    row_mean = lax.optimization_barrier(jnp.mean(row_data, axis=-1, keepdims=True))
    centered = row_data - row_mean
    variance = lax.optimization_barrier(jnp.mean(centered * centered, axis=-1, keepdims=True))
    return centered * lax.rsqrt(variance + 1e-05) * gain + shift

def sublayer(row_data, gain, shift, w_up, b_up, w_down, b_down):
    normed = low(layer_norm(row_data, gain, shift))
    piece_width = w_up.shape[1] // N_BATCH
    totals = jnp.zeros(row_data.shape, jnp.float32)
    for portion in range(N_BATCH):
        first_col = portion * piece_width
        w_in = lax.slice_in_dim(w_up, first_col, first_col + piece_width, axis=1)
        b_in = lax.slice_in_dim(b_up, first_col, first_col + piece_width, axis=0)
        w_out = lax.slice_in_dim(w_down, first_col, first_col + piece_width, axis=0)
        pre_act = low_back(jnp.dot(low_back(normed), w_in, precision=lax.Precision.HIGHEST) + b_in)
        activity = low(jax.nn.gelu(pre_act, approximate=False))
        totals = totals + low(jnp.dot(activity, w_out, precision=lax.Precision.HIGHEST))
    return row_data + totals + b_down

def expert_rows(row_data, gains, shifts, w_ups, b_ups, w_downs, b_downs):
    for expert_layer_step in range(SUBLAYERS):
        if expert_layer_step > 0:
            row_data = low(low_back(row_data))
        row_data = sublayer(row_data, gains[expert_layer_step], shifts[expert_layer_step], w_ups[expert_layer_step], b_ups[expert_layer_step], w_downs[expert_layer_step], b_downs[expert_layer_step])
    return row_data

def forward(tokens, centroids, sublayer_norm_gain, sublayer_norm_bias, up_weight, up_bias, down_weight, down_bias, row_table, token_row, onehot, live):
    extended = jnp.concatenate([tokens, jnp.zeros((1, tokens.shape[1]), jnp.float32)], axis=0)

    def one_expert(inputs):
        index_list, gains, shifts, w_ups, b_ups, w_downs, b_downs = inputs
        row_data = low_back(extended[index_list])
        return expert_rows(row_data, gains, shifts, w_ups, b_ups, w_downs, b_downs)
    stacked = tuple((jnp.moveaxis(array, 1, 0) for array in (sublayer_norm_gain, sublayer_norm_bias, up_weight, up_bias, down_weight, down_bias)))
    expert_out = lax.map(jax.checkpoint(one_expert), (row_table,) + stacked)
    expert_out = low(low_back(expert_out.reshape(-1, tokens.shape[1])))
    returned = expert_out[token_row]
    logits = jnp.dot(tokens, centroids.T, precision=lax.Precision.HIGHEST)
    chosen = low_back(lax.optimization_barrier(jnp.sum(logits * onehot, axis=1)))
    gate = jax.nn.sigmoid(chosen)
    mixed = live[:, None] * (tokens + gate[:, None] * returned)
    return (mixed, gate)

def reference(tokens, lengths, expert_ids, slots, centroids, sublayer_norm_gain, sublayer_norm_bias, up_weight, up_bias, down_weight, down_bias, cotangent):
    sequences = TOKENS // TOK_DEV
    position = jnp.arange(TOKENS, dtype=jnp.int32)
    owner = (position // TOK_DEV).astype(jnp.int32)
    live = (position % TOK_DEV < lengths[owner]).astype(jnp.float32)
    per_expert = sequences * CAP
    row_total = EXPERTS * per_expert
    token_row = jnp.where(slots >= 0, expert_ids * per_expert + owner * CAP + slots, row_total).astype(jnp.int32)
    row_table = jnp.full((row_total + 1,), TOKENS, jnp.int32).at[token_row].set(position)[:row_total]
    row_table = row_table.reshape(EXPERTS, per_expert).astype(jnp.int32)
    onehot = (expert_ids[:, None] == jnp.arange(EXPERTS, dtype=jnp.int32)[None, :]).astype(jnp.float32)
    safe_row = jnp.minimum(token_row, row_total - 1).astype(jnp.int32)
    floats = tuple((array.astype(jnp.float32) for array in (tokens, centroids, sublayer_norm_gain, sublayer_norm_bias, up_weight, up_bias, down_weight, down_bias)))

    def closed(*params):
        return forward(*params, row_table, safe_row, onehot, live)
    mixed, pullback, gate = jax.vjp(closed, *floats, has_aux=True)
    grads = pullback(cotangent.astype(jnp.float32))
    used = onehot * live[:, None]
    denominator = jnp.float32(CAP * sequences)
    gate_mass = lax.optimization_barrier(jnp.sum(used * gate[:, None], axis=0)) / denominator
    load = lax.optimization_barrier(jnp.sum(used, axis=0)) / denominator
    return (mixed.astype(jnp.bfloat16), grads[0].astype(jnp.bfloat16), grads[1], grads[2], grads[3], grads[4], grads[5], grads[6], grads[7], gate_mass, load)
```

```python
import functools

import jax
import jax.numpy as jnp
from jax import lax
from jax.experimental import pallas as pl
from jax.experimental.pallas import tpu as pltpu
from jax.sharding import PartitionSpec as P


def gelu_exact(values):
    return jax.nn.gelu(values, approximate=False)


def apply_layer_norm(row_block):
    values = row_block.astype(jnp.float32)
    row_mean = jnp.mean(values, axis=-1, keepdims=True)
    centered = values - row_mean
    row_inverse_scale = lax.rsqrt(jnp.mean(centered * centered, axis=-1, keepdims=True) + 1e-05)
    return (centered * row_inverse_scale, row_inverse_scale)


def per_device(
    tokens,
    lengths,
    expert_ids,
    slots,
    centroids,
    sublayer_norm_gain,
    sublayer_norm_bias,
    up_weight,
    up_bias,
    down_weight,
    down_bias,
    cotangent,
):
    tok_rows, width = tokens.shape
    layers = sublayer_norm_gain.shape[0]
    local_count = up_weight.shape[1]
    expert_count = centroids.shape[0]
    capacity = tok_rows // expert_count
    groups = lax.axis_size("expert")
    batches = lax.axis_size("batch")
    position = jnp.arange(tok_rows, dtype=jnp.int32)
    live = (position < lengths[0]).astype(jnp.float32)[:, None]
    target = jnp.where(slots >= 0, expert_ids * capacity + slots, tok_rows)
    source = jnp.full((tok_rows + 1,), -1, jnp.int32).at[target].set(position)[:tok_rows]
    filled = (source >= 0)[:, None]
    safe_source = jnp.maximum(source, 0)
    safe_target = jnp.minimum(target, tok_rows - 1)

    def pack(values):
        return jnp.where(filled, values[safe_source], jnp.zeros((), values.dtype))

    onehot = (expert_ids[:, None] == jnp.arange(expert_count, dtype=jnp.int32)[None, :]).astype(
        jnp.float32
    )
    logits = jnp.einsum("td,ed->te", tokens, centroids, preferred_element_type=jnp.float32)
    gate = jax.nn.sigmoid(jnp.sum(logits * onehot, axis=1))[:, None]
    used = onehot * live
    usage_gate = jnp.sum(used * gate, axis=0)
    usage_count = jnp.sum(used, axis=0)
    gate_total, count_total = lax.psum((usage_gate, usage_count), ("expert", "batch"))

    def expand_hidden(values, expert_layer_step):
        return values[expert_layer_step].astype(jnp.float32)[None, :, None, :]

    arrived = lax.all_to_all(pack(tokens), "expert", split_axis=0, concat_axis=0, tiled=True)
    current = arrived
    inputs = []
    kept = []
    for expert_layer_step in range(layers):
        gathered = lax.all_gather(current, "batch", axis=0, tiled=True)
        row_layout_grid = gathered.reshape(-1, local_count, capacity, width)
        standardized_input, row_inverse_scale = apply_layer_norm(row_layout_grid)
        normalized_rows = (
            standardized_input * expand_hidden(sublayer_norm_gain, expert_layer_step)
            + expand_hidden(sublayer_norm_bias, expert_layer_step)
        ).astype(jnp.bfloat16)
        pre_rows = jnp.einsum(
            "nlcd,ldf->nlcf",
            normalized_rows,
            up_weight[expert_layer_step],
            preferred_element_type=jnp.float32,
        ) + expand_hidden(up_bias, expert_layer_step)
        hidden_parts = (normalized_rows, pre_rows, gelu_exact(pre_rows).astype(jnp.bfloat16))

        def down_part(start, count, activity=hidden_parts[2], expert_layer_step=expert_layer_step):
            return jnp.einsum(
                "nlcf,lfd->nlcd",
                activity,
                down_weight[expert_layer_step],
                preferred_element_type=jnp.float32,
            )

        mixed_part = lax.psum_scatter(
            down_part(jnp.int32(0), lax.axis_size("batch") * groups).astype(jnp.bfloat16),
            "batch",
            scatter_dimension=0,
            tiled=True,
        ).astype(jnp.float32)
        own_grid = current.reshape(groups, local_count, capacity, width).astype(jnp.float32)
        result = (own_grid + mixed_part + expand_hidden(down_bias, expert_layer_step)).astype(
            jnp.bfloat16
        )
        inputs.append(current)
        kept.append(hidden_parts)
        current = result.reshape(tok_rows, width)
    returned = lax.all_to_all(current, "expert", split_axis=0, concat_axis=0, tiled=True)
    expert_tok = returned[safe_target].astype(jnp.float32)
    mixed = (live * (tokens.astype(jnp.float32) + gate * expert_tok)).astype(jnp.bfloat16)
    upstream = cotangent.astype(jnp.float32) * live
    gate_grad = jnp.sum(upstream * expert_tok, axis=1, keepdims=True)
    logit_grad = (gate_grad * gate * (1.0 - gate)).astype(jnp.bfloat16)
    route_grad = (onehot * logit_grad.astype(jnp.float32)).astype(jnp.bfloat16)
    centroid_part = jnp.einsum("te,td->ed", route_grad, tokens, preferred_element_type=jnp.float32)
    gate_input = jnp.einsum("te,ed->td", route_grad, centroids, preferred_element_type=jnp.float32)
    expert_grad = (gate * upstream).astype(jnp.bfloat16)
    grad_rows = lax.all_to_all(pack(expert_grad), "expert", split_axis=0, concat_axis=0, tiled=True)
    gain_parts = [None] * layers
    shift_parts = [None] * layers
    down_bias_parts = [None] * layers
    up_weight_grads = [None] * layers
    up_bias_grads = [None] * layers
    down_weight_grads = [None] * layers
    for expert_layer_step in range(layers - 1, -1, -1):
        own_rows = inputs[expert_layer_step]
        grads_all = lax.all_gather(grad_rows, "batch", axis=0, tiled=True).reshape(
            -1, local_count, capacity, width
        )
        normed, pre_act, activity = kept[expert_layer_step]
        act_grad = jnp.einsum(
            "nlcd,lfd->nlcf",
            grads_all,
            down_weight[expert_layer_step],
            preferred_element_type=jnp.float32,
        )
        pre_grad = jax.vjp(gelu_exact, pre_act)[1](act_grad)[0].astype(jnp.bfloat16)
        down_weight_grads[expert_layer_step] = jnp.einsum(
            "nlcf,nlcd->lfd", activity, grads_all, preferred_element_type=jnp.float32
        )
        up_weight_grads[expert_layer_step] = jnp.einsum(
            "nlcd,nlcf->ldf", normed, pre_grad, preferred_element_type=jnp.float32
        )
        up_bias_grads[expert_layer_step] = jnp.sum(pre_grad.astype(jnp.float32), axis=(0, 2))

        def up_part(start, count, pre_grad=pre_grad, expert_layer_step=expert_layer_step):
            return jnp.einsum(
                "nlcf,ldf->nlcd",
                pre_grad,
                up_weight[expert_layer_step],
                preferred_element_type=jnp.float32,
            )

        normed_grad = lax.psum_scatter(
            up_part(jnp.int32(0), lax.axis_size("batch") * groups).astype(jnp.bfloat16),
            "batch",
            scatter_dimension=0,
            tiled=True,
        ).astype(jnp.float32)
        out_grad = grad_rows.reshape(groups, local_count, capacity, width).astype(jnp.float32)
        down_bias_parts[expert_layer_step] = jnp.sum(out_grad, axis=(0, 2))
        own_hat, own_scale = apply_layer_norm(
            own_rows.reshape(groups, local_count, capacity, width)
        )
        gain_parts[expert_layer_step] = jnp.sum(normed_grad * own_hat, axis=(0, 2))
        shift_parts[expert_layer_step] = jnp.sum(normed_grad, axis=(0, 2))
        hat_grad = normed_grad * expand_hidden(sublayer_norm_gain, expert_layer_step)
        row_grad = own_scale * (
            hat_grad
            - jnp.mean(hat_grad, axis=-1, keepdims=True)
            - own_hat * jnp.mean(hat_grad * own_hat, axis=-1, keepdims=True)
        )
        grad_rows = (out_grad + row_grad).astype(jnp.bfloat16).reshape(tok_rows, width)
    gain_grad, shift_grad, down_bias_grad = lax.psum(
        (jnp.stack(gain_parts), jnp.stack(shift_parts), jnp.stack(down_bias_parts)), "batch"
    )
    token_back = lax.all_to_all(grad_rows, "expert", split_axis=0, concat_axis=0, tiled=True)
    tokens_grad = (
        upstream + gate_input + live * token_back[safe_target].astype(jnp.float32)
    ).astype(jnp.bfloat16)
    centroid_grad = lax.psum(centroid_part, ("expert", "batch"))
    denominator = jnp.float32(capacity * groups * batches)
    gate_mass = gate_total / denominator
    load = count_total / denominator
    return (
        mixed,
        tokens_grad,
        centroid_grad,
        gain_grad,
        shift_grad,
        jnp.stack(up_weight_grads),
        jnp.stack(up_bias_grads),
        jnp.stack(down_weight_grads),
        down_bias_grad,
        gate_mass,
        load,
    )


MESH = pl.DeviceIdType.MESH
F32 = jnp.float32
BF16 = jnp.bfloat16
ROW_STEP = 32
COL_STEP = 256
EMPTY = 8.0
LINK_KINDS = ("x", "g", "sum0", "out", "ngrad1", "ngrad0")
CORE_KINDS = ("x", "g", "part0", "h", "part1", "ngrad1", "hgrad", "ngrad0")
ROUTE_KINDS = ("x", "ct", "mixed", "tgrad", "totals")


def fused_fits(mesh):
    groups, batches = mesh.shape["expert"], mesh.shape["batch"]
    return batches == 4 and groups == 8


def rows_at(start, count, unit):
    return pl.ds(pl.multiple_of(start, unit), count)


def loop_rows(count, step, body):
    def one(i, carry):
        body(i * step, step)
        return carry

    lax.fori_loop(0, count // step, one, 0)


def normalize(values):
    centered = values - jnp.mean(values, axis=-1, keepdims=True)
    scale = lax.rsqrt(jnp.mean(centered * centered, axis=-1, keepdims=True) + 1e-05)
    return centered * scale, scale


def dot(a, b, dims):
    return lax.dot_general(a, b, (dims, ((), ())), preferred_element_type=F32)


NN = ((1,), (0,))
NT = ((1,), (1,))
TN = ((0,), (0,))


def fused_kernel(
    groups,
    capacity,
    chunks,
    ids_ref,
    slots_ref,
    tok_ref,
    ct_ref,
    cent_ref,
    gain_ref,
    bias_ref,
    up_bias_ref,
    down_bias_ref,
    up_hbm,
    down_hbm,
    mixed_ref,
    tgrad_ref,
    totals_ref,
    small_ref,
    ub_ref,
    up_grad_hbm,
    down_grad_hbm,
    up_w,
    down_w,
    perm,
    pack_x,
    pack_ct,
    xa,
    ga,
    ha,
    hga,
    n_s,
    a_s,
    d_s,
    part,
    part_in,
    half_out,
    half_in,
    own_out,
    own_in,
    ct_own,
    gate_s,
    lg_s,
    back_out,
    back_in,
    stage,
    acc,
    red,
    totals_in,
    w_sem,
    route_send,
    route_recv,
    link_send,
    link_recv,
    core_send,
    core_recv,
    red_send,
    red_recv,
    out_sem,
):
    tok_rows, width = tok_ref.shape
    hidden = up_w.shape[2]
    per = groups // chunks
    rows_m = per * 4 * capacity
    rows_h = rows_m // 2
    rows_o = rows_m // 4
    e = lax.axis_index("expert")
    b = lax.axis_index("batch")
    x = b // 2
    c = lax.rem(b, 2)
    sib = (e, x * 2 + (1 - c))
    far = (e, (1 - x) * 2 + c)

    def flipped(m):
        out = jnp.int32(0)
        bit = 1
        while bit < groups:
            digit = lax.rem(e // bit, 2)
            out = out + bit * ((1 - digit) if m & bit else digit)
            bit *= 2
        return out

    half = c * rows_h
    sib_half = (1 - c) * rows_h
    own = half + x * rows_o
    pairs = [tuple(range(j * per, (j + 1) * per)) for j in range(chunks)]
    order = [pairs[0]] + pairs[2:] + [pairs[1]]
    place = {m: (k, i) for k, ms in enumerate(order) for i, m in enumerate(ms)}
    order_flat = [m for ms in order for m in ms]

    def at_half(k):
        return rows_at(k * rows_m + half, rows_h, rows_h)

    def at_sib_half(k):
        return rows_at(k * rows_m + sib_half, rows_h, rows_h)

    def at_own(k):
        return rows_at(k * rows_m + own, rows_o, rows_o)

    def at_all(k):
        return pl.ds(k * rows_m, rows_m)

    def copy_to(device, src, dst, send, recv):
        return pltpu.make_async_remote_copy(
            src_ref=src,
            dst_ref=dst,
            send_sem=send,
            recv_sem=recv,
            device_id=device,
            device_id_type=MESH,
        )

    def route(kind, m):
        n = ROUTE_KINDS.index(kind)
        k, i = place[m]
        to = flipped(m)
        theirs = rows_at(to * capacity, capacity, capacity)
        mine = rows_at(e * capacity, capacity, capacity)
        if kind == "x":
            src = pack_x.at[theirs]
            dst = xa.at[rows_at(k * rows_m + own + i * capacity, capacity, capacity)]
        elif kind == "ct":
            src = pack_ct.at[theirs]
            dst = ct_own.at[pl.ds(k * rows_o + i * capacity, capacity)]
        elif kind == "totals":
            src = red.at[0]
            dst = totals_in.at[e]
        else:
            s = 0 if kind == "mixed" else 1
            src = back_out.at[s, pl.ds(k * rows_o + i * capacity, capacity)]
            dst = back_in.at[s, mine]
        return copy_to((to, b), src, dst, route_send.at[n, m], route_recv.at[n, m])

    def link(kind, k):
        n = LINK_KINDS.index(kind)
        if kind == "x":
            src = dst = xa.at[at_own(k)]
        elif kind == "g":
            src = dst = ga.at[at_own(k)]
        elif kind in ("sum0", "ngrad1"):
            s = 0 if kind == "sum0" else 1
            at = pl.ds(k * rows_h, rows_h)
            src, dst = half_out.at[s, at], half_in.at[s, at]
        else:
            s = 0 if kind == "out" else 1
            at = pl.ds(k * rows_o, rows_o)
            src, dst = own_out.at[s, at], own_in.at[s, at]
        return copy_to(far, src, dst, link_send.at[n, k], link_recv.at[n, k])

    def core(kind, k):
        n = CORE_KINDS.index(kind)
        whole = {"x": xa, "g": ga, "h": ha, "hgrad": hga}
        if kind in whole:
            src = dst = whole[kind].at[at_half(k)]
        else:
            s = ("part0", "part1", "ngrad1", "ngrad0").index(kind)
            src = part.at[s, at_sib_half(k)]
            dst = part_in.at[s, pl.ds(k * rows_h, rows_h)]
        return copy_to(sib, src, dst, core_send.at[n, k], core_recv.at[n, k])

    barrier = pltpu.get_barrier_semaphore()
    peers = [sib, far] + [(flipped(m), b) for m in range(1, groups)]
    for peer in peers:
        pl.semaphore_signal(barrier, inc=1, device_id=peer, device_id_type=MESH)
    loads = []
    for j in range(2):
        loads.append(pltpu.make_async_copy(up_hbm.at[j, 0], up_w.at[j], w_sem.at[2 * j]))
        loads.append(pltpu.make_async_copy(down_hbm.at[j, 0], down_w.at[j], w_sem.at[2 * j + 1]))
    for load in loads:
        load.start()
    target = jnp.where(
        slots_ref[...] >= 0, ids_ref[...] * capacity + slots_ref[...], -1
    )
    slot = lax.broadcasted_iota(jnp.int32, (tok_rows, tok_rows), 0)
    onehot = jnp.where(slot == target, 1.0, 0.0)
    perm[...] = onehot.astype(BF16)
    empty = EMPTY * (1.0 - jnp.sum(onehot, axis=1, keepdims=True))

    def pack(start, step):
        cols = rows_at(start, step, step)
        pack_x[:, cols] = (dot(perm[...], tok_ref[:, cols], NN) + empty).astype(BF16)
        pack_ct[:, cols] = dot(perm[...], ct_ref[:, cols], NN).astype(BF16)

    loop_rows(width, COL_STEP, pack)
    acc[...] = jnp.zeros_like(acc)
    cent_rows = cent_ref[...].astype(F32)
    cent_at = lax.broadcasted_iota(jnp.int32, cent_rows.shape, 0)
    cent = jnp.sum(jnp.where(cent_at == e, cent_rows, 0.0), axis=0, keepdims=True)
    pl.semaphore_wait(barrier, len(peers))
    for kind in ("x", "ct"):
        for m in order_flat[1:]:
            route(kind, m).start()
    mine = rows_at(e * capacity, capacity, capacity)
    xa[rows_at(own, capacity, capacity)] = pack_x[mine]
    ct_own[pl.ds(0, capacity)] = pack_ct[mine]

    def send_x(k):
        for m in order[k]:
            if m:
                route("x", m).wait_recv()
        link("x", k).start()

    def send_g(k):
        for m in order[k]:
            if m:
                route("ct", m).wait_recv()

        def gated(start, step):
            at = rows_at(k * rows_m + own + start, step, step)
            at_o = rows_at(k * rows_o + start, step, step)
            values = xa[at].astype(F32)
            logit = jnp.sum(values * cent, axis=-1, keepdims=True)
            gate = jax.nn.sigmoid(logit)
            gate_s[at_o] = jnp.broadcast_to(gate, (step, 128))
            ga[at] = (gate * ct_own[at_o].astype(F32)).astype(BF16)
            used = jnp.where(values[:, 0:1] < 7.0, 1.0, 0.0)
            acc[5:6] += jnp.broadcast_to(
                jnp.sum(used * gate, axis=0, keepdims=True), (1, width)
            )
            acc[6:7] += jnp.broadcast_to(jnp.sum(used, axis=0, keepdims=True), (1, width))

        loop_rows(rows_o, ROW_STEP, gated)
        link("g", k).start()

    def spread(kind, k):
        link(kind, k).wait_recv()
        core(kind, k).start()

    def up_step(j, rows_ref, k):
        gain = gain_ref[j].astype(F32)
        bias = bias_ref[j].astype(F32)

        def norm(start, step):
            at = rows_at(k * rows_m + start, step, step)
            rhat, _ = normalize(rows_ref[at].astype(F32))
            n_s[j, at] = (rhat * gain + bias).astype(BF16)

        loop_rows(rows_m, ROW_STEP, norm)

        def up(start, step):
            cols = rows_at(start, step, step)
            pre = dot(n_s[j, at_all(k)], up_w[j, :, cols], NN) + up_bias_ref[j, :, cols].astype(
                F32
            )
            cdf = 0.5 * (1.0 + lax.erf(pre * (0.5**0.5)))
            pdf = jnp.exp(-0.5 * pre * pre) * 0.3989422804014327
            a_s[j, at_all(k), cols] = (pre * cdf).astype(BF16)
            d_s[j, at_all(k), cols] = (cdf + pre * pdf).astype(BF16)

        loop_rows(hidden, COL_STEP, up)

    def down_step(j, k):
        kind = "part%d" % j

        def down(start, step):
            cols = rows_at(start, step, step)
            part[j, at_all(k), cols] = dot(a_s[j, at_all(k)], down_w[j, :, cols], NN).astype(BF16)

        loop_rows(width, COL_STEP, down)
        core(kind, k).start()

    def back_step(j, grads_ref, k):
        kind = "ngrad%d" % j
        s = 3 - j

        def act(start, step):
            cols = rows_at(start, step, step)
            grad = dot(grads_ref[at_all(k)], down_w[j, cols, :], NT)
            d_s[j, at_all(k), cols] = (grad * d_s[j, at_all(k), cols].astype(F32)).astype(BF16)

        loop_rows(hidden, COL_STEP, act)

        def up(start, step):
            cols = rows_at(start, step, step)
            part[s, at_all(k), cols] = dot(d_s[j, at_all(k)], up_w[j, cols, :], NT).astype(BF16)

        loop_rows(width, COL_STEP, up)
        core(kind, k).start()

    def sum_half(kind, link_kind, k):
        s = ("part0", "part1", "ngrad1", "ngrad0").index(kind)
        o = ("sum0", "ngrad1").index(link_kind)
        core(kind, k).wait_recv()

        def add(start, step):
            at = rows_at(k * rows_m + half + start, step, step)
            at_h = rows_at(k * rows_h + start, step, step)
            total = part[s, at].astype(F32) + part_in[s, at_h].astype(F32)
            half_out[o, at_h] = total.astype(BF16)

        loop_rows(rows_h, ROW_STEP, add)
        link(link_kind, k).start()

    def sum_far(kind, link_kind, k):
        s = ("part0", "part1", "ngrad1", "ngrad0").index(kind)
        o = ("out", "ngrad0").index(link_kind)
        core(kind, k).wait_recv()

        def add(start, step):
            at = rows_at(k * rows_m + half + (1 - x) * rows_o + start, step, step)
            at_h = rows_at(k * rows_h + (1 - x) * rows_o + start, step, step)
            at_o = rows_at(k * rows_o + start, step, step)
            total = part[s, at].astype(F32) + part_in[s, at_h].astype(F32)
            own_out[o, at_o] = total.astype(BF16)

        loop_rows(rows_o, ROW_STEP, add)
        link(link_kind, k).start()

    def sum_own(s, o, k, start, step):
        at = rows_at(k * rows_m + own + start, step, step)
        at_h = rows_at(k * rows_h + x * rows_o + start, step, step)
        at_o = rows_at(k * rows_o + start, step, step)
        mine = part[s, at].astype(F32) + part_in[s, at_h].astype(F32)
        return mine + own_in[o, at_o].astype(F32)

    def make_h(k):
        link("sum0", k).wait_recv()
        shift = down_bias_ref[0].astype(F32)

        def add(start, step):
            at = rows_at(k * rows_m + half + start, step, step)
            at_h = rows_at(k * rows_h + start, step, step)
            total = half_out[0, at_h].astype(F32) + half_in[0, at_h].astype(F32)
            ha[at] = (xa[at].astype(F32) + total + shift).astype(BF16)

        loop_rows(rows_h, ROW_STEP, add)
        core("h", k).start()

    def norm_back(rows, ngrad, gain):
        rhat, scale = normalize(rows)
        q = ngrad * gain
        back = scale * (
            q - jnp.mean(q, axis=-1, keepdims=True) - rhat * jnp.mean(q * rhat, axis=-1, keepdims=True)
        )
        return back, rhat

    def make_hgrad(k):
        link("ngrad1", k).wait_recv()
        gain = gain_ref[1].astype(F32)

        def grad(start, step):
            at = rows_at(k * rows_m + half + start, step, step)
            at_h = rows_at(k * rows_h + start, step, step)
            ngrad = half_out[1, at_h].astype(F32) + half_in[1, at_h].astype(F32)
            back, rhat = norm_back(ha[at].astype(F32), ngrad, gain)
            hga[at] = (ga[at].astype(F32) + back).astype(BF16)
            acc[1:2] += 0.5 * jnp.sum(ngrad * rhat, axis=0, keepdims=True)
            acc[3:4] += 0.5 * jnp.sum(ngrad, axis=0, keepdims=True)

        loop_rows(rows_h, ROW_STEP, grad)
        core("hgrad", k).start()

    def give_back(kind, k):
        for m in order[k]:
            if m:
                route(kind, m).start()
            else:
                s = 0 if kind == "mixed" else 1
                _, i = place[0]
                back_in[s, mine] = back_out[s, pl.ds(k * rows_o + i * capacity, capacity)]

    def make_mixed(k):
        link("out", k).wait_recv()
        shift = down_bias_ref[1].astype(F32)

        def mix(start, step):
            at = rows_at(k * rows_m + own + start, step, step)
            at_o = rows_at(k * rows_o + start, step, step)
            out = (ha[at].astype(F32) + sum_own(1, 0, k, start, step) + shift).astype(BF16).astype(F32)
            rows = xa[at].astype(F32)
            gate = gate_s[at_o][:, 0:1]
            back_out[0, at_o] = (rows + gate * out).astype(BF16)
            along = jnp.sum(ct_own[at_o].astype(F32) * out, axis=-1, keepdims=True)
            lgrad = (along * gate * (1.0 - gate)).astype(BF16).astype(F32)
            lg_s[at_o] = jnp.broadcast_to(lgrad, (step, 128))
            acc[4:5] += jnp.sum(lgrad * rows, axis=0, keepdims=True)

        loop_rows(rows_o, ROW_STEP, mix)
        give_back("mixed", k)

    def make_tgrad(k):
        link("ngrad0", k).wait_recv()
        gain = gain_ref[0].astype(F32)

        def grad(start, step):
            at = rows_at(k * rows_m + own + start, step, step)
            at_o = rows_at(k * rows_o + start, step, step)
            ngrad = sum_own(3, 1, k, start, step)
            back, rhat = norm_back(xa[at].astype(F32), ngrad, gain)
            back = (hga[at].astype(F32) + back).astype(BF16).astype(F32)
            back_out[1, at_o] = (
                ct_own[at_o].astype(F32) + lg_s[at_o][:, 0:1] * cent + back
            ).astype(BF16)
            acc[0:1] += jnp.sum(ngrad * rhat, axis=0, keepdims=True)
            acc[2:3] += jnp.sum(ngrad, axis=0, keepdims=True)

        loop_rows(rows_o, ROW_STEP, grad)
        give_back("tgrad", k)

    def column_sums(rows_ref):
        def one(i, total):
            values = rows_ref[rows_at(i * ROW_STEP, ROW_STEP, ROW_STEP)].astype(F32)
            return total + jnp.sum(values, axis=0, keepdims=True)

        return lax.fori_loop(
            0, rows_ref.shape[0] // ROW_STEP, one, jnp.zeros((1, rows_ref.shape[1]), F32)
        )

    def weight_grads(j, grads_ref):
        small_ref[4 + j : 5 + j] = column_sums(grads_ref)
        ub_ref[j : j + 1] = column_sums(d_s.at[j])
        for into, left, right in (
            (down_grad_hbm, a_s.at[j], grads_ref),
            (up_grad_hbm, n_s.at[j], d_s.at[j]),
        ):
            tiles = left.shape[1] // COL_STEP

            def tile_copy(t):
                at = rows_at(t * COL_STEP, COL_STEP, COL_STEP)
                slot = lax.rem(t, 2)
                return pltpu.make_async_copy(stage.at[slot], into.at[j, 0, at], out_sem.at[slot])

            def one(t, carry):
                @pl.when(t >= 2)
                def _():
                    tile_copy(t - 2).wait()

                at = rows_at(t * COL_STEP, COL_STEP, COL_STEP)
                stage[lax.rem(t, 2)] = dot(left[:, at], right[...], TN).astype(BF16)
                tile_copy(t).start()
                return carry

            lax.fori_loop(0, tiles, one, 0)
            tile_copy(tiles - 2).wait()
            tile_copy(tiles - 1).wait()

    steps = range(chunks)
    for k in steps:
        send_x(k)
    spread("x", 0)
    send_g(0)
    for j in range(2):
        loads[j].wait()
    for k in steps:
        core("x", k).wait_recv()
        up_step(0, xa, k)
        if k + 1 < chunks:
            spread("x", k + 1)
            send_g(k + 1)
        if k > 0:
            sum_half("part0", "sum0", k - 1)
        down_step(0, k)
        if k > 1:
            make_h(k - 2)
        spread("g", k)
    sum_half("part0", "sum0", chunks - 1)
    make_h(chunks - 2)
    for j in range(2, 4):
        loads[j].wait()
    for k in steps:
        core("h", k).wait_recv()
        up_step(1, ha, k)
        if k == 0:
            make_h(chunks - 1)
        core("g", k).wait_recv()
        back_step(1, ga, k)
        down_step(1, k)
        sum_half("ngrad1", "ngrad1", k)
        sum_far("part1", "out", k)
        if k > 1:
            make_hgrad(k - 2)
            make_mixed(k - 2)
    weight_grads(1, ga)
    for k in steps:
        if k >= chunks - 2:
            make_hgrad(k)
            make_mixed(k)
        core("hgrad", k).wait_recv()
        back_step(0, hga, k)
        sum_far("ngrad0", "ngrad0", k)
        if k > 0:
            make_tgrad(k - 1)
    weight_grads(0, hga)
    make_tgrad(chunks - 1)

    red[1] = acc[...]
    over = copy_to(sib, red.at[1], red.at[2], red_send.at[0], red_recv.at[0])
    over.start()
    over.wait_recv()
    red[3] = red[1] + red[2]
    across = copy_to(far, red.at[3], red.at[4], red_send.at[1], red_recv.at[1])
    across.start()
    across.wait_recv()
    red[0] = red[3] + red[4]
    totals_in[e] = red[0]
    for m in order_flat[1:]:
        route("totals", m).start()
    small_ref[0:4] = red[0, 0:4]

    def unpack(kind, out_ref):
        s = 0 if kind == "mixed" else 1
        for m in order_flat[1:]:
            route(kind, m).wait_recv()

        def one(start, step):
            cols = rows_at(start, step, step)
            out_ref[:, cols] = dot(perm[...], back_in[s, :, cols], TN).astype(BF16)

        loop_rows(width, COL_STEP, one)

    unpack("mixed", mixed_ref)
    unpack("tgrad", tgrad_ref)
    for m in order_flat[1:]:
        route("totals", m).wait_recv()
    totals_ref[...] = totals_in[...]
    over.wait_send()
    across.wait_send()
    for m in order_flat[1:]:
        for kind in ROUTE_KINDS:
            route(kind, m).wait_send()
    for k in steps:
        for kind in LINK_KINDS:
            link(kind, k).wait_send()
        for kind in CORE_KINDS:
            core(kind, k).wait_send()


def per_device_fused(
    tokens,
    lengths,
    expert_ids,
    slots,
    centroids,
    sublayer_norm_gain,
    sublayer_norm_bias,
    up_weight,
    up_bias,
    down_weight,
    down_bias,
    cotangent,
):
    tok_rows, width = tokens.shape
    groups = lax.axis_size("expert")
    batches = lax.axis_size("batch")
    experts = centroids.shape[0]
    capacity = tok_rows // experts
    hidden = up_weight.shape[3]
    chunks = 4
    total = groups * batches * capacity
    vmem = pl.BlockSpec(memory_space=pltpu.VMEM)
    hbm = pl.BlockSpec(memory_space=pl.ANY)
    outs = pl.pallas_call(
        functools.partial(fused_kernel, groups, capacity, chunks),
        out_shape=[
            jax.ShapeDtypeStruct((tok_rows, width), BF16),
            jax.ShapeDtypeStruct((tok_rows, width), BF16),
            jax.ShapeDtypeStruct((groups, 8, width), F32),
            jax.ShapeDtypeStruct((8, width), F32),
            jax.ShapeDtypeStruct((8, hidden), F32),
            jax.ShapeDtypeStruct(up_weight.shape, BF16),
            jax.ShapeDtypeStruct(down_weight.shape, BF16),
        ],
        in_specs=[vmem] * 9 + [hbm] * 2,
        out_specs=[vmem] * 5 + [hbm] * 2,
        scratch_shapes=[
            pltpu.VMEM((2, width, hidden), BF16),
            pltpu.VMEM((2, hidden, width), BF16),
            pltpu.VMEM((tok_rows, tok_rows), BF16),
            pltpu.VMEM((tok_rows, width), BF16),
            pltpu.VMEM((tok_rows, width), BF16),
            pltpu.VMEM((total, width), BF16),
            pltpu.VMEM((total, width), BF16),
            pltpu.VMEM((total, width), BF16),
            pltpu.VMEM((total, width), BF16),
            pltpu.VMEM((2, total, width), BF16),
            pltpu.VMEM((2, total, hidden), BF16),
            pltpu.VMEM((2, total, hidden), BF16),
            pltpu.VMEM((4, total, width), BF16),
            pltpu.VMEM((4, total // 2, width), BF16),
            pltpu.VMEM((2, total // 2, width), BF16),
            pltpu.VMEM((2, total // 2, width), BF16),
            pltpu.VMEM((2, total // 4, width), BF16),
            pltpu.VMEM((2, total // 4, width), BF16),
            pltpu.VMEM((tok_rows, width), BF16),
            pltpu.VMEM((tok_rows, 128), F32),
            pltpu.VMEM((tok_rows, 128), F32),
            pltpu.VMEM((2, tok_rows, width), BF16),
            pltpu.VMEM((2, tok_rows, width), BF16),
            pltpu.VMEM((2, COL_STEP, width), BF16),
            pltpu.VMEM((8, width), F32),
            pltpu.VMEM((5, 8, width), F32),
            pltpu.VMEM((groups, 8, width), F32),
            pltpu.SemaphoreType.DMA((4,)),
            pltpu.SemaphoreType.DMA((len(ROUTE_KINDS), groups)),
            pltpu.SemaphoreType.DMA((len(ROUTE_KINDS), groups)),
            pltpu.SemaphoreType.DMA((len(LINK_KINDS), chunks)),
            pltpu.SemaphoreType.DMA((len(LINK_KINDS), chunks)),
            pltpu.SemaphoreType.DMA((len(CORE_KINDS), chunks)),
            pltpu.SemaphoreType.DMA((len(CORE_KINDS), chunks)),
            pltpu.SemaphoreType.DMA((2,)),
            pltpu.SemaphoreType.DMA((2,)),
            pltpu.SemaphoreType.DMA((2,)),
        ],
        compiler_params=pltpu.CompilerParams(
            collective_id=0, has_side_effects=True, vmem_limit_bytes=62 << 20
        ),
        cost_estimate=pl.CostEstimate(
            flops=24 * total * width * hidden, bytes_accessed=40 << 20, transcendentals=0
        ),
    )(
        expert_ids.reshape(1, tok_rows),
        slots.reshape(1, tok_rows),
        tokens,
        cotangent,
        centroids,
        sublayer_norm_gain,
        sublayer_norm_bias,
        up_bias,
        down_bias,
        up_weight,
        down_weight,
    )
    mixed, tokens_grad, totals, small, ub, up_grad, down_grad = outs
    denominator = jnp.float32(capacity * groups * batches)
    return (
        mixed,
        tokens_grad,
        totals[:, 4],
        small[0:2][:, None],
        small[2:4][:, None],
        up_grad.astype(F32),
        ub[0:2][:, None],
        down_grad.astype(F32),
        small[4:6][:, None],
        totals[:, 5, 0] / denominator,
        totals[:, 6, 0] / denominator,
    )


def solution(mesh):
    in_specs = (
        P(("expert", "batch"), None),
        P(("expert", "batch")),
        P(("expert", "batch")),
        P(("expert", "batch")),
        P(),
        P(None, "expert", None),
        P(None, "expert", None),
        P(None, "expert", None, "batch"),
        P(None, "expert", "batch"),
        P(None, "expert", "batch", None),
        P(None, "expert", None),
        P(("expert", "batch"), None),
    )
    out_specs = (
        P(("expert", "batch"), None),
        P(("expert", "batch"), None),
        P(),
        P(None, "expert", None),
        P(None, "expert", None),
        P(None, "expert", None, "batch"),
        P(None, "expert", "batch"),
        P(None, "expert", "batch", None),
        P(None, "expert", None),
        P(),
        P(),
    )
    body = per_device_fused if fused_fits(mesh) else per_device
    return jax.shard_map(
        body, mesh=mesh, in_specs=in_specs, out_specs=out_specs, check_vma=False
    )
```

```python
import functools

import jax
import jax.numpy as jnp
from jax import lax
from jax.experimental import pallas as pl
from jax.experimental.pallas import tpu as pltpu
from jax.sharding import PartitionSpec as P


def gelu_exact(values):
    return jax.nn.gelu(values, approximate=False)


def apply_layer_norm(row_block):
    values = row_block.astype(jnp.float32)
    row_mean = jnp.mean(values, axis=-1, keepdims=True)
    centered = values - row_mean
    row_inverse_scale = lax.rsqrt(jnp.mean(centered * centered, axis=-1, keepdims=True) + 1e-05)
    return (centered * row_inverse_scale, row_inverse_scale)


def per_device(
    tokens,
    lengths,
    expert_ids,
    slots,
    centroids,
    sublayer_norm_gain,
    sublayer_norm_bias,
    up_weight,
    up_bias,
    down_weight,
    down_bias,
    cotangent,
):
    tok_rows, width = tokens.shape
    layers = sublayer_norm_gain.shape[0]
    local_count = up_weight.shape[1]
    expert_count = centroids.shape[0]
    capacity = tok_rows // expert_count
    groups = lax.axis_size("expert")
    batches = lax.axis_size("batch")
    position = jnp.arange(tok_rows, dtype=jnp.int32)
    live = (position < lengths[0]).astype(jnp.float32)[:, None]
    target = jnp.where(slots >= 0, expert_ids * capacity + slots, tok_rows)
    source = jnp.full((tok_rows + 1,), -1, jnp.int32).at[target].set(position)[:tok_rows]
    filled = (source >= 0)[:, None]
    safe_source = jnp.maximum(source, 0)
    safe_target = jnp.minimum(target, tok_rows - 1)

    def pack(values):
        return jnp.where(filled, values[safe_source], jnp.zeros((), values.dtype))

    onehot = (expert_ids[:, None] == jnp.arange(expert_count, dtype=jnp.int32)[None, :]).astype(
        jnp.float32
    )
    logits = jnp.einsum("td,ed->te", tokens, centroids, preferred_element_type=jnp.float32)
    gate = jax.nn.sigmoid(jnp.sum(logits * onehot, axis=1))[:, None]
    used = onehot * live
    usage_gate = jnp.sum(used * gate, axis=0)
    usage_count = jnp.sum(used, axis=0)
    gate_total, count_total = lax.psum((usage_gate, usage_count), ("expert", "batch"))

    def expand_hidden(values, expert_layer_step):
        return values[expert_layer_step].astype(jnp.float32)[None, :, None, :]

    arrived = lax.all_to_all(pack(tokens), "expert", split_axis=0, concat_axis=0, tiled=True)
    current = arrived
    inputs = []
    kept = []
    for expert_layer_step in range(layers):
        gathered = lax.all_gather(current, "batch", axis=0, tiled=True)
        row_layout_grid = gathered.reshape(-1, local_count, capacity, width)
        standardized_input, row_inverse_scale = apply_layer_norm(row_layout_grid)
        normalized_rows = (
            standardized_input * expand_hidden(sublayer_norm_gain, expert_layer_step)
            + expand_hidden(sublayer_norm_bias, expert_layer_step)
        ).astype(jnp.bfloat16)
        pre_rows = jnp.einsum(
            "nlcd,ldf->nlcf",
            normalized_rows,
            up_weight[expert_layer_step],
            preferred_element_type=jnp.float32,
        ) + expand_hidden(up_bias, expert_layer_step)
        hidden_parts = (normalized_rows, pre_rows, gelu_exact(pre_rows).astype(jnp.bfloat16))

        def down_part(start, count, activity=hidden_parts[2], expert_layer_step=expert_layer_step):
            return jnp.einsum(
                "nlcf,lfd->nlcd",
                activity,
                down_weight[expert_layer_step],
                preferred_element_type=jnp.float32,
            )

        mixed_part = lax.psum_scatter(
            down_part(jnp.int32(0), lax.axis_size("batch") * groups).astype(jnp.bfloat16),
            "batch",
            scatter_dimension=0,
            tiled=True,
        ).astype(jnp.float32)
        own_grid = current.reshape(groups, local_count, capacity, width).astype(jnp.float32)
        result = (own_grid + mixed_part + expand_hidden(down_bias, expert_layer_step)).astype(
            jnp.bfloat16
        )
        inputs.append(current)
        kept.append(hidden_parts)
        current = result.reshape(tok_rows, width)
    returned = lax.all_to_all(current, "expert", split_axis=0, concat_axis=0, tiled=True)
    expert_tok = returned[safe_target].astype(jnp.float32)
    mixed = (live * (tokens.astype(jnp.float32) + gate * expert_tok)).astype(jnp.bfloat16)
    upstream = cotangent.astype(jnp.float32) * live
    gate_grad = jnp.sum(upstream * expert_tok, axis=1, keepdims=True)
    logit_grad = (gate_grad * gate * (1.0 - gate)).astype(jnp.bfloat16)
    route_grad = (onehot * logit_grad.astype(jnp.float32)).astype(jnp.bfloat16)
    centroid_part = jnp.einsum("te,td->ed", route_grad, tokens, preferred_element_type=jnp.float32)
    gate_input = jnp.einsum("te,ed->td", route_grad, centroids, preferred_element_type=jnp.float32)
    expert_grad = (gate * upstream).astype(jnp.bfloat16)
    grad_rows = lax.all_to_all(pack(expert_grad), "expert", split_axis=0, concat_axis=0, tiled=True)
    gain_parts = [None] * layers
    shift_parts = [None] * layers
    down_bias_parts = [None] * layers
    up_weight_grads = [None] * layers
    up_bias_grads = [None] * layers
    down_weight_grads = [None] * layers
    for expert_layer_step in range(layers - 1, -1, -1):
        own_rows = inputs[expert_layer_step]
        grads_all = lax.all_gather(grad_rows, "batch", axis=0, tiled=True).reshape(
            -1, local_count, capacity, width
        )
        normed, pre_act, activity = kept[expert_layer_step]
        act_grad = jnp.einsum(
            "nlcd,lfd->nlcf",
            grads_all,
            down_weight[expert_layer_step],
            preferred_element_type=jnp.float32,
        )
        pre_grad = jax.vjp(gelu_exact, pre_act)[1](act_grad)[0].astype(jnp.bfloat16)
        down_weight_grads[expert_layer_step] = jnp.einsum(
            "nlcf,nlcd->lfd", activity, grads_all, preferred_element_type=jnp.float32
        )
        up_weight_grads[expert_layer_step] = jnp.einsum(
            "nlcd,nlcf->ldf", normed, pre_grad, preferred_element_type=jnp.float32
        )
        up_bias_grads[expert_layer_step] = jnp.sum(pre_grad.astype(jnp.float32), axis=(0, 2))

        def up_part(start, count, pre_grad=pre_grad, expert_layer_step=expert_layer_step):
            return jnp.einsum(
                "nlcf,ldf->nlcd",
                pre_grad,
                up_weight[expert_layer_step],
                preferred_element_type=jnp.float32,
            )

        normed_grad = lax.psum_scatter(
            up_part(jnp.int32(0), lax.axis_size("batch") * groups).astype(jnp.bfloat16),
            "batch",
            scatter_dimension=0,
            tiled=True,
        ).astype(jnp.float32)
        out_grad = grad_rows.reshape(groups, local_count, capacity, width).astype(jnp.float32)
        down_bias_parts[expert_layer_step] = jnp.sum(out_grad, axis=(0, 2))
        own_hat, own_scale = apply_layer_norm(
            own_rows.reshape(groups, local_count, capacity, width)
        )
        gain_parts[expert_layer_step] = jnp.sum(normed_grad * own_hat, axis=(0, 2))
        shift_parts[expert_layer_step] = jnp.sum(normed_grad, axis=(0, 2))
        hat_grad = normed_grad * expand_hidden(sublayer_norm_gain, expert_layer_step)
        row_grad = own_scale * (
            hat_grad
            - jnp.mean(hat_grad, axis=-1, keepdims=True)
            - own_hat * jnp.mean(hat_grad * own_hat, axis=-1, keepdims=True)
        )
        grad_rows = (out_grad + row_grad).astype(jnp.bfloat16).reshape(tok_rows, width)
    gain_grad, shift_grad, down_bias_grad = lax.psum(
        (jnp.stack(gain_parts), jnp.stack(shift_parts), jnp.stack(down_bias_parts)), "batch"
    )
    token_back = lax.all_to_all(grad_rows, "expert", split_axis=0, concat_axis=0, tiled=True)
    tokens_grad = (
        upstream + gate_input + live * token_back[safe_target].astype(jnp.float32)
    ).astype(jnp.bfloat16)
    centroid_grad = lax.psum(centroid_part, ("expert", "batch"))
    denominator = jnp.float32(capacity * groups * batches)
    gate_mass = gate_total / denominator
    load = count_total / denominator
    return (
        mixed,
        tokens_grad,
        centroid_grad,
        gain_grad,
        shift_grad,
        jnp.stack(up_weight_grads),
        jnp.stack(up_bias_grads),
        jnp.stack(down_weight_grads),
        down_bias_grad,
        gate_mass,
        load,
    )


MESH = pl.DeviceIdType.MESH
F32 = jnp.float32
BF16 = jnp.bfloat16
ROW_STEP = 64
COL_STEP = 256
EMPTY = 8.0
LINK_KINDS = ("x", "g", "sum0", "out", "ngrad1", "ngrad0")
CORE_KINDS = ("x", "g", "part0", "h", "part1", "ngrad1", "hgrad", "ngrad0")
WGRAD_PARTS = 2
SCHEDULE = (
    "SX.3 SX.0 SG.3 SG.0",
    "PX.0 U0.0 SX.1 D0.0",
    "SX.2 S0.0 PX.1 U0.1",
    "D0.1 PX.2 S0.1 U0.2",
    "SG.1 D0.2 PX.3 S0.2",
    "U0.3 SG.2 D0.3 H.0",
    "PG.0 S0.3 U1.0 H.1",
    "B1.0 D1.0 S1.0 U1.1",
    "PG.1 SO.0 H.2 B1.1",
    "D1.1 S1.1 U1.2 PG.2",
    "SO.1 H.3 B1.2 D1.2",
    "S1.2 U1.3 PG.3 SO.2",
    "B1.3 D1.3 S1.3 HG.0",
    "SO.3 W1.0 B0.0 W1.1",
    "SQ.0 HG.1 MX.0 B0.1",
    "W1.2 SQ.1 HG.2 MX.1",
    "B0.2 W1.3 SQ.2 HG.3",
    "MX.2 TG.0 B0.3 TG.1",
    "MX.3 SQ.3 TG.2 W0.0",
    "W0.1 TG.3 W0.2 W0.3",
)
ROUTE_KINDS = ("x", "ct", "mixed", "tgrad", "totals")


def fused_fits(mesh):
    groups, batches = mesh.shape["expert"], mesh.shape["batch"]
    return batches == 4 and groups == 8


def rows_at(start, count, unit):
    return pl.ds(pl.multiple_of(start, unit), count)


def loop_rows(count, step, body):
    step = min(step, count)
    for start in range(0, count, step):
        body(start, step)


def normalize(values):
    centered = values - jnp.mean(values, axis=-1, keepdims=True)
    scale = lax.rsqrt(jnp.mean(centered * centered, axis=-1, keepdims=True) + 1e-05)
    return centered * scale, scale


def dot(a, b, dims):
    return lax.dot_general(a, b, (dims, ((), ())), preferred_element_type=F32)


NN = ((1,), (0,))
NT = ((1,), (1,))
TN = ((0,), (0,))


def fused_kernel(
    groups,
    capacity,
    chunks,
    ids_ref,
    slots_ref,
    tok_ref,
    ct_ref,
    cent_ref,
    gain_ref,
    bias_ref,
    up_bias_ref,
    down_bias_ref,
    up_hbm,
    down_hbm,
    mixed_ref,
    tgrad_ref,
    totals_ref,
    small_ref,
    ub_ref,
    up_grad_hbm,
    down_grad_hbm,
    up_w,
    down_w,
    perm,
    pack_x,
    pack_ct,
    xa,
    ga,
    ha,
    hga,
    n_s,
    a_s,
    d_s,
    part,
    part_in,
    half_out,
    half_in,
    own_out,
    own_in,
    ct_own,
    gate_s,
    lg_s,
    back_out,
    back_in,
    stage,
    acc,
    red,
    totals_in,
    w_sem,
    route_send,
    route_recv,
    link_send,
    link_recv,
    core_send,
    core_recv,
    red_send,
    red_recv,
    out_sem,
):
    tok_rows, width = tok_ref.shape
    hidden = up_w.shape[2]
    per = groups // chunks
    rows_m = per * 4 * capacity
    rows_h = rows_m // 2
    rows_o = rows_m // 4
    e = lax.axis_index("expert")
    b = lax.axis_index("batch")
    x = b // 2
    c = lax.rem(b, 2)
    sib = (e, x * 2 + (1 - c))
    far = (e, (1 - x) * 2 + c)

    def flipped(m):
        out = jnp.int32(0)
        bit = 1
        while bit < groups:
            digit = lax.rem(e // bit, 2)
            out = out + bit * ((1 - digit) if m & bit else digit)
            bit *= 2
        return out

    half = c * rows_h
    sib_half = (1 - c) * rows_h
    own = half + x * rows_o
    pairs = [tuple(range(j * per, (j + 1) * per)) for j in range(chunks)]
    order = pairs[1:] + pairs[:1]
    place = {m: (k, i) for k, ms in enumerate(order) for i, m in enumerate(ms)}
    others = range(1, groups)

    def at_half(k):
        return rows_at(k * rows_m + half, rows_h, rows_h)

    def at_sib_half(k):
        return rows_at(k * rows_m + sib_half, rows_h, rows_h)

    def at_own(k):
        return rows_at(k * rows_m + own, rows_o, rows_o)

    def at_all(k):
        return pl.ds(k * rows_m, rows_m)

    def copy_to(device, src, dst, send, recv):
        return pltpu.make_async_remote_copy(
            src_ref=src,
            dst_ref=dst,
            send_sem=send,
            recv_sem=recv,
            device_id=device,
            device_id_type=MESH,
        )

    def route(kind, m):
        n = ROUTE_KINDS.index(kind)
        k, i = place[m]
        to = flipped(m)
        theirs = rows_at(to * capacity, capacity, capacity)
        mine = rows_at(e * capacity, capacity, capacity)
        if kind == "x":
            src = pack_x.at[theirs]
            dst = xa.at[rows_at(k * rows_m + own + i * capacity, capacity, capacity)]
        elif kind == "ct":
            src = pack_ct.at[theirs]
            dst = ct_own.at[pl.ds(k * rows_o + i * capacity, capacity)]
        elif kind == "totals":
            src = red.at[0]
            dst = totals_in.at[e]
        else:
            s = 0 if kind == "mixed" else 1
            src = back_out.at[s, pl.ds(k * rows_o + i * capacity, capacity)]
            dst = back_in.at[s, mine]
        return copy_to((to, b), src, dst, route_send.at[n, m], route_recv.at[n, m])

    def link(kind, k):
        n = LINK_KINDS.index(kind)
        if kind == "x":
            src = dst = xa.at[at_own(k)]
        elif kind == "g":
            src = dst = ga.at[at_own(k)]
        elif kind in ("sum0", "ngrad1"):
            s = 0 if kind == "sum0" else 1
            at = pl.ds(k * rows_h, rows_h)
            src, dst = half_out.at[s, at], half_in.at[s, at]
        else:
            s = 0 if kind == "out" else 1
            at = pl.ds(k * rows_o, rows_o)
            src, dst = own_out.at[s, at], own_in.at[s, at]
        return copy_to(far, src, dst, link_send.at[n, k], link_recv.at[n, k])

    def core(kind, k):
        n = CORE_KINDS.index(kind)
        whole = {"x": xa, "g": ga, "h": ha, "hgrad": hga}
        if kind in whole:
            src = dst = whole[kind].at[at_half(k)]
        else:
            s = ("part0", "part1", "ngrad1", "ngrad0").index(kind)
            src = part.at[s, at_sib_half(k)]
            dst = part_in.at[s, pl.ds(k * rows_h, rows_h)]
        return copy_to(sib, src, dst, core_send.at[n, k], core_recv.at[n, k])

    barrier = pltpu.get_barrier_semaphore()
    peers = [sib, far] + [(flipped(m), b) for m in range(1, groups)]
    for peer in peers:
        pl.semaphore_signal(barrier, inc=1, device_id=peer, device_id_type=MESH)
    loads = []
    for j in range(2):
        loads.append(pltpu.make_async_copy(up_hbm.at[j, 0], up_w.at[j], w_sem.at[2 * j]))
        loads.append(pltpu.make_async_copy(down_hbm.at[j, 0], down_w.at[j], w_sem.at[2 * j + 1]))
    for load in loads:
        load.start()
    target = jnp.where(
        slots_ref[...] >= 0, ids_ref[...] * capacity + slots_ref[...], -1
    )
    slot = lax.broadcasted_iota(jnp.int32, (tok_rows, tok_rows), 0)
    onehot = jnp.where(slot == target, 1.0, 0.0)
    perm[...] = onehot.astype(BF16)
    empty = EMPTY * (1.0 - jnp.sum(onehot, axis=1, keepdims=True))

    def pack(start, step):
        cols = rows_at(start, step, step)
        pack_x[:, cols] = (dot(perm[...], tok_ref[:, cols], NN) + empty).astype(BF16)
        pack_ct[:, cols] = dot(perm[...], ct_ref[:, cols], NN).astype(BF16)

    loop_rows(width, COL_STEP, pack)
    acc[...] = jnp.zeros_like(acc)
    cent_rows = cent_ref[...].astype(F32)
    cent_at = lax.broadcasted_iota(jnp.int32, cent_rows.shape, 0)
    cent = jnp.sum(jnp.where(cent_at == e, cent_rows, 0.0), axis=0, keepdims=True)
    pl.semaphore_wait(barrier, len(peers))
    near = 2 * per
    for kind, masks in (
        ("x", range(1, near)),
        ("ct", range(1, per)),
        ("x", range(near, groups)),
        ("ct", range(per, groups)),
    ):
        for m in masks:
            route(kind, m).start()
    mine = rows_at(e * capacity, capacity, capacity)
    first_k, first_i = place[0]
    at = rows_at(first_k * rows_m + own + first_i * capacity, capacity, capacity)
    xa[at] = pack_x[mine]
    ct_own[pl.ds(first_k * rows_o + first_i * capacity, capacity)] = pack_ct[mine]

    def send_x(k):
        for m in order[k]:
            if m:
                route("x", m).wait_recv()
        link("x", k).start()

    def send_g(k):
        for m in order[k]:
            if m:
                route("ct", m).wait_recv()

        def gated(start, step):
            at = rows_at(k * rows_m + own + start, step, step)
            at_o = rows_at(k * rows_o + start, step, step)
            values = xa[at].astype(F32)
            logit = jnp.sum(values * cent, axis=-1, keepdims=True)
            gate = jax.nn.sigmoid(logit)
            gate_s[at_o] = jnp.broadcast_to(gate, (step, 128))
            ga[at] = (gate * ct_own[at_o].astype(F32)).astype(BF16)
            used = jnp.where(values[:, 0:1] < 7.0, 1.0, 0.0)
            acc[5:6] += jnp.broadcast_to(
                jnp.sum(used * gate, axis=0, keepdims=True), (1, width)
            )
            acc[6:7] += jnp.broadcast_to(jnp.sum(used, axis=0, keepdims=True), (1, width))

        loop_rows(rows_o, ROW_STEP, gated)
        link("g", k).start()

    def spread(kind, k):
        link(kind, k).wait_recv()
        core(kind, k).start()

    def up_step(j, rows_ref, k):
        gain = gain_ref[j : j + 1].astype(F32)
        bias = bias_ref[j : j + 1].astype(F32)

        def norm(start, step):
            at = rows_at(k * rows_m + start, step, step)
            rhat, _ = normalize(rows_ref[at].astype(F32))
            n_s[j, at] = (rhat * gain + bias).astype(BF16)

        loop_rows(rows_m, ROW_STEP, norm)

        def up(start, step):
            cols = rows_at(start, step, step)
            pre = dot(n_s[j, at_all(k)], up_w[j, :, cols], NN) + up_bias_ref[j : j + 1, cols].astype(
                F32
            )
            cdf = 0.5 * (1.0 + lax.erf(pre * (0.5**0.5)))
            pdf = jnp.exp(-0.5 * pre * pre) * 0.3989422804014327
            a_s[j, at_all(k), cols] = (pre * cdf).astype(BF16)
            d_s[j, at_all(k), cols] = (cdf + pre * pdf).astype(BF16)

        loop_rows(hidden, COL_STEP, up)

    def down_step(j, k):
        kind = "part%d" % j

        def down(start, step):
            cols = rows_at(start, step, step)
            part[j, at_all(k), cols] = dot(a_s[j, at_all(k)], down_w[j, :, cols], NN).astype(BF16)

        loop_rows(width, COL_STEP, down)
        core(kind, k).start()

    def back_step(j, grads_ref, k):
        kind = "ngrad%d" % j
        s = 3 - j

        def act(start, step):
            cols = rows_at(start, step, step)
            grad = dot(grads_ref[at_all(k)], down_w[j, cols, :], NT)
            d_s[j, at_all(k), cols] = (grad * d_s[j, at_all(k), cols].astype(F32)).astype(BF16)

        loop_rows(hidden, COL_STEP, act)

        def up_back(start, step):
            cols = rows_at(start, step, step)
            part[s, at_all(k), cols] = dot(d_s[j, at_all(k)], up_w[j, cols, :], NT).astype(BF16)

        loop_rows(width, COL_STEP, up_back)
        core(kind, k).start()

    def sum_half(kind, link_kind, k):
        s = ("part0", "part1", "ngrad1", "ngrad0").index(kind)
        o = ("sum0", "ngrad1").index(link_kind)
        core(kind, k).wait_recv()

        def add_half(start, step):
            at = rows_at(k * rows_m + half + start, step, step)
            at_h = rows_at(k * rows_h + start, step, step)
            total = part[s, at].astype(F32) + part_in[s, at_h].astype(F32)
            half_out[o, at_h] = total.astype(BF16)

        loop_rows(rows_h, ROW_STEP, add_half)
        link(link_kind, k).start()

    def sum_far(kind, link_kind, k):
        s = ("part0", "part1", "ngrad1", "ngrad0").index(kind)
        o = ("out", "ngrad0").index(link_kind)
        core(kind, k).wait_recv()

        def add_far(start, step):
            at = rows_at(k * rows_m + half + (1 - x) * rows_o + start, step, step)
            at_h = rows_at(k * rows_h + (1 - x) * rows_o + start, step, step)
            at_o = rows_at(k * rows_o + start, step, step)
            total = part[s, at].astype(F32) + part_in[s, at_h].astype(F32)
            own_out[o, at_o] = total.astype(BF16)

        loop_rows(rows_o, ROW_STEP, add_far)
        link(link_kind, k).start()

    def sum_own(s, o, k, start, step):
        at = rows_at(k * rows_m + own + start, step, step)
        at_h = rows_at(k * rows_h + x * rows_o + start, step, step)
        at_o = rows_at(k * rows_o + start, step, step)
        mine = part[s, at].astype(F32) + part_in[s, at_h].astype(F32)
        return mine + own_in[o, at_o].astype(F32)

    def make_h(k):
        link("sum0", k).wait_recv()
        shift = down_bias_ref[0:1].astype(F32)

        def add_h(start, step):
            at = rows_at(k * rows_m + half + start, step, step)
            at_h = rows_at(k * rows_h + start, step, step)
            total = half_out[0, at_h].astype(F32) + half_in[0, at_h].astype(F32)
            ha[at] = (xa[at].astype(F32) + total + shift).astype(BF16)

        loop_rows(rows_h, ROW_STEP, add_h)
        core("h", k).start()

    def norm_back(rows, ngrad, gain):
        rhat, scale = normalize(rows)
        q = ngrad * gain
        back = scale * (
            q - jnp.mean(q, axis=-1, keepdims=True) - rhat * jnp.mean(q * rhat, axis=-1, keepdims=True)
        )
        return back, rhat

    def make_hgrad(k):
        link("ngrad1", k).wait_recv()
        gain = gain_ref[1:2].astype(F32)

        def grad_h(start, step):
            at = rows_at(k * rows_m + half + start, step, step)
            at_h = rows_at(k * rows_h + start, step, step)
            ngrad = half_out[1, at_h].astype(F32) + half_in[1, at_h].astype(F32)
            back, rhat = norm_back(ha[at].astype(F32), ngrad, gain)
            hga[at] = (ga[at].astype(F32) + back).astype(BF16)
            acc[1:2] += 0.5 * jnp.sum(ngrad * rhat, axis=0, keepdims=True)
            acc[3:4] += 0.5 * jnp.sum(ngrad, axis=0, keepdims=True)

        loop_rows(rows_h, ROW_STEP, grad_h)
        core("hgrad", k).start()

    def give_back(kind, k):
        for m in order[k]:
            if m:
                route(kind, m).start()
            else:
                s = 0 if kind == "mixed" else 1
                _, i = place[0]
                back_in[s, mine] = back_out[s, pl.ds(k * rows_o + i * capacity, capacity)]

    def make_mixed(k):
        link("out", k).wait_recv()
        shift = down_bias_ref[1:2].astype(F32)

        def mix(start, step):
            at = rows_at(k * rows_m + own + start, step, step)
            at_o = rows_at(k * rows_o + start, step, step)
            out = (ha[at].astype(F32) + sum_own(1, 0, k, start, step) + shift).astype(BF16).astype(F32)
            rows = xa[at].astype(F32)
            gate = gate_s[at_o][:, 0:1]
            back_out[0, at_o] = (rows + gate * out).astype(BF16)
            along = jnp.sum(ct_own[at_o].astype(F32) * out, axis=-1, keepdims=True)
            lgrad = (along * gate * (1.0 - gate)).astype(BF16).astype(F32)
            lg_s[at_o] = jnp.broadcast_to(lgrad, (step, 128))
            acc[4:5] += jnp.sum(lgrad * rows, axis=0, keepdims=True)

        loop_rows(rows_o, ROW_STEP, mix)
        give_back("mixed", k)

    def make_tgrad(k):
        link("ngrad0", k).wait_recv()
        gain = gain_ref[0:1].astype(F32)

        def grad_t(start, step):
            at = rows_at(k * rows_m + own + start, step, step)
            at_o = rows_at(k * rows_o + start, step, step)
            ngrad = sum_own(3, 1, k, start, step)
            back, rhat = norm_back(xa[at].astype(F32), ngrad, gain)
            back = (hga[at].astype(F32) + back).astype(BF16).astype(F32)
            back_out[1, at_o] = (
                ct_own[at_o].astype(F32) + lg_s[at_o][:, 0:1] * cent + back
            ).astype(BF16)
            acc[0:1] += jnp.sum(ngrad * rhat, axis=0, keepdims=True)
            acc[2:3] += jnp.sum(ngrad, axis=0, keepdims=True)

        loop_rows(rows_o, ROW_STEP, grad_t)
        give_back("tgrad", k)

    def column_sums(rows_ref):
        def one(i, total):
            values = rows_ref[rows_at(i * ROW_STEP, ROW_STEP, ROW_STEP)].astype(F32)
            return total + jnp.sum(values, axis=0, keepdims=True)

        return lax.fori_loop(
            0, rows_ref.shape[0] // ROW_STEP, one, jnp.zeros((1, rows_ref.shape[1]), F32)
        )

    tiles = []

    def weight_grad(j, which, part_of):
        grads_ref = (ga, hga)[1 - j]
        into, left, right = (
            (down_grad_hbm, a_s.at[j], grads_ref),
            (up_grad_hbm, n_s.at[j], d_s.at[j]),
        )[which]
        if part_of == 0 and which == 0:
            small_ref[4 + j : 5 + j] = column_sums(grads_ref)
        if part_of == 0 and which == 1:
            ub_ref[j : j + 1] = column_sums(right)
        count = left.shape[1] // WGRAD_PARTS // COL_STEP
        for t in range(part_of * count, (part_of + 1) * count):
            slot = len(tiles) % stage.shape[0]
            if len(tiles) >= stage.shape[0]:
                tiles[len(tiles) - stage.shape[0]].wait()
            at = pl.ds(t * COL_STEP, COL_STEP)
            stage[slot] = dot(left[:, at], right[...], TN).astype(BF16)
            tiles.append(pltpu.make_async_copy(stage.at[slot], into.at[j, 0, at], out_sem.at[slot]))
            tiles[-1].start()

    steps = range(chunks)

    def up_0(k):
        if k == first_use[0]:
            loads[0].wait()
        core("x", k).wait_recv()
        up_step(0, xa, k)

    def down_0(k):
        if k == first_use[0]:
            loads[1].wait()
        down_step(0, k)

    def up_1(k):
        if k == first_use[1]:
            loads[2].wait()
            loads[3].wait()
        core("h", k).wait_recv()
        up_step(1, ha, k)

    def back_1(k):
        core("g", k).wait_recv()
        back_step(1, ga, k)

    def back_0(k):
        core("hgrad", k).wait_recv()
        back_step(0, hga, k)

    tasks = {
        "SX": send_x,
        "SG": send_g,
        "PX": functools.partial(spread, "x"),
        "PG": functools.partial(spread, "g"),
        "U0": up_0,
        "D0": down_0,
        "S0": functools.partial(sum_half, "part0", "sum0"),
        "H": make_h,
        "U1": up_1,
        "B1": back_1,
        "D1": functools.partial(down_step, 1),
        "S1": functools.partial(sum_half, "ngrad1", "ngrad1"),
        "SO": functools.partial(sum_far, "part1", "out"),
        "HG": make_hgrad,
        "MX": make_mixed,
        "B0": back_0,
        "SQ": functools.partial(sum_far, "ngrad0", "ngrad0"),
        "TG": make_tgrad,
        "W1": lambda q: weight_grad(1, q // WGRAD_PARTS, q % WGRAD_PARTS),
        "W0": lambda q: weight_grad(0, q // WGRAD_PARTS, q % WGRAD_PARTS),
    }
    plan = [word.split(".") for line in SCHEDULE for word in line.split()]
    first_use = [next(int(k) for name, k in plan if name == u) for u in ("U0", "U1")]
    for name, k in plan:
        tasks[name](int(k))

    red[1] = acc[...]
    over = copy_to(sib, red.at[1], red.at[2], red_send.at[0], red_recv.at[0])
    over.start()
    over.wait_recv()
    red[3] = red[1] + red[2]
    across = copy_to(far, red.at[3], red.at[4], red_send.at[1], red_recv.at[1])
    across.start()
    across.wait_recv()
    red[0] = red[3] + red[4]
    totals_in[e] = red[0]
    for m in others:
        route("totals", m).start()
    small_ref[0:4] = red[0, 0:4]

    def unpack(kind, out_ref):
        s = 0 if kind == "mixed" else 1
        for m in others:
            route(kind, m).wait_recv()

        def place_tokens(start, step):
            cols = rows_at(start, step, step)
            out_ref[:, cols] = dot(perm[...], back_in[s, :, cols], TN).astype(BF16)

        loop_rows(width, COL_STEP, place_tokens)

    unpack("mixed", mixed_ref)
    unpack("tgrad", tgrad_ref)
    for m in others:
        route("totals", m).wait_recv()
    totals_ref[...] = totals_in[...]
    for tile in tiles[-stage.shape[0] :]:
        tile.wait()
    over.wait_send()
    across.wait_send()
    for m in others:
        for kind in ROUTE_KINDS:
            route(kind, m).wait_send()
    for k in steps:
        for kind in LINK_KINDS:
            link(kind, k).wait_send()
        for kind in CORE_KINDS:
            core(kind, k).wait_send()


def widen_kernel(
    denominator,
    mixed_hbm,
    tgrad_hbm,
    totals_ref,
    small_ref,
    ub_ref,
    up_hbm,
    down_hbm,
    mixed_out,
    tgrad_out,
    cent_out,
    gain_out,
    shift_out,
    up_out,
    ub_out,
    down_out,
    db_out,
    mass_out,
    load_out,
    up_low,
    down_low,
    up_wide,
    down_wide,
    row_sem,
    in_sem,
    out_sem,
):
    layers, tiles, rows = up_low.shape[:3]
    moves = [
        pltpu.make_async_copy(mixed_hbm, mixed_out, row_sem.at[0]),
        pltpu.make_async_copy(tgrad_hbm, tgrad_out, row_sem.at[1]),
    ]
    pairs = []
    for j in range(layers):
        for n, (src, low, wide, dst) in enumerate(
            ((down_hbm, down_low, down_wide, down_out), (up_hbm, up_low, up_wide, up_out))
        ):
            for t in range(tiles):
                at = pl.ds(t * rows, rows)
                pairs.append(
                    (
                        pltpu.make_async_copy(src.at[j, 0, at], low.at[j, t], in_sem.at[n, j, t]),
                        low.at[j, t],
                        wide.at[j, t],
                        pltpu.make_async_copy(wide.at[j, t], dst.at[j, 0, at], out_sem.at[n, j, t]),
                    )
                )
    for pair in pairs:
        pair[0].start()
    for move in moves:
        move.start()
    for arrive, low, wide, leave in pairs:
        arrive.wait()
        wide[...] = low[...].astype(F32)
        leave.start()
    cent_out[...] = totals_ref[:, 4]
    for j in range(layers):
        gain_out[j] = small_ref[j : j + 1]
        shift_out[j] = small_ref[2 + j : 3 + j]
        db_out[j] = small_ref[4 + j : 5 + j]
        ub_out[j] = ub_ref[j : j + 1]
    experts = totals_ref.shape[0]
    diagonal = lax.broadcasted_iota(jnp.int32, (experts, 128), 0) == lax.broadcasted_iota(
        jnp.int32, (experts, 128), 1
    )
    for out, n in ((mass_out, 5), (load_out, 6)):
        values = jnp.sum(jnp.where(diagonal, totals_ref[:, n, 0:128], 0.0), axis=0)
        out[...] = values[0:experts] / jnp.float32(denominator)
    for _, _, _, leave in pairs:
        leave.wait()
    for move in moves:
        move.wait()


def per_device_fused(
    tokens,
    lengths,
    expert_ids,
    slots,
    centroids,
    sublayer_norm_gain,
    sublayer_norm_bias,
    up_weight,
    up_bias,
    down_weight,
    down_bias,
    cotangent,
):
    tok_rows, width = tokens.shape
    groups = lax.axis_size("expert")
    batches = lax.axis_size("batch")
    experts = centroids.shape[0]
    capacity = tok_rows // experts
    hidden = up_weight.shape[3]
    chunks = 4
    total = groups * batches * capacity
    def flat(values):
        return values.reshape(values.shape[0], -1)

    vmem = pl.BlockSpec(memory_space=pltpu.VMEM)
    hbm = pl.BlockSpec(memory_space=pl.ANY)
    outs = pl.pallas_call(
        functools.partial(fused_kernel, groups, capacity, chunks),
        out_shape=[
            jax.ShapeDtypeStruct((tok_rows, width), BF16),
            jax.ShapeDtypeStruct((tok_rows, width), BF16),
            jax.ShapeDtypeStruct((groups, 8, width), F32),
            jax.ShapeDtypeStruct((8, width), F32),
            jax.ShapeDtypeStruct((8, hidden), F32),
            jax.ShapeDtypeStruct(up_weight.shape, BF16),
            jax.ShapeDtypeStruct(down_weight.shape, BF16),
        ],
        in_specs=[vmem] * 9 + [hbm] * 2,
        out_specs=[vmem] * 5 + [hbm] * 2,
        scratch_shapes=[
            pltpu.VMEM((2, width, hidden), BF16),
            pltpu.VMEM((2, hidden, width), BF16),
            pltpu.VMEM((tok_rows, tok_rows), BF16),
            pltpu.VMEM((tok_rows, width), BF16),
            pltpu.VMEM((tok_rows, width), BF16),
            pltpu.VMEM((total, width), BF16),
            pltpu.VMEM((total, width), BF16),
            pltpu.VMEM((total, width), BF16),
            pltpu.VMEM((total, width), BF16),
            pltpu.VMEM((2, total, width), BF16),
            pltpu.VMEM((2, total, hidden), BF16),
            pltpu.VMEM((2, total, hidden), BF16),
            pltpu.VMEM((4, total, width), BF16),
            pltpu.VMEM((4, total // 2, width), BF16),
            pltpu.VMEM((2, total // 2, width), BF16),
            pltpu.VMEM((2, total // 2, width), BF16),
            pltpu.VMEM((2, total // 4, width), BF16),
            pltpu.VMEM((2, total // 4, width), BF16),
            pltpu.VMEM((tok_rows, width), BF16),
            pltpu.VMEM((tok_rows, 128), F32),
            pltpu.VMEM((tok_rows, 128), F32),
            pltpu.VMEM((2, tok_rows, width), BF16),
            pltpu.VMEM((2, tok_rows, width), BF16),
            pltpu.VMEM((4, COL_STEP, width), BF16),
            pltpu.VMEM((8, width), F32),
            pltpu.VMEM((5, 8, width), F32),
            pltpu.VMEM((groups, 8, width), F32),
            pltpu.SemaphoreType.DMA((4,)),
            pltpu.SemaphoreType.DMA((len(ROUTE_KINDS), groups)),
            pltpu.SemaphoreType.DMA((len(ROUTE_KINDS), groups)),
            pltpu.SemaphoreType.DMA((len(LINK_KINDS), chunks)),
            pltpu.SemaphoreType.DMA((len(LINK_KINDS), chunks)),
            pltpu.SemaphoreType.DMA((len(CORE_KINDS), chunks)),
            pltpu.SemaphoreType.DMA((len(CORE_KINDS), chunks)),
            pltpu.SemaphoreType.DMA((2,)),
            pltpu.SemaphoreType.DMA((2,)),
            pltpu.SemaphoreType.DMA((4,)),
        ],
        compiler_params=pltpu.CompilerParams(
            collective_id=0, has_side_effects=True, vmem_limit_bytes=62 << 20
        ),
        cost_estimate=pl.CostEstimate(
            flops=24 * total * width * hidden, bytes_accessed=40 << 20, transcendentals=0
        ),
    )(
        expert_ids.reshape(1, tok_rows),
        slots.reshape(1, tok_rows),
        tokens,
        cotangent,
        centroids,
        flat(sublayer_norm_gain),
        flat(sublayer_norm_bias),
        flat(up_bias),
        flat(down_bias),
        up_weight,
        down_weight,
    )
    layers = up_weight.shape[0]
    tiles = 4
    row = jax.ShapeDtypeStruct((layers, 1, width), F32)
    return pl.pallas_call(
        functools.partial(widen_kernel, capacity * groups * batches),
        out_shape=[
            jax.ShapeDtypeStruct(tokens.shape, BF16),
            jax.ShapeDtypeStruct(tokens.shape, BF16),
            jax.ShapeDtypeStruct((experts, width), F32),
            row,
            row,
            jax.ShapeDtypeStruct(up_weight.shape, F32),
            jax.ShapeDtypeStruct((layers, 1, hidden), F32),
            jax.ShapeDtypeStruct(down_weight.shape, F32),
            row,
            jax.ShapeDtypeStruct((experts,), F32),
            jax.ShapeDtypeStruct((experts,), F32),
        ],
        in_specs=[hbm, hbm, vmem, vmem, vmem, hbm, hbm],
        out_specs=[hbm, hbm, vmem, vmem, vmem, hbm, vmem, hbm, vmem, vmem, vmem],
        scratch_shapes=[
            pltpu.VMEM((layers, tiles, width // tiles, hidden), BF16),
            pltpu.VMEM((layers, tiles, hidden // tiles, width), BF16),
            pltpu.VMEM((layers, tiles, width // tiles, hidden), F32),
            pltpu.VMEM((layers, tiles, hidden // tiles, width), F32),
            pltpu.SemaphoreType.DMA((2,)),
            pltpu.SemaphoreType.DMA((2, layers, tiles)),
            pltpu.SemaphoreType.DMA((2, layers, tiles)),
        ],
        compiler_params=pltpu.CompilerParams(vmem_limit_bytes=62 << 20),
        cost_estimate=pl.CostEstimate(
            flops=0, bytes_accessed=12 * layers * width * hidden, transcendentals=0
        ),
    )(*outs)


def solution(mesh):
    in_specs = (
        P(("expert", "batch"), None),
        P(("expert", "batch")),
        P(("expert", "batch")),
        P(("expert", "batch")),
        P(),
        P(None, "expert", None),
        P(None, "expert", None),
        P(None, "expert", None, "batch"),
        P(None, "expert", "batch"),
        P(None, "expert", "batch", None),
        P(None, "expert", None),
        P(("expert", "batch"), None),
    )
    out_specs = (
        P(("expert", "batch"), None),
        P(("expert", "batch"), None),
        P(),
        P(None, "expert", None),
        P(None, "expert", None),
        P(None, "expert", None, "batch"),
        P(None, "expert", "batch"),
        P(None, "expert", "batch", None),
        P(None, "expert", None),
        P(),
        P(),
    )
    body = per_device_fused if fused_fits(mesh) else per_device
    return jax.shard_map(
        body, mesh=mesh, in_specs=in_specs, out_specs=out_specs, check_vma=False
    )
```

```python
import functools

import jax
import jax.numpy as jnp
from jax import lax
from jax.experimental import pallas as pl
from jax.experimental.pallas import tpu as pltpu
from jax.sharding import PartitionSpec as P


def gelu_exact(values):
    return jax.nn.gelu(values, approximate=False)


def apply_layer_norm(row_block):
    values = row_block.astype(jnp.float32)
    row_mean = jnp.mean(values, axis=-1, keepdims=True)
    centered = values - row_mean
    row_inverse_scale = lax.rsqrt(jnp.mean(centered * centered, axis=-1, keepdims=True) + 1e-05)
    return (centered * row_inverse_scale, row_inverse_scale)


def per_device(
    tokens,
    lengths,
    expert_ids,
    slots,
    centroids,
    sublayer_norm_gain,
    sublayer_norm_bias,
    up_weight,
    up_bias,
    down_weight,
    down_bias,
    cotangent,
):
    tok_rows, width = tokens.shape
    layers = sublayer_norm_gain.shape[0]
    local_count = up_weight.shape[1]
    expert_count = centroids.shape[0]
    capacity = tok_rows // expert_count
    groups = lax.axis_size("expert")
    batches = lax.axis_size("batch")
    position = jnp.arange(tok_rows, dtype=jnp.int32)
    live = (position < lengths[0]).astype(jnp.float32)[:, None]
    target = jnp.where(slots >= 0, expert_ids * capacity + slots, tok_rows)
    source = jnp.full((tok_rows + 1,), -1, jnp.int32).at[target].set(position)[:tok_rows]
    filled = (source >= 0)[:, None]
    safe_source = jnp.maximum(source, 0)
    safe_target = jnp.minimum(target, tok_rows - 1)

    def pack(values):
        return jnp.where(filled, values[safe_source], jnp.zeros((), values.dtype))

    onehot = (expert_ids[:, None] == jnp.arange(expert_count, dtype=jnp.int32)[None, :]).astype(
        jnp.float32
    )
    logits = jnp.einsum("td,ed->te", tokens, centroids, preferred_element_type=jnp.float32)
    gate = jax.nn.sigmoid(jnp.sum(logits * onehot, axis=1))[:, None]
    used = onehot * live
    usage_gate = jnp.sum(used * gate, axis=0)
    usage_count = jnp.sum(used, axis=0)
    gate_total, count_total = lax.psum((usage_gate, usage_count), ("expert", "batch"))

    def expand_hidden(values, expert_layer_step):
        return values[expert_layer_step].astype(jnp.float32)[None, :, None, :]

    arrived = lax.all_to_all(pack(tokens), "expert", split_axis=0, concat_axis=0, tiled=True)
    current = arrived
    inputs = []
    kept = []
    for expert_layer_step in range(layers):
        gathered = lax.all_gather(current, "batch", axis=0, tiled=True)
        row_layout_grid = gathered.reshape(-1, local_count, capacity, width)
        standardized_input, row_inverse_scale = apply_layer_norm(row_layout_grid)
        normalized_rows = (
            standardized_input * expand_hidden(sublayer_norm_gain, expert_layer_step)
            + expand_hidden(sublayer_norm_bias, expert_layer_step)
        ).astype(jnp.bfloat16)
        pre_rows = jnp.einsum(
            "nlcd,ldf->nlcf",
            normalized_rows,
            up_weight[expert_layer_step],
            preferred_element_type=jnp.float32,
        ) + expand_hidden(up_bias, expert_layer_step)
        hidden_parts = (normalized_rows, pre_rows, gelu_exact(pre_rows).astype(jnp.bfloat16))

        def down_part(start, count, activity=hidden_parts[2], expert_layer_step=expert_layer_step):
            return jnp.einsum(
                "nlcf,lfd->nlcd",
                activity,
                down_weight[expert_layer_step],
                preferred_element_type=jnp.float32,
            )

        mixed_part = lax.psum_scatter(
            down_part(jnp.int32(0), lax.axis_size("batch") * groups).astype(jnp.bfloat16),
            "batch",
            scatter_dimension=0,
            tiled=True,
        ).astype(jnp.float32)
        own_grid = current.reshape(groups, local_count, capacity, width).astype(jnp.float32)
        result = (own_grid + mixed_part + expand_hidden(down_bias, expert_layer_step)).astype(
            jnp.bfloat16
        )
        inputs.append(current)
        kept.append(hidden_parts)
        current = result.reshape(tok_rows, width)
    returned = lax.all_to_all(current, "expert", split_axis=0, concat_axis=0, tiled=True)
    expert_tok = returned[safe_target].astype(jnp.float32)
    mixed = (live * (tokens.astype(jnp.float32) + gate * expert_tok)).astype(jnp.bfloat16)
    upstream = cotangent.astype(jnp.float32) * live
    gate_grad = jnp.sum(upstream * expert_tok, axis=1, keepdims=True)
    logit_grad = (gate_grad * gate * (1.0 - gate)).astype(jnp.bfloat16)
    route_grad = (onehot * logit_grad.astype(jnp.float32)).astype(jnp.bfloat16)
    centroid_part = jnp.einsum("te,td->ed", route_grad, tokens, preferred_element_type=jnp.float32)
    gate_input = jnp.einsum("te,ed->td", route_grad, centroids, preferred_element_type=jnp.float32)
    expert_grad = (gate * upstream).astype(jnp.bfloat16)
    grad_rows = lax.all_to_all(pack(expert_grad), "expert", split_axis=0, concat_axis=0, tiled=True)
    gain_parts = [None] * layers
    shift_parts = [None] * layers
    down_bias_parts = [None] * layers
    up_weight_grads = [None] * layers
    up_bias_grads = [None] * layers
    down_weight_grads = [None] * layers
    for expert_layer_step in range(layers - 1, -1, -1):
        own_rows = inputs[expert_layer_step]
        grads_all = lax.all_gather(grad_rows, "batch", axis=0, tiled=True).reshape(
            -1, local_count, capacity, width
        )
        normed, pre_act, activity = kept[expert_layer_step]
        act_grad = jnp.einsum(
            "nlcd,lfd->nlcf",
            grads_all,
            down_weight[expert_layer_step],
            preferred_element_type=jnp.float32,
        )
        pre_grad = jax.vjp(gelu_exact, pre_act)[1](act_grad)[0].astype(jnp.bfloat16)
        down_weight_grads[expert_layer_step] = jnp.einsum(
            "nlcf,nlcd->lfd", activity, grads_all, preferred_element_type=jnp.float32
        )
        up_weight_grads[expert_layer_step] = jnp.einsum(
            "nlcd,nlcf->ldf", normed, pre_grad, preferred_element_type=jnp.float32
        )
        up_bias_grads[expert_layer_step] = jnp.sum(pre_grad.astype(jnp.float32), axis=(0, 2))

        def up_part(start, count, pre_grad=pre_grad, expert_layer_step=expert_layer_step):
            return jnp.einsum(
                "nlcf,ldf->nlcd",
                pre_grad,
                up_weight[expert_layer_step],
                preferred_element_type=jnp.float32,
            )

        normed_grad = lax.psum_scatter(
            up_part(jnp.int32(0), lax.axis_size("batch") * groups).astype(jnp.bfloat16),
            "batch",
            scatter_dimension=0,
            tiled=True,
        ).astype(jnp.float32)
        out_grad = grad_rows.reshape(groups, local_count, capacity, width).astype(jnp.float32)
        down_bias_parts[expert_layer_step] = jnp.sum(out_grad, axis=(0, 2))
        own_hat, own_scale = apply_layer_norm(
            own_rows.reshape(groups, local_count, capacity, width)
        )
        gain_parts[expert_layer_step] = jnp.sum(normed_grad * own_hat, axis=(0, 2))
        shift_parts[expert_layer_step] = jnp.sum(normed_grad, axis=(0, 2))
        hat_grad = normed_grad * expand_hidden(sublayer_norm_gain, expert_layer_step)
        row_grad = own_scale * (
            hat_grad
            - jnp.mean(hat_grad, axis=-1, keepdims=True)
            - own_hat * jnp.mean(hat_grad * own_hat, axis=-1, keepdims=True)
        )
        grad_rows = (out_grad + row_grad).astype(jnp.bfloat16).reshape(tok_rows, width)
    gain_grad, shift_grad, down_bias_grad = lax.psum(
        (jnp.stack(gain_parts), jnp.stack(shift_parts), jnp.stack(down_bias_parts)), "batch"
    )
    token_back = lax.all_to_all(grad_rows, "expert", split_axis=0, concat_axis=0, tiled=True)
    tokens_grad = (
        upstream + gate_input + live * token_back[safe_target].astype(jnp.float32)
    ).astype(jnp.bfloat16)
    centroid_grad = lax.psum(centroid_part, ("expert", "batch"))
    denominator = jnp.float32(capacity * groups * batches)
    gate_mass = gate_total / denominator
    load = count_total / denominator
    return (
        mixed,
        tokens_grad,
        centroid_grad,
        gain_grad,
        shift_grad,
        jnp.stack(up_weight_grads),
        jnp.stack(up_bias_grads),
        jnp.stack(down_weight_grads),
        down_bias_grad,
        gate_mass,
        load,
    )


MESH = pl.DeviceIdType.MESH
F32 = jnp.float32
BF16 = jnp.bfloat16
ROW_STEP = 64
COL_STEP = 256
EMPTY = 8.0
LINK_KINDS = ("x", "g", "sum0", "out", "ngrad1", "ngrad0")
CORE_KINDS = ("x", "g", "part0", "h", "part1", "ngrad1", "hgrad", "ngrad0")
SCHEDULE = (
    "SX.0 SG.0 SX.1 SX.2",
    "SX.3 SX.4 PX.3 SX.5",
    "U0.3 SG.2 PX.0 D0.3",
    "SG.3 U0.0 SX.6 D0.0",
    "SX.7 PX.1 S0.0 SG.1",
    "U0.1 S0.3 D0.1 PX.2",
    "U0.2 SG.5 S0.1 PG.3",
    "H.3 PG.0 H.0 SG.4",
    "D0.2 SG.6 U1.3 D1.3",
    "U1.0 S0.2 H.1 PG.1",
    "SG.7 U1.1 B1.1 S1.1",
    "B1.3 PG.2 H.2 D1.1",
    "B1.0 SO.1 S1.0 U1.2",
    "B1.2 MX.1 HG.1 W1.1",
    "S1.2 W1.5 D1.0 S1.3",
    "D1.2 HG.0 SO.2 B0.0",
    "W1.3 B0.1 SO.0 W1.2",
    "W1.6 HG.2 B0.2 HG.3",
    "MX.2 SQ.2 SO.3 B0.3",
    "W0.6 SQ.1 SQ.0 W0.0",
    "TG.2 W0.5 MX.0 W0.7",
    "MX.3 W1.4 R1.0 SQ.3",
    "W1.7 TG.1 W1.0 R1.1",
    "W0.4 TG.0 TG.3 R1.2",
    "R0.0 W0.2 R0.1 W0.1",
    "W0.3 UP.1 R0.2 UP.0",
)
ROUTE_KINDS = ("x", "ct", "mixed", "tgrad", "totals")


def fused_fits(mesh):
    groups, batches = mesh.shape["expert"], mesh.shape["batch"]
    return batches == 4 and groups == 8


def rows_at(start, count, unit):
    return pl.ds(pl.multiple_of(start, unit), count)


def loop_rows(count, step, body):
    step = min(step, count)
    for start in range(0, count, step):
        body(start, step)


def normalize(values):
    centered = values - jnp.mean(values, axis=-1, keepdims=True)
    scale = lax.rsqrt(jnp.mean(centered * centered, axis=-1, keepdims=True) + 1e-05)
    return centered * scale, scale


def dot(a, b, dims):
    return lax.dot_general(a, b, (dims, ((), ())), preferred_element_type=F32)


NN = ((1,), (0,))
NT = ((1,), (1,))
TN = ((0,), (0,))


def fused_kernel(
    groups,
    capacity,
    chunks,
    ids_ref,
    slots_ref,
    tok_ref,
    ct_ref,
    cent_ref,
    gain_ref,
    bias_ref,
    up_bias_ref,
    down_bias_ref,
    up_hbm,
    down_hbm,
    mixed_ref,
    tgrad_ref,
    totals_ref,
    small_ref,
    ub_ref,
    up_grad_hbm,
    down_grad_hbm,
    up_w,
    down_w,
    perm,
    pack_x,
    pack_ct,
    xa,
    ga,
    ha,
    hga,
    n_s,
    a_s,
    d_s,
    part,
    part_in,
    half_out,
    half_in,
    own_out,
    own_in,
    ct_own,
    gate_s,
    lg_s,
    back_out,
    back_in,
    stage,
    acc,
    acc_0,
    red,
    totals_in,
    w_sem,
    route_send,
    route_recv,
    link_send,
    link_recv,
    core_send,
    core_recv,
    red_send,
    red_recv,
    out_sem,
):
    tok_rows, width = tok_ref.shape
    hidden = up_w.shape[2]
    per = groups // chunks
    rows_m = per * 4 * capacity
    rows_h = rows_m // 2
    rows_o = rows_m // 4
    e = lax.axis_index("expert")
    b = lax.axis_index("batch")
    x = b // 2
    c = lax.rem(b, 2)
    sib = (e, x * 2 + (1 - c))
    far = (e, (1 - x) * 2 + c)

    def flipped(m):
        out = jnp.int32(0)
        bit = 1
        while bit < groups:
            digit = lax.rem(e // bit, 2)
            out = out + bit * ((1 - digit) if m & bit else digit)
            bit *= 2
        return out

    half = c * rows_h
    sib_half = (1 - c) * rows_h
    own = half + x * rows_o
    pairs = [tuple(range(j * per, (j + 1) * per)) for j in range(chunks)]
    order = pairs[1:] + pairs[:1]
    place = {m: (k, i) for k, ms in enumerate(order) for i, m in enumerate(ms)}
    others = range(1, groups)

    def at_half(k):
        return rows_at(k * rows_m + half, rows_h, rows_h)

    def at_sib_half(k):
        return rows_at(k * rows_m + sib_half, rows_h, rows_h)

    def at_block(m):
        k, i = place[m]
        return rows_at(k * rows_m + own + i * capacity, capacity, capacity)

    def at_all(k):
        return pl.ds(k * rows_m, rows_m)

    def copy_to(device, src, dst, send, recv):
        return pltpu.make_async_remote_copy(
            src_ref=src,
            dst_ref=dst,
            send_sem=send,
            recv_sem=recv,
            device_id=device,
            device_id_type=MESH,
        )

    def route(kind, m):
        n = ROUTE_KINDS.index(kind)
        k, i = place[m]
        to = flipped(m)
        theirs = rows_at(to * capacity, capacity, capacity)
        mine = rows_at(e * capacity, capacity, capacity)
        if kind == "x":
            src = pack_x.at[theirs]
            dst = xa.at[at_block(m)]
        elif kind == "ct":
            src = pack_ct.at[theirs]
            dst = ct_own.at[pl.ds(k * rows_o + i * capacity, capacity)]
        elif kind == "totals":
            src = dst = totals_in.at[e]
        else:
            s = 0 if kind == "mixed" else 1
            src = back_out.at[s, pl.ds(k * rows_o + i * capacity, capacity)]
            dst = back_in.at[s, mine]
        return copy_to((to, b), src, dst, route_send.at[n, m], route_recv.at[n, m])

    def link(kind, k):
        n = LINK_KINDS.index(kind)
        if kind in ("x", "g"):
            src = dst = {"x": xa, "g": ga}[kind].at[at_block(k)]
        elif kind in ("sum0", "ngrad1"):
            s = 0 if kind == "sum0" else 1
            at = pl.ds(k * rows_h, rows_h)
            src, dst = half_out.at[s, at], half_in.at[s, at]
        else:
            s = 0 if kind == "out" else 1
            at = pl.ds(k * rows_o, rows_o)
            src, dst = own_out.at[s, at], own_in.at[s, at]
        return copy_to(far, src, dst, link_send.at[n, k], link_recv.at[n, k])

    def core(kind, k):
        n = CORE_KINDS.index(kind)
        whole = {"x": xa, "g": ga, "h": ha, "hgrad": hga}
        if kind in whole:
            src = dst = whole[kind].at[at_half(k)]
        else:
            s = ("part0", "part1", "ngrad1", "ngrad0").index(kind)
            src = part.at[s, at_sib_half(k)]
            dst = part_in.at[s, pl.ds(k * rows_h, rows_h)]
        return copy_to(sib, src, dst, core_send.at[n, k], core_recv.at[n, k])

    barrier = pltpu.get_barrier_semaphore()
    peers = [sib, far] + [(flipped(m), b) for m in range(1, groups)]
    for peer in peers:
        pl.semaphore_signal(barrier, inc=1, device_id=peer, device_id_type=MESH)
    loads = []
    for j in range(2):
        loads.append(pltpu.make_async_copy(up_hbm.at[j, 0], up_w.at[j], w_sem.at[2 * j]))
        loads.append(pltpu.make_async_copy(down_hbm.at[j, 0], down_w.at[j], w_sem.at[2 * j + 1]))
    for load in loads:
        load.start()
    target = jnp.where(
        slots_ref[...] >= 0, ids_ref[...] * capacity + slots_ref[...], -1
    )
    slot = lax.broadcasted_iota(jnp.int32, (tok_rows, tok_rows), 0)
    onehot = jnp.where(slot == target, 1.0, 0.0)
    perm[...] = onehot.astype(BF16)
    empty = EMPTY * (1.0 - jnp.sum(onehot, axis=1, keepdims=True))

    def pack(start, step):
        cols = rows_at(start, step, step)
        pack_x[:, cols] = (dot(perm[...], tok_ref[:, cols], NN) + empty).astype(BF16)
        pack_ct[:, cols] = dot(perm[...], ct_ref[:, cols], NN).astype(BF16)

    loop_rows(width, COL_STEP, pack)
    acc[...] = jnp.zeros_like(acc)
    acc_0[...] = jnp.zeros_like(acc_0)
    cent_rows = cent_ref[...].astype(F32)
    cent_at = lax.broadcasted_iota(jnp.int32, cent_rows.shape, 0)
    cent = jnp.sum(jnp.where(cent_at == e, cent_rows, 0.0), axis=0, keepdims=True)
    pl.semaphore_wait(barrier, len(peers))
    near = 2 * per
    for kind, masks in (
        ("x", range(1, near)),
        ("ct", range(1, per)),
        ("x", range(near, groups)),
        ("ct", range(per, groups)),
    ):
        for m in masks:
            route(kind, m).start()
    mine = rows_at(e * capacity, capacity, capacity)
    xa[at_block(0)] = pack_x[mine]
    first_k, first_i = place[0]
    ct_own[pl.ds(first_k * rows_o + first_i * capacity, capacity)] = pack_ct[mine]

    def send_x(m):
        if m:
            route("x", m).wait_recv()
        link("x", m).start()

    def send_g(m):
        if m:
            route("ct", m).wait_recv()
        k, i = place[m]
        at_o = pl.ds(k * rows_o + i * capacity, capacity)
        values = xa[at_block(m)].astype(F32)
        gate = jax.nn.sigmoid(jnp.sum(values * cent, axis=-1, keepdims=True))
        gate_s[at_o] = jnp.broadcast_to(gate, (capacity, 128))
        ga[at_block(m)] = (gate * ct_own[at_o].astype(F32)).astype(BF16)
        used = jnp.where(values[:, 0:1] < 7.0, 1.0, 0.0)
        acc[3:4] += jnp.broadcast_to(jnp.sum(used * gate, axis=0, keepdims=True), (1, width))
        acc[4:5] += jnp.broadcast_to(jnp.sum(used, axis=0, keepdims=True), (1, width))
        link("g", m).start()

    def spread(kind, k):
        for m in order[k]:
            link(kind, m).wait_recv()
        core(kind, k).start()

    def up_step(j, rows_ref, k):
        gain = gain_ref[j : j + 1].astype(F32)
        bias = bias_ref[j : j + 1].astype(F32)

        def norm(start, step):
            at = rows_at(k * rows_m + start, step, step)
            rhat, _ = normalize(rows_ref[at].astype(F32))
            n_s[j, at] = (rhat * gain + bias).astype(BF16)

        loop_rows(rows_m, ROW_STEP, norm)

        def up(start, step):
            cols = rows_at(start, step, step)
            pre = dot(n_s[j, at_all(k)], up_w[j, :, cols], NN) + up_bias_ref[j : j + 1, cols].astype(
                F32
            )
            cdf = 0.5 * (1.0 + lax.erf(pre * (0.5**0.5)))
            pdf = jnp.exp(-0.5 * pre * pre) * 0.3989422804014327
            a_s[j, at_all(k), cols] = (pre * cdf).astype(BF16)
            d_s[j, at_all(k), cols] = (cdf + pre * pdf).astype(BF16)

        loop_rows(hidden, COL_STEP, up)

    def down_step(j, k):
        kind = "part%d" % j

        def down(start, step):
            cols = rows_at(start, step, step)
            part[j, at_all(k), cols] = dot(a_s[j, at_all(k)], down_w[j, :, cols], NN).astype(BF16)

        loop_rows(width, COL_STEP, down)
        core(kind, k).start()

    def back_step(j, grads_ref, k):
        kind = "ngrad%d" % j
        s = 3 - j

        def act(start, step):
            cols = rows_at(start, step, step)
            grad = dot(grads_ref[at_all(k)], down_w[j, cols, :], NT)
            d_s[j, at_all(k), cols] = (grad * d_s[j, at_all(k), cols].astype(F32)).astype(BF16)

        loop_rows(hidden, COL_STEP, act)

        def up_back(start, step):
            cols = rows_at(start, step, step)
            part[s, at_all(k), cols] = dot(d_s[j, at_all(k)], up_w[j, cols, :], NT).astype(BF16)

        loop_rows(width, COL_STEP, up_back)
        core(kind, k).start()

    def sum_half(kind, link_kind, k):
        s = ("part0", "part1", "ngrad1", "ngrad0").index(kind)
        o = ("sum0", "ngrad1").index(link_kind)
        core(kind, k).wait_recv()

        def add_half(start, step):
            at = rows_at(k * rows_m + half + start, step, step)
            at_h = rows_at(k * rows_h + start, step, step)
            total = part[s, at].astype(F32) + part_in[s, at_h].astype(F32)
            half_out[o, at_h] = total.astype(BF16)

        loop_rows(rows_h, ROW_STEP, add_half)
        link(link_kind, k).start()

    def sum_far(kind, link_kind, k):
        s = ("part0", "part1", "ngrad1", "ngrad0").index(kind)
        o = ("out", "ngrad0").index(link_kind)
        core(kind, k).wait_recv()

        def add_far(start, step):
            at = rows_at(k * rows_m + half + (1 - x) * rows_o + start, step, step)
            at_h = rows_at(k * rows_h + (1 - x) * rows_o + start, step, step)
            at_o = rows_at(k * rows_o + start, step, step)
            total = part[s, at].astype(F32) + part_in[s, at_h].astype(F32)
            own_out[o, at_o] = total.astype(BF16)

        loop_rows(rows_o, ROW_STEP, add_far)
        link(link_kind, k).start()

    def sum_own(s, o, k, start, step):
        at = rows_at(k * rows_m + own + start, step, step)
        at_h = rows_at(k * rows_h + x * rows_o + start, step, step)
        at_o = rows_at(k * rows_o + start, step, step)
        mine = part[s, at].astype(F32) + part_in[s, at_h].astype(F32)
        return mine + own_in[o, at_o].astype(F32)

    def make_h(k):
        link("sum0", k).wait_recv()
        shift = down_bias_ref[0:1].astype(F32)

        def add_h(start, step):
            at = rows_at(k * rows_m + half + start, step, step)
            at_h = rows_at(k * rows_h + start, step, step)
            total = half_out[0, at_h].astype(F32) + half_in[0, at_h].astype(F32)
            ha[at] = (xa[at].astype(F32) + total + shift).astype(BF16)

        loop_rows(rows_h, ROW_STEP, add_h)
        core("h", k).start()

    def norm_back(rows, ngrad, gain):
        rhat, scale = normalize(rows)
        q = ngrad * gain
        back = scale * (
            q - jnp.mean(q, axis=-1, keepdims=True) - rhat * jnp.mean(q * rhat, axis=-1, keepdims=True)
        )
        return back, rhat

    def make_hgrad(k):
        link("ngrad1", k).wait_recv()
        gain = gain_ref[1:2].astype(F32)

        def grad_h(start, step):
            at = rows_at(k * rows_m + half + start, step, step)
            at_h = rows_at(k * rows_h + start, step, step)
            ngrad = half_out[1, at_h].astype(F32) + half_in[1, at_h].astype(F32)
            back, rhat = norm_back(ha[at].astype(F32), ngrad, gain)
            hga[at] = (ga[at].astype(F32) + back).astype(BF16)
            acc[0:1] += 0.5 * jnp.sum(ngrad * rhat, axis=0, keepdims=True)
            acc[1:2] += 0.5 * jnp.sum(ngrad, axis=0, keepdims=True)

        loop_rows(rows_h, ROW_STEP, grad_h)
        core("hgrad", k).start()

    def give_back(kind, k):
        for m in order[k]:
            if m:
                route(kind, m).start()
            else:
                s = 0 if kind == "mixed" else 1
                _, i = place[0]
                back_in[s, mine] = back_out[s, pl.ds(k * rows_o + i * capacity, capacity)]

    def make_mixed(k):
        link("out", k).wait_recv()
        shift = down_bias_ref[1:2].astype(F32)

        def mix(start, step):
            at = rows_at(k * rows_m + own + start, step, step)
            at_o = rows_at(k * rows_o + start, step, step)
            out = (ha[at].astype(F32) + sum_own(1, 0, k, start, step) + shift).astype(BF16).astype(F32)
            rows = xa[at].astype(F32)
            gate = gate_s[at_o][:, 0:1]
            back_out[0, at_o] = (rows + gate * out).astype(BF16)
            along = jnp.sum(ct_own[at_o].astype(F32) * out, axis=-1, keepdims=True)
            lgrad = (along * gate * (1.0 - gate)).astype(BF16).astype(F32)
            lg_s[at_o] = jnp.broadcast_to(lgrad, (step, 128))
            acc[2:3] += jnp.sum(lgrad * rows, axis=0, keepdims=True)

        loop_rows(rows_o, ROW_STEP, mix)
        give_back("mixed", k)

    def make_tgrad(k):
        link("ngrad0", k).wait_recv()
        gain = gain_ref[0:1].astype(F32)

        def grad_t(start, step):
            at = rows_at(k * rows_m + own + start, step, step)
            at_o = rows_at(k * rows_o + start, step, step)
            ngrad = sum_own(3, 1, k, start, step)
            back, rhat = norm_back(xa[at].astype(F32), ngrad, gain)
            back = (hga[at].astype(F32) + back).astype(BF16).astype(F32)
            back_out[1, at_o] = (
                ct_own[at_o].astype(F32) + lg_s[at_o][:, 0:1] * cent + back
            ).astype(BF16)
            acc_0[0:1] += jnp.sum(ngrad * rhat, axis=0, keepdims=True)
            acc_0[1:2] += jnp.sum(ngrad, axis=0, keepdims=True)

        loop_rows(rows_o, ROW_STEP, grad_t)
        give_back("tgrad", k)

    def column_sums(rows_ref):
        def one(i, total):
            values = rows_ref[rows_at(i * ROW_STEP, ROW_STEP, ROW_STEP)].astype(F32)
            return total + jnp.sum(values, axis=0, keepdims=True)

        return lax.fori_loop(
            0, rows_ref.shape[0] // ROW_STEP, one, jnp.zeros((1, rows_ref.shape[1]), F32)
        )

    tiles = []

    def weight_grad(j, t):
        grads_ref = (hga, ga)[j]
        downs = hidden // COL_STEP
        if t < downs:
            into, left, right = down_grad_hbm, a_s.at[j], grads_ref
        else:
            into, left, right = up_grad_hbm, n_s.at[j], d_s.at[j]
        if t == 0:
            small_ref[4 + j : 5 + j] = column_sums(right)
        if t == downs:
            ub_ref[j : j + 1] = column_sums(right)
        slot = len(tiles) % stage.shape[0]
        if len(tiles) >= stage.shape[0]:
            tiles[len(tiles) - stage.shape[0]].wait()
        at = pl.ds(t % downs * COL_STEP, COL_STEP)
        stage[slot] = dot(left[:, at], right[...], TN).astype(BF16)
        tiles.append(pltpu.make_async_copy(stage.at[slot], into.at[j, 0, at], out_sem.at[slot]))
        tiles[-1].start()

    def over(s):
        return copy_to(sib, red.at[s, 0], red.at[s, 1], red_send.at[s, 0], red_recv.at[s, 0])

    def across(s):
        return copy_to(far, red.at[s, 0], red.at[s, 2], red_send.at[s, 1], red_recv.at[s, 1])

    def total(s, step):
        if step == 0:
            red[s, 0] = (acc, acc_0)[s][...]
            over(s).start()
        elif step == 1:
            over(s).wait()
            red[s, 0] = red[s, 0] + red[s, 1]
            across(s).start()
        else:
            across(s).wait()
            sums = red[s, 0] + red[s, 2]
            if s == 0:
                small_ref[1:2] = sums[0:1]
                small_ref[3:4] = sums[1:2]
                for i in range(width // 128):
                    totals_in[e, i : i + 1] = sums[2:3, i * 128 : (i + 1) * 128]
                totals_in[e, 8:10] = sums[3:5, 0:128]
                for m in others:
                    route("totals", m).start()
            else:
                small_ref[0:1] = sums[0:1]
                small_ref[2:3] = sums[1:2]

    def unpack(s):
        kind, out_ref = (("mixed", mixed_ref), ("tgrad", tgrad_ref))[s]
        for m in others:
            route(kind, m).wait_recv()

        def place_tokens(start, step):
            cols = rows_at(start, step, step)
            out_ref[:, cols] = dot(perm[...], back_in[s, :, cols], TN).astype(BF16)

        loop_rows(width, COL_STEP, place_tokens)

    steps = range(chunks)

    def up_0(k):
        if k == first_use[0]:
            loads[0].wait()
        core("x", k).wait_recv()
        up_step(0, xa, k)

    def down_0(k):
        if k == first_use[2]:
            loads[1].wait()
        down_step(0, k)

    def up_1(k):
        if k == first_use[1]:
            loads[2].wait()
            loads[3].wait()
        core("h", k).wait_recv()
        up_step(1, ha, k)

    def back_1(k):
        core("g", k).wait_recv()
        back_step(1, ga, k)

    def back_0(k):
        core("hgrad", k).wait_recv()
        back_step(0, hga, k)

    tasks = {
        "SX": send_x,
        "SG": send_g,
        "PX": functools.partial(spread, "x"),
        "PG": functools.partial(spread, "g"),
        "U0": up_0,
        "D0": down_0,
        "S0": functools.partial(sum_half, "part0", "sum0"),
        "H": make_h,
        "U1": up_1,
        "B1": back_1,
        "D1": functools.partial(down_step, 1),
        "S1": functools.partial(sum_half, "ngrad1", "ngrad1"),
        "SO": functools.partial(sum_far, "part1", "out"),
        "HG": make_hgrad,
        "MX": make_mixed,
        "B0": back_0,
        "SQ": functools.partial(sum_far, "ngrad0", "ngrad0"),
        "TG": make_tgrad,
        "W1": functools.partial(weight_grad, 1),
        "W0": functools.partial(weight_grad, 0),
        "R1": functools.partial(total, 0),
        "R0": functools.partial(total, 1),
        "UP": unpack,
    }
    plan = [word.split(".") for line in SCHEDULE for word in line.split()]
    first_use = [next(int(k) for name, k in plan if name == u) for u in ("U0", "U1", "D0")]
    for name, k in plan:
        tasks[name](int(k))

    for m in others:
        route("totals", m).wait_recv()
    totals_ref[...] = totals_in[...]
    for tile in tiles[-stage.shape[0] :]:
        tile.wait()
    for m in others:
        for kind in ROUTE_KINDS:
            route(kind, m).wait_send()
    for m in range(groups):
        for kind in LINK_KINDS[:2]:
            link(kind, m).wait_send()
    for k in steps:
        for kind in LINK_KINDS[2:]:
            link(kind, k).wait_send()
        for kind in CORE_KINDS:
            core(kind, k).wait_send()


def widen_kernel(
    denominator,
    mixed_hbm,
    tgrad_hbm,
    totals_ref,
    small_ref,
    ub_ref,
    up_hbm,
    down_hbm,
    mixed_out,
    tgrad_out,
    cent_out,
    gain_out,
    shift_out,
    up_out,
    ub_out,
    down_out,
    db_out,
    mass_out,
    load_out,
    rows_s,
    up_low,
    down_low,
    up_wide,
    down_wide,
    row_sem,
    in_sem,
    out_sem,
):
    layers, tiles, rows = up_low.shape[:3]
    moves = [
        (
            pltpu.make_async_copy(src, rows_s.at[n], row_sem.at[0, n]),
            pltpu.make_async_copy(rows_s.at[n], dst, row_sem.at[1, n]),
        )
        for n, (src, dst) in enumerate(((mixed_hbm, mixed_out), (tgrad_hbm, tgrad_out)))
    ]
    pairs = []
    for j in range(layers):
        for n, (src, low, wide, dst) in enumerate(
            ((down_hbm, down_low, down_wide, down_out), (up_hbm, up_low, up_wide, up_out))
        ):
            for t in range(tiles):
                at = pl.ds(t * rows, rows)
                pairs.append(
                    (
                        pltpu.make_async_copy(src.at[j, 0, at], low.at[j, t], in_sem.at[n, j, t]),
                        low.at[j, t],
                        wide.at[j, t],
                        pltpu.make_async_copy(wide.at[j, t], dst.at[j, 0, at], out_sem.at[n, j, t]),
                    )
                )
    for pair in pairs:
        pair[0].start()
    for arrive, _ in moves:
        arrive.start()
    for arrive, low, wide, leave in pairs:
        arrive.wait()
        wide[...] = low[...].astype(F32)
        leave.start()
    for arrive, leave in moves:
        arrive.wait()
        leave.start()
    for i in range(cent_out.shape[1] // 128):
        cent_out[:, i * 128 : (i + 1) * 128] = totals_ref[:, i]
    for j in range(layers):
        gain_out[j] = small_ref[j : j + 1]
        shift_out[j] = small_ref[2 + j : 3 + j]
        db_out[j] = small_ref[4 + j : 5 + j]
        ub_out[j] = ub_ref[j : j + 1]
    experts = totals_ref.shape[0]
    diagonal = lax.broadcasted_iota(jnp.int32, (experts, 128), 0) == lax.broadcasted_iota(
        jnp.int32, (experts, 128), 1
    )
    for out, n in ((mass_out, 8), (load_out, 9)):
        values = jnp.sum(jnp.where(diagonal, totals_ref[:, n], 0.0), axis=0)
        out[...] = values[0:experts] / jnp.float32(denominator)
    for _, _, _, leave in pairs:
        leave.wait()
    for _, leave in moves:
        leave.wait()


def per_device_fused(
    tokens,
    lengths,
    expert_ids,
    slots,
    centroids,
    sublayer_norm_gain,
    sublayer_norm_bias,
    up_weight,
    up_bias,
    down_weight,
    down_bias,
    cotangent,
):
    tok_rows, width = tokens.shape
    groups = lax.axis_size("expert")
    batches = lax.axis_size("batch")
    experts = centroids.shape[0]
    capacity = tok_rows // experts
    hidden = up_weight.shape[3]
    chunks = 4
    total = groups * batches * capacity
    def flat(values):
        return values.reshape(values.shape[0], -1)

    vmem = pl.BlockSpec(memory_space=pltpu.VMEM)
    hbm = pl.BlockSpec(memory_space=pl.ANY)
    outs = pl.pallas_call(
        functools.partial(fused_kernel, groups, capacity, chunks),
        out_shape=[
            jax.ShapeDtypeStruct((tok_rows, width), BF16),
            jax.ShapeDtypeStruct((tok_rows, width), BF16),
            jax.ShapeDtypeStruct((groups, 16, 128), F32),
            jax.ShapeDtypeStruct((8, width), F32),
            jax.ShapeDtypeStruct((8, hidden), F32),
            jax.ShapeDtypeStruct(up_weight.shape, BF16),
            jax.ShapeDtypeStruct(down_weight.shape, BF16),
        ],
        in_specs=[vmem] * 9 + [hbm] * 2,
        out_specs=[vmem] * 5 + [hbm] * 2,
        scratch_shapes=[
            pltpu.VMEM((2, width, hidden), BF16),
            pltpu.VMEM((2, hidden, width), BF16),
            pltpu.VMEM((tok_rows, tok_rows), BF16),
            pltpu.VMEM((tok_rows, width), BF16),
            pltpu.VMEM((tok_rows, width), BF16),
            pltpu.VMEM((total, width), BF16),
            pltpu.VMEM((total, width), BF16),
            pltpu.VMEM((total, width), BF16),
            pltpu.VMEM((total, width), BF16),
            pltpu.VMEM((2, total, width), BF16),
            pltpu.VMEM((2, total, hidden), BF16),
            pltpu.VMEM((2, total, hidden), BF16),
            pltpu.VMEM((4, total, width), BF16),
            pltpu.VMEM((4, total // 2, width), BF16),
            pltpu.VMEM((2, total // 2, width), BF16),
            pltpu.VMEM((2, total // 2, width), BF16),
            pltpu.VMEM((2, total // 4, width), BF16),
            pltpu.VMEM((2, total // 4, width), BF16),
            pltpu.VMEM((tok_rows, width), BF16),
            pltpu.VMEM((tok_rows, 128), F32),
            pltpu.VMEM((tok_rows, 128), F32),
            pltpu.VMEM((2, tok_rows, width), BF16),
            pltpu.VMEM((2, tok_rows, width), BF16),
            pltpu.VMEM((4, COL_STEP, width), BF16),
            pltpu.VMEM((8, width), F32),
            pltpu.VMEM((8, width), F32),
            pltpu.VMEM((2, 3, 8, width), F32),
            pltpu.VMEM((groups, 16, 128), F32),
            pltpu.SemaphoreType.DMA((4,)),
            pltpu.SemaphoreType.DMA((len(ROUTE_KINDS), groups)),
            pltpu.SemaphoreType.DMA((len(ROUTE_KINDS), groups)),
            pltpu.SemaphoreType.DMA((len(LINK_KINDS), groups)),
            pltpu.SemaphoreType.DMA((len(LINK_KINDS), groups)),
            pltpu.SemaphoreType.DMA((len(CORE_KINDS), chunks)),
            pltpu.SemaphoreType.DMA((len(CORE_KINDS), chunks)),
            pltpu.SemaphoreType.DMA((2, 2)),
            pltpu.SemaphoreType.DMA((2, 2)),
            pltpu.SemaphoreType.DMA((4,)),
        ],
        compiler_params=pltpu.CompilerParams(
            collective_id=0, has_side_effects=True, vmem_limit_bytes=62 << 20
        ),
        cost_estimate=pl.CostEstimate(
            flops=24 * total * width * hidden, bytes_accessed=40 << 20, transcendentals=0
        ),
    )(
        expert_ids.reshape(1, tok_rows),
        slots.reshape(1, tok_rows),
        tokens,
        cotangent,
        centroids,
        flat(sublayer_norm_gain),
        flat(sublayer_norm_bias),
        flat(up_bias),
        flat(down_bias),
        up_weight,
        down_weight,
    )
    layers = up_weight.shape[0]
    tiles = 2
    row = jax.ShapeDtypeStruct((layers, 1, width), F32)
    return pl.pallas_call(
        functools.partial(widen_kernel, capacity * groups * batches),
        out_shape=[
            jax.ShapeDtypeStruct(tokens.shape, BF16),
            jax.ShapeDtypeStruct(tokens.shape, BF16),
            jax.ShapeDtypeStruct((experts, width), F32),
            row,
            row,
            jax.ShapeDtypeStruct(up_weight.shape, F32),
            jax.ShapeDtypeStruct((layers, 1, hidden), F32),
            jax.ShapeDtypeStruct(down_weight.shape, F32),
            row,
            jax.ShapeDtypeStruct((experts,), F32),
            jax.ShapeDtypeStruct((experts,), F32),
        ],
        in_specs=[hbm, hbm, vmem, vmem, vmem, hbm, hbm],
        out_specs=[hbm, hbm, vmem, vmem, vmem, hbm, vmem, hbm, vmem, vmem, vmem],
        scratch_shapes=[
            pltpu.VMEM((2,) + tokens.shape, BF16),
            pltpu.VMEM((layers, tiles, width // tiles, hidden), BF16),
            pltpu.VMEM((layers, tiles, hidden // tiles, width), BF16),
            pltpu.VMEM((layers, tiles, width // tiles, hidden), F32),
            pltpu.VMEM((layers, tiles, hidden // tiles, width), F32),
            pltpu.SemaphoreType.DMA((2, 2)),
            pltpu.SemaphoreType.DMA((2, layers, tiles)),
            pltpu.SemaphoreType.DMA((2, layers, tiles)),
        ],
        compiler_params=pltpu.CompilerParams(vmem_limit_bytes=62 << 20),
        cost_estimate=pl.CostEstimate(
            flops=0, bytes_accessed=12 * layers * width * hidden, transcendentals=0
        ),
    )(*outs)


def solution(mesh):
    in_specs = (
        P(("expert", "batch"), None),
        P(("expert", "batch")),
        P(("expert", "batch")),
        P(("expert", "batch")),
        P(),
        P(None, "expert", None),
        P(None, "expert", None),
        P(None, "expert", None, "batch"),
        P(None, "expert", "batch"),
        P(None, "expert", "batch", None),
        P(None, "expert", None),
        P(("expert", "batch"), None),
    )
    out_specs = (
        P(("expert", "batch"), None),
        P(("expert", "batch"), None),
        P(),
        P(None, "expert", None),
        P(None, "expert", None),
        P(None, "expert", None, "batch"),
        P(None, "expert", "batch"),
        P(None, "expert", "batch", None),
        P(None, "expert", None),
        P(),
        P(),
    )
    body = per_device_fused if fused_fits(mesh) else per_device
    return jax.shard_map(
        body, mesh=mesh, in_specs=in_specs, out_specs=out_specs, check_vma=False
    )
```

```python
import functools

import jax
import jax.numpy as jnp
from jax import lax
from jax.experimental import pallas as pl
from jax.experimental.pallas import tpu as pltpu
from jax.sharding import PartitionSpec as P


def gelu_exact(values):
    return jax.nn.gelu(values, approximate=False)


def apply_layer_norm(row_block):
    values = row_block.astype(jnp.float32)
    row_mean = jnp.mean(values, axis=-1, keepdims=True)
    centered = values - row_mean
    row_inverse_scale = lax.rsqrt(jnp.mean(centered * centered, axis=-1, keepdims=True) + 1e-05)
    return (centered * row_inverse_scale, row_inverse_scale)


def per_device(
    tokens,
    lengths,
    expert_ids,
    slots,
    centroids,
    sublayer_norm_gain,
    sublayer_norm_bias,
    up_weight,
    up_bias,
    down_weight,
    down_bias,
    cotangent,
):
    tok_rows, width = tokens.shape
    layers = sublayer_norm_gain.shape[0]
    local_count = up_weight.shape[1]
    expert_count = centroids.shape[0]
    capacity = tok_rows // expert_count
    groups = lax.axis_size("expert")
    batches = lax.axis_size("batch")
    position = jnp.arange(tok_rows, dtype=jnp.int32)
    live = (position < lengths[0]).astype(jnp.float32)[:, None]
    target = jnp.where(slots >= 0, expert_ids * capacity + slots, tok_rows)
    source = jnp.full((tok_rows + 1,), -1, jnp.int32).at[target].set(position)[:tok_rows]
    filled = (source >= 0)[:, None]
    safe_source = jnp.maximum(source, 0)
    safe_target = jnp.minimum(target, tok_rows - 1)

    def pack(values):
        return jnp.where(filled, values[safe_source], jnp.zeros((), values.dtype))

    onehot = (expert_ids[:, None] == jnp.arange(expert_count, dtype=jnp.int32)[None, :]).astype(
        jnp.float32
    )
    logits = jnp.einsum("td,ed->te", tokens, centroids, preferred_element_type=jnp.float32)
    gate = jax.nn.sigmoid(jnp.sum(logits * onehot, axis=1))[:, None]
    used = onehot * live
    usage_gate = jnp.sum(used * gate, axis=0)
    usage_count = jnp.sum(used, axis=0)
    gate_total, count_total = lax.psum((usage_gate, usage_count), ("expert", "batch"))

    def expand_hidden(values, expert_layer_step):
        return values[expert_layer_step].astype(jnp.float32)[None, :, None, :]

    arrived = lax.all_to_all(pack(tokens), "expert", split_axis=0, concat_axis=0, tiled=True)
    current = arrived
    inputs = []
    kept = []
    for expert_layer_step in range(layers):
        gathered = lax.all_gather(current, "batch", axis=0, tiled=True)
        row_layout_grid = gathered.reshape(-1, local_count, capacity, width)
        standardized_input, row_inverse_scale = apply_layer_norm(row_layout_grid)
        normalized_rows = (
            standardized_input * expand_hidden(sublayer_norm_gain, expert_layer_step)
            + expand_hidden(sublayer_norm_bias, expert_layer_step)
        ).astype(jnp.bfloat16)
        pre_rows = jnp.einsum(
            "nlcd,ldf->nlcf",
            normalized_rows,
            up_weight[expert_layer_step],
            preferred_element_type=jnp.float32,
        ) + expand_hidden(up_bias, expert_layer_step)
        hidden_parts = (normalized_rows, pre_rows, gelu_exact(pre_rows).astype(jnp.bfloat16))

        def down_part(start, count, activity=hidden_parts[2], expert_layer_step=expert_layer_step):
            return jnp.einsum(
                "nlcf,lfd->nlcd",
                activity,
                down_weight[expert_layer_step],
                preferred_element_type=jnp.float32,
            )

        mixed_part = lax.psum_scatter(
            down_part(jnp.int32(0), lax.axis_size("batch") * groups).astype(jnp.bfloat16),
            "batch",
            scatter_dimension=0,
            tiled=True,
        ).astype(jnp.float32)
        own_grid = current.reshape(groups, local_count, capacity, width).astype(jnp.float32)
        result = (own_grid + mixed_part + expand_hidden(down_bias, expert_layer_step)).astype(
            jnp.bfloat16
        )
        inputs.append(current)
        kept.append(hidden_parts)
        current = result.reshape(tok_rows, width)
    returned = lax.all_to_all(current, "expert", split_axis=0, concat_axis=0, tiled=True)
    expert_tok = returned[safe_target].astype(jnp.float32)
    mixed = (live * (tokens.astype(jnp.float32) + gate * expert_tok)).astype(jnp.bfloat16)
    upstream = cotangent.astype(jnp.float32) * live
    gate_grad = jnp.sum(upstream * expert_tok, axis=1, keepdims=True)
    logit_grad = (gate_grad * gate * (1.0 - gate)).astype(jnp.bfloat16)
    route_grad = (onehot * logit_grad.astype(jnp.float32)).astype(jnp.bfloat16)
    centroid_part = jnp.einsum("te,td->ed", route_grad, tokens, preferred_element_type=jnp.float32)
    gate_input = jnp.einsum("te,ed->td", route_grad, centroids, preferred_element_type=jnp.float32)
    expert_grad = (gate * upstream).astype(jnp.bfloat16)
    grad_rows = lax.all_to_all(pack(expert_grad), "expert", split_axis=0, concat_axis=0, tiled=True)
    gain_parts = [None] * layers
    shift_parts = [None] * layers
    down_bias_parts = [None] * layers
    up_weight_grads = [None] * layers
    up_bias_grads = [None] * layers
    down_weight_grads = [None] * layers
    for expert_layer_step in range(layers - 1, -1, -1):
        own_rows = inputs[expert_layer_step]
        grads_all = lax.all_gather(grad_rows, "batch", axis=0, tiled=True).reshape(
            -1, local_count, capacity, width
        )
        normed, pre_act, activity = kept[expert_layer_step]
        act_grad = jnp.einsum(
            "nlcd,lfd->nlcf",
            grads_all,
            down_weight[expert_layer_step],
            preferred_element_type=jnp.float32,
        )
        pre_grad = jax.vjp(gelu_exact, pre_act)[1](act_grad)[0].astype(jnp.bfloat16)
        down_weight_grads[expert_layer_step] = jnp.einsum(
            "nlcf,nlcd->lfd", activity, grads_all, preferred_element_type=jnp.float32
        )
        up_weight_grads[expert_layer_step] = jnp.einsum(
            "nlcd,nlcf->ldf", normed, pre_grad, preferred_element_type=jnp.float32
        )
        up_bias_grads[expert_layer_step] = jnp.sum(pre_grad.astype(jnp.float32), axis=(0, 2))

        def up_part(start, count, pre_grad=pre_grad, expert_layer_step=expert_layer_step):
            return jnp.einsum(
                "nlcf,ldf->nlcd",
                pre_grad,
                up_weight[expert_layer_step],
                preferred_element_type=jnp.float32,
            )

        normed_grad = lax.psum_scatter(
            up_part(jnp.int32(0), lax.axis_size("batch") * groups).astype(jnp.bfloat16),
            "batch",
            scatter_dimension=0,
            tiled=True,
        ).astype(jnp.float32)
        out_grad = grad_rows.reshape(groups, local_count, capacity, width).astype(jnp.float32)
        down_bias_parts[expert_layer_step] = jnp.sum(out_grad, axis=(0, 2))
        own_hat, own_scale = apply_layer_norm(
            own_rows.reshape(groups, local_count, capacity, width)
        )
        gain_parts[expert_layer_step] = jnp.sum(normed_grad * own_hat, axis=(0, 2))
        shift_parts[expert_layer_step] = jnp.sum(normed_grad, axis=(0, 2))
        hat_grad = normed_grad * expand_hidden(sublayer_norm_gain, expert_layer_step)
        row_grad = own_scale * (
            hat_grad
            - jnp.mean(hat_grad, axis=-1, keepdims=True)
            - own_hat * jnp.mean(hat_grad * own_hat, axis=-1, keepdims=True)
        )
        grad_rows = (out_grad + row_grad).astype(jnp.bfloat16).reshape(tok_rows, width)
    gain_grad, shift_grad, down_bias_grad = lax.psum(
        (jnp.stack(gain_parts), jnp.stack(shift_parts), jnp.stack(down_bias_parts)), "batch"
    )
    token_back = lax.all_to_all(grad_rows, "expert", split_axis=0, concat_axis=0, tiled=True)
    tokens_grad = (
        upstream + gate_input + live * token_back[safe_target].astype(jnp.float32)
    ).astype(jnp.bfloat16)
    centroid_grad = lax.psum(centroid_part, ("expert", "batch"))
    denominator = jnp.float32(capacity * groups * batches)
    gate_mass = gate_total / denominator
    load = count_total / denominator
    return (
        mixed,
        tokens_grad,
        centroid_grad,
        gain_grad,
        shift_grad,
        jnp.stack(up_weight_grads),
        jnp.stack(up_bias_grads),
        jnp.stack(down_weight_grads),
        down_bias_grad,
        gate_mass,
        load,
    )


MESH = pl.DeviceIdType.MESH
F32 = jnp.float32
BF16 = jnp.bfloat16
ROW_STEP = 64
COL_STEP = 256
EMPTY = 8.0
LINK_KINDS = ("x", "g", "sum0", "out", "ngrad1", "ngrad0")
CORE_KINDS = ("x", "g", "part0", "h", "part1", "ngrad1", "hgrad", "ngrad0")
SCHEDULE = (
    "SX.0 SG.0 SX.1 SX.2",
    "SX.3 SX.4 PX.3 SX.5",
    "U0.3 SG.2 PX.0 D0.3",
    "SG.3 U0.0 SX.6 D0.0",
    "SX.7 PX.1 S0.0 SG.1",
    "U0.1 S0.3 D0.1 PX.2",
    "U0.2 SG.5 S0.1 PG.3",
    "H.3 PG.0 H.0 SG.4",
    "D0.2 SG.6 U1.3 D1.3",
    "U1.0 S0.2 H.1 PG.1",
    "SG.7 U1.1 B1.1 S1.1",
    "B1.3 PG.2 H.2 D1.1",
    "B1.0 SO.1 S1.0 U1.2",
    "B1.2 MX.1 HG.1 W1.1",
    "S1.2 D1.0 S1.3 D1.2",
    "HG.0 SO.2 B0.0 W1.3",
    "B0.1 SO.0 W1.2 HG.2",
    "B0.2 HG.3 MX.2 SQ.2",
    "SO.3 B0.3 SQ.1 SQ.0",
    "W0.0 TG.2 MX.0 MX.3",
    "R1.0 SQ.3 TG.1 W1.0",
    "R1.1 TG.0 TG.3 R1.2",
    "R0.0 W0.2 R0.1 W0.1",
    "W0.3 UP.1 R0.2 UP.0",
)
PART_SLOT = {"part0": 0, "part1": 0, "ngrad1": 1, "ngrad0": 1}
ROUTE_KINDS = ("x", "ct", "mixed", "tgrad", "totals")


def fused_fits(mesh):
    groups, batches = mesh.shape["expert"], mesh.shape["batch"]
    return batches == 4 and groups == 8


def rows_at(start, count, unit):
    return pl.ds(pl.multiple_of(start, unit), count)


def loop_rows(count, step, body):
    step = min(step, count)
    for start in range(0, count, step):
        body(start, step)


def loop_tiles(count, step, body):
    def one(i, carry):
        body(pl.multiple_of(i * step, step), step)
        return carry

    lax.fori_loop(0, count // step, one, 0)


def normalize(values):
    centered = values - jnp.mean(values, axis=-1, keepdims=True)
    scale = lax.rsqrt(jnp.mean(centered * centered, axis=-1, keepdims=True) + 1e-05)
    return centered * scale, scale


def dot(a, b, dims):
    return lax.dot_general(a, b, (dims, ((), ())), preferred_element_type=F32)


NN = ((1,), (0,))
NT = ((1,), (1,))
TN = ((0,), (0,))


def fused_kernel(
    groups,
    capacity,
    chunks,
    ids_ref,
    slots_ref,
    tok_ref,
    ct_ref,
    cent_ref,
    gain_ref,
    bias_ref,
    up_bias_ref,
    down_bias_ref,
    up_hbm,
    down_hbm,
    mixed_ref,
    tgrad_ref,
    totals_ref,
    small_ref,
    ub_ref,
    up_grad_ref,
    down_grad_ref,
    up_w,
    down_w,
    perm,
    pack_x,
    pack_ct,
    xa,
    ga,
    ha,
    hga,
    n_s,
    a_s,
    d_s,
    part,
    part_in,
    half_out,
    half_in,
    own_out,
    own_in,
    ct_own,
    gate_s,
    lg_s,
    back_out,
    back_in,
    acc,
    acc_0,
    red,
    totals_in,
    w_sem,
    route_send,
    route_recv,
    link_send,
    link_recv,
    core_send,
    core_recv,
    red_send,
    red_recv,
):
    tok_rows, width = tok_ref.shape
    hidden = up_w.shape[2]
    per = groups // chunks
    rows_m = per * 4 * capacity
    rows_h = rows_m // 2
    rows_o = rows_m // 4
    e = lax.axis_index("expert")
    b = lax.axis_index("batch")
    x = b // 2
    c = lax.rem(b, 2)
    sib = (e, x * 2 + (1 - c))
    far = (e, (1 - x) * 2 + c)

    def flipped(m):
        out = jnp.int32(0)
        bit = 1
        while bit < groups:
            digit = lax.rem(e // bit, 2)
            out = out + bit * ((1 - digit) if m & bit else digit)
            bit *= 2
        return out

    half = c * rows_h
    sib_half = (1 - c) * rows_h
    own = half + x * rows_o
    pairs = [tuple(range(j * per, (j + 1) * per)) for j in range(chunks)]
    order = pairs[1:] + pairs[:1]
    place = {m: (k, i) for k, ms in enumerate(order) for i, m in enumerate(ms)}
    others = range(1, groups)

    def at_half(k):
        return rows_at(k * rows_m + half, rows_h, rows_h)

    def at_sib_half(k):
        return rows_at(k * rows_m + sib_half, rows_h, rows_h)

    def at_block(m):
        k, i = place[m]
        return rows_at(k * rows_m + own + i * capacity, capacity, capacity)

    def at_all(k):
        return pl.ds(k * rows_m, rows_m)

    def copy_to(device, src, dst, send, recv):
        return pltpu.make_async_remote_copy(
            src_ref=src,
            dst_ref=dst,
            send_sem=send,
            recv_sem=recv,
            device_id=device,
            device_id_type=MESH,
        )

    def route(kind, m):
        n = ROUTE_KINDS.index(kind)
        k, i = place[m]
        to = flipped(m)
        theirs = rows_at(to * capacity, capacity, capacity)
        mine = rows_at(e * capacity, capacity, capacity)
        if kind == "x":
            src = pack_x.at[theirs]
            dst = xa.at[at_block(m)]
        elif kind == "ct":
            src = pack_ct.at[theirs]
            dst = ct_own.at[pl.ds(k * rows_o + i * capacity, capacity)]
        elif kind == "totals":
            src = dst = totals_in.at[e]
        else:
            s = 0 if kind == "mixed" else 1
            src = back_out.at[s, pl.ds(k * rows_o + i * capacity, capacity)]
            dst = back_in.at[s, mine]
        return copy_to((to, b), src, dst, route_send.at[n, m], route_recv.at[n, m])

    def link(kind, k):
        n = LINK_KINDS.index(kind)
        if kind in ("x", "g"):
            src = dst = {"x": xa, "g": ga}[kind].at[at_block(k)]
        elif kind in ("sum0", "ngrad1"):
            s = 0 if kind == "sum0" else 1
            at = pl.ds(k * rows_h, rows_h)
            src, dst = half_out.at[s, at], half_in.at[s, at]
        else:
            s = 0 if kind == "out" else 1
            at = pl.ds(k * rows_o, rows_o)
            src, dst = own_out.at[s, at], own_in.at[s, at]
        return copy_to(far, src, dst, link_send.at[n, k], link_recv.at[n, k])

    def core(kind, k):
        n = CORE_KINDS.index(kind)
        whole = {"x": xa, "g": ga, "h": ha, "hgrad": hga}
        if kind in whole:
            src = dst = whole[kind].at[at_half(k)]
        else:
            s = PART_SLOT[kind]
            src = part.at[s, at_sib_half(k)]
            dst = part_in.at[s, pl.ds(k * rows_h, rows_h)]
        return copy_to(sib, src, dst, core_send.at[n, k], core_recv.at[n, k])

    barrier = pltpu.get_barrier_semaphore()
    peers = [sib, far] + [(flipped(m), b) for m in range(1, groups)]
    for peer in peers:
        pl.semaphore_signal(barrier, inc=1, device_id=peer, device_id_type=MESH)
    loads = []
    for j in range(2):
        loads.append(pltpu.make_async_copy(up_hbm.at[j, 0], up_w.at[j], w_sem.at[2 * j]))
        loads.append(pltpu.make_async_copy(down_hbm.at[j, 0], down_w.at[j], w_sem.at[2 * j + 1]))
    for load in loads:
        load.start()
    target = jnp.where(
        slots_ref[...] >= 0, ids_ref[...] * capacity + slots_ref[...], -1
    )
    slot = lax.broadcasted_iota(jnp.int32, (tok_rows, tok_rows), 0)
    onehot = jnp.where(slot == target, 1.0, 0.0)
    perm[...] = onehot.astype(BF16)
    empty = EMPTY * (1.0 - jnp.sum(onehot, axis=1, keepdims=True))

    def pack(start, step):
        cols = rows_at(start, step, step)
        pack_x[:, cols] = (dot(perm[...], tok_ref[:, cols], NN) + empty).astype(BF16)
        pack_ct[:, cols] = dot(perm[...], ct_ref[:, cols], NN).astype(BF16)

    loop_rows(width, COL_STEP, pack)
    acc[...] = jnp.zeros_like(acc)
    acc_0[...] = jnp.zeros_like(acc_0)
    cent_rows = cent_ref[...].astype(F32)
    cent_at = lax.broadcasted_iota(jnp.int32, cent_rows.shape, 0)
    cent = jnp.sum(jnp.where(cent_at == e, cent_rows, 0.0), axis=0, keepdims=True)
    pl.semaphore_wait(barrier, len(peers))
    near = 2 * per
    for kind, masks in (
        ("x", range(1, near)),
        ("ct", range(1, per)),
        ("x", range(near, groups)),
        ("ct", range(per, groups)),
    ):
        for m in masks:
            route(kind, m).start()
    mine = rows_at(e * capacity, capacity, capacity)
    xa[at_block(0)] = pack_x[mine]
    first_k, first_i = place[0]
    ct_own[pl.ds(first_k * rows_o + first_i * capacity, capacity)] = pack_ct[mine]

    def send_x(m):
        if m:
            route("x", m).wait_recv()
        link("x", m).start()

    def send_g(m):
        if m:
            route("ct", m).wait_recv()
        k, i = place[m]
        at_o = pl.ds(k * rows_o + i * capacity, capacity)
        values = xa[at_block(m)].astype(F32)
        gate = jax.nn.sigmoid(jnp.sum(values * cent, axis=-1, keepdims=True))
        gate_s[at_o] = jnp.broadcast_to(gate, (capacity, 128))
        ga[at_block(m)] = (gate * ct_own[at_o].astype(F32)).astype(BF16)
        used = jnp.where(values[:, 0:1] < 7.0, 1.0, 0.0)
        acc[3:4] += jnp.broadcast_to(jnp.sum(used * gate, axis=0, keepdims=True), (1, width))
        acc[4:5] += jnp.broadcast_to(jnp.sum(used, axis=0, keepdims=True), (1, width))
        link("g", m).start()

    def spread(kind, k):
        for m in order[k]:
            link(kind, m).wait_recv()
        core(kind, k).start()

    def up_step(j, rows_ref, k):
        gain = gain_ref[j : j + 1].astype(F32)
        bias = bias_ref[j : j + 1].astype(F32)

        def norm(start, step):
            at = rows_at(k * rows_m + start, step, step)
            rhat, _ = normalize(rows_ref[at].astype(F32))
            n_s[j, at] = (rhat * gain + bias).astype(BF16)

        loop_tiles(rows_m, 2 * ROW_STEP, norm)

        def up(start, step):
            cols = rows_at(start, step, step)
            pre = dot(n_s[j, at_all(k)], up_w[j, :, cols], NN) + up_bias_ref[j : j + 1, cols].astype(
                F32
            )
            cdf = 0.5 * (1.0 + lax.erf(pre * (0.5**0.5)))
            pdf = jnp.exp(-0.5 * pre * pre) * 0.3989422804014327
            a_s[j, at_all(k), cols] = (pre * cdf).astype(BF16)
            d_s[j, at_all(k), cols] = (cdf + pre * pdf).astype(BF16)

        loop_tiles(hidden, 2 * COL_STEP, up)

    def down_step(j, k):
        kind = "part%d" % j
        if j == 1:
            core("part0", k).wait_send()

        def down(start, step):
            cols = rows_at(start, step, step)
            part[0, at_all(k), cols] = dot(a_s[j, at_all(k)], down_w[j, :, cols], NN).astype(BF16)

        loop_tiles(width, 2 * COL_STEP, down)
        core(kind, k).start()

    def back_step(j, grads_ref, k):
        kind = "ngrad%d" % j
        if j == 0:
            core("ngrad1", k).wait_send()

        def act(start, step):
            cols = rows_at(start, step, step)
            grad = dot(grads_ref[at_all(k)], down_w[j, cols, :], NT)
            d_s[j, at_all(k), cols] = (grad * d_s[j, at_all(k), cols].astype(F32)).astype(BF16)

        loop_tiles(hidden, 2 * COL_STEP, act)

        def up_back(start, step):
            cols = rows_at(start, step, step)
            part[1, at_all(k), cols] = dot(d_s[j, at_all(k)], up_w[j, cols, :], NT).astype(BF16)

        loop_tiles(width, 2 * COL_STEP, up_back)
        core(kind, k).start()

    def sum_half(kind, link_kind, k):
        s = PART_SLOT[kind]
        o = ("sum0", "ngrad1").index(link_kind)
        core(kind, k).wait_recv()

        def add_half(start, step):
            at = rows_at(k * rows_m + half + start, step, step)
            at_h = rows_at(k * rows_h + start, step, step)
            total = part[s, at].astype(F32) + part_in[s, at_h].astype(F32)
            half_out[o, at_h] = total.astype(BF16)

        loop_rows(rows_h, ROW_STEP, add_half)
        link(link_kind, k).start()

    def sum_far(kind, link_kind, k):
        s = PART_SLOT[kind]
        o = ("out", "ngrad0").index(link_kind)
        core(kind, k).wait_recv()

        def add_far(start, step):
            at = rows_at(k * rows_m + half + (1 - x) * rows_o + start, step, step)
            at_h = rows_at(k * rows_h + (1 - x) * rows_o + start, step, step)
            at_o = rows_at(k * rows_o + start, step, step)
            total = part[s, at].astype(F32) + part_in[s, at_h].astype(F32)
            own_out[o, at_o] = total.astype(BF16)

        loop_rows(rows_o, ROW_STEP, add_far)
        link(link_kind, k).start()

    def sum_own(s, o, k, start, step):
        at = rows_at(k * rows_m + own + start, step, step)
        at_h = rows_at(k * rows_h + x * rows_o + start, step, step)
        at_o = rows_at(k * rows_o + start, step, step)
        mine = part[s, at].astype(F32) + part_in[s, at_h].astype(F32)
        return mine + own_in[o, at_o].astype(F32)

    def make_h(k):
        link("sum0", k).wait_recv()
        shift = down_bias_ref[0:1].astype(F32)

        def add_h(start, step):
            at = rows_at(k * rows_m + half + start, step, step)
            at_h = rows_at(k * rows_h + start, step, step)
            total = half_out[0, at_h].astype(F32) + half_in[0, at_h].astype(F32)
            ha[at] = (xa[at].astype(F32) + total + shift).astype(BF16)

        loop_rows(rows_h, ROW_STEP, add_h)
        core("h", k).start()

    def norm_back(rows, ngrad, gain):
        rhat, scale = normalize(rows)
        q = ngrad * gain
        back = scale * (
            q - jnp.mean(q, axis=-1, keepdims=True) - rhat * jnp.mean(q * rhat, axis=-1, keepdims=True)
        )
        return back, rhat

    def make_hgrad(k):
        link("ngrad1", k).wait_recv()
        gain = gain_ref[1:2].astype(F32)

        def grad_h(start, step):
            at = rows_at(k * rows_m + half + start, step, step)
            at_h = rows_at(k * rows_h + start, step, step)
            ngrad = half_out[1, at_h].astype(F32) + half_in[1, at_h].astype(F32)
            back, rhat = norm_back(ha[at].astype(F32), ngrad, gain)
            hga[at] = (ga[at].astype(F32) + back).astype(BF16)
            acc[0:1] += 0.5 * jnp.sum(ngrad * rhat, axis=0, keepdims=True)
            acc[1:2] += 0.5 * jnp.sum(ngrad, axis=0, keepdims=True)

        loop_tiles(rows_h, ROW_STEP, grad_h)
        core("hgrad", k).start()

    def give_back(kind, k):
        for m in order[k]:
            if m:
                route(kind, m).start()
            else:
                s = 0 if kind == "mixed" else 1
                _, i = place[0]
                back_in[s, mine] = back_out[s, pl.ds(k * rows_o + i * capacity, capacity)]

    def make_mixed(k):
        link("out", k).wait_recv()
        shift = down_bias_ref[1:2].astype(F32)

        def mix(start, step):
            at = rows_at(k * rows_m + own + start, step, step)
            at_o = rows_at(k * rows_o + start, step, step)
            out = (ha[at].astype(F32) + sum_own(0, 0, k, start, step) + shift).astype(BF16).astype(F32)
            rows = xa[at].astype(F32)
            gate = gate_s[at_o][:, 0:1]
            back_out[0, at_o] = (rows + gate * out).astype(BF16)
            along = jnp.sum(ct_own[at_o].astype(F32) * out, axis=-1, keepdims=True)
            lgrad = (along * gate * (1.0 - gate)).astype(BF16).astype(F32)
            lg_s[at_o] = jnp.broadcast_to(lgrad, (step, 128))
            acc[2:3] += jnp.sum(lgrad * rows, axis=0, keepdims=True)

        loop_rows(rows_o, ROW_STEP, mix)
        give_back("mixed", k)

    def make_tgrad(k):
        link("ngrad0", k).wait_recv()
        gain = gain_ref[0:1].astype(F32)

        def grad_t(start, step):
            at = rows_at(k * rows_m + own + start, step, step)
            at_o = rows_at(k * rows_o + start, step, step)
            ngrad = sum_own(1, 1, k, start, step)
            back, rhat = norm_back(xa[at].astype(F32), ngrad, gain)
            back = (hga[at].astype(F32) + back).astype(BF16).astype(F32)
            back_out[1, at_o] = (
                ct_own[at_o].astype(F32) + lg_s[at_o][:, 0:1] * cent + back
            ).astype(BF16)
            acc_0[0:1] += jnp.sum(ngrad * rhat, axis=0, keepdims=True)
            acc_0[1:2] += jnp.sum(ngrad, axis=0, keepdims=True)

        loop_rows(rows_o, ROW_STEP, grad_t)
        give_back("tgrad", k)

    def column_sums(rows_ref):
        def one(i, total):
            values = rows_ref[rows_at(i * ROW_STEP, ROW_STEP, ROW_STEP)].astype(F32)
            return total + jnp.sum(values, axis=0, keepdims=True)

        return lax.fori_loop(
            0, rows_ref.shape[0] // ROW_STEP, one, jnp.zeros((1, rows_ref.shape[1]), F32)
        )

    def weight_grad(j, q):
        grads_ref = (hga, ga)[j]
        into, left, right = (
            (down_grad_ref, a_s.at[j], grads_ref),
            (up_grad_ref, n_s.at[j], d_s.at[j]),
        )[q // 2]
        if q == 0:
            small_ref[4 + j : 5 + j] = column_sums(right)
        if q == 2:
            ub_ref[j : j + 1] = column_sums(right)
        count = left.shape[1] // 2

        def tile(start, step):
            at = rows_at(q % 2 * count + start, step, step)
            into[j, 0, at] = dot(left[:, at], right[...], TN).astype(BF16)

        loop_tiles(count, COL_STEP, tile)

    def over(s):
        return copy_to(sib, red.at[s, 0], red.at[s, 1], red_send.at[s, 0], red_recv.at[s, 0])

    def across(s):
        return copy_to(far, red.at[s, 0], red.at[s, 2], red_send.at[s, 1], red_recv.at[s, 1])

    def total(s, step):
        if step == 0:
            red[s, 0] = (acc, acc_0)[s][...]
            over(s).start()
        elif step == 1:
            over(s).wait()
            red[s, 0] = red[s, 0] + red[s, 1]
            across(s).start()
        else:
            across(s).wait()
            sums = red[s, 0] + red[s, 2]
            if s == 0:
                small_ref[1:2] = sums[0:1]
                small_ref[3:4] = sums[1:2]
                for i in range(width // 128):
                    totals_in[e, i : i + 1] = sums[2:3, i * 128 : (i + 1) * 128]
                totals_in[e, 8:10] = sums[3:5, 0:128]
                for m in others:
                    route("totals", m).start()
            else:
                small_ref[0:1] = sums[0:1]
                small_ref[2:3] = sums[1:2]

    def unpack(s):
        kind, out_ref = (("mixed", mixed_ref), ("tgrad", tgrad_ref))[s]
        for m in others:
            route(kind, m).wait_recv()

        def place_tokens(start, step):
            cols = rows_at(start, step, step)
            out_ref[:, cols] = dot(perm[...], back_in[s, :, cols], TN).astype(BF16)

        loop_rows(width, COL_STEP, place_tokens)

    steps = range(chunks)

    def up_0(k):
        if k == first_use[0]:
            loads[0].wait()
        core("x", k).wait_recv()
        up_step(0, xa, k)

    def down_0(k):
        if k == first_use[2]:
            loads[1].wait()
        down_step(0, k)

    def up_1(k):
        if k == first_use[1]:
            loads[2].wait()
            loads[3].wait()
        core("h", k).wait_recv()
        up_step(1, ha, k)

    def back_1(k):
        core("g", k).wait_recv()
        back_step(1, ga, k)

    def back_0(k):
        core("hgrad", k).wait_recv()
        back_step(0, hga, k)

    tasks = {
        "SX": send_x,
        "SG": send_g,
        "PX": functools.partial(spread, "x"),
        "PG": functools.partial(spread, "g"),
        "U0": up_0,
        "D0": down_0,
        "S0": functools.partial(sum_half, "part0", "sum0"),
        "H": make_h,
        "U1": up_1,
        "B1": back_1,
        "D1": functools.partial(down_step, 1),
        "S1": functools.partial(sum_half, "ngrad1", "ngrad1"),
        "SO": functools.partial(sum_far, "part1", "out"),
        "HG": make_hgrad,
        "MX": make_mixed,
        "B0": back_0,
        "SQ": functools.partial(sum_far, "ngrad0", "ngrad0"),
        "TG": make_tgrad,
        "W1": functools.partial(weight_grad, 1),
        "W0": functools.partial(weight_grad, 0),
        "R1": functools.partial(total, 0),
        "R0": functools.partial(total, 1),
        "UP": unpack,
    }
    plan = [word.split(".") for line in SCHEDULE for word in line.split()]
    first_use = [next(int(k) for name, k in plan if name == u) for u in ("U0", "U1", "D0")]
    for name, k in plan:
        tasks[name](int(k))

    for m in others:
        route("totals", m).wait_recv()
    totals_ref[...] = totals_in[...]
    for m in others:
        for kind in ROUTE_KINDS:
            route(kind, m).wait_send()
    for m in range(groups):
        for kind in LINK_KINDS[:2]:
            link(kind, m).wait_send()
    for k in steps:
        for kind in LINK_KINDS[2:]:
            link(kind, k).wait_send()
        for kind in CORE_KINDS:
            if kind not in ("part0", "ngrad1"):
                core(kind, k).wait_send()


def widen_kernel(
    denominator,
    mixed_ref,
    tgrad_ref,
    totals_ref,
    small_ref,
    ub_ref,
    up_ref,
    down_ref,
    mixed_out,
    tgrad_out,
    cent_out,
    gain_out,
    shift_out,
    up_out,
    ub_out,
    down_out,
    db_out,
    mass_out,
    load_out,
    up_wide,
    down_wide,
    row_sem,
    out_sem,
):
    layers, tiles, rows = up_wide.shape[:3]
    leaving = [
        pltpu.make_async_copy(mixed_ref, mixed_out, row_sem.at[0]),
        pltpu.make_async_copy(tgrad_ref, tgrad_out, row_sem.at[1]),
    ]
    for move in leaving:
        move.start()
    for j in range(layers):
        for n, (src, wide, dst) in enumerate(
            ((down_ref, down_wide, down_out), (up_ref, up_wide, up_out))
        ):
            for t in range(tiles):
                at = pl.ds(t * rows, rows)
                wide[j, t] = src[j, 0, at].astype(F32)
                move = pltpu.make_async_copy(wide.at[j, t], dst.at[j, 0, at], out_sem.at[n, j, t])
                move.start()
                leaving.append(move)
    for i in range(cent_out.shape[1] // 128):
        cent_out[:, i * 128 : (i + 1) * 128] = totals_ref[:, i]
    for j in range(layers):
        gain_out[j] = small_ref[j : j + 1]
        shift_out[j] = small_ref[2 + j : 3 + j]
        db_out[j] = small_ref[4 + j : 5 + j]
        ub_out[j] = ub_ref[j : j + 1]
    experts = totals_ref.shape[0]
    diagonal = lax.broadcasted_iota(jnp.int32, (experts, 128), 0) == lax.broadcasted_iota(
        jnp.int32, (experts, 128), 1
    )
    for out, n in ((mass_out, 8), (load_out, 9)):
        values = jnp.sum(jnp.where(diagonal, totals_ref[:, n], 0.0), axis=0)
        out[...] = values[0:experts] / jnp.float32(denominator)
    for move in leaving:
        move.wait()


def per_device_fused(
    tokens,
    lengths,
    expert_ids,
    slots,
    centroids,
    sublayer_norm_gain,
    sublayer_norm_bias,
    up_weight,
    up_bias,
    down_weight,
    down_bias,
    cotangent,
):
    tok_rows, width = tokens.shape
    groups = lax.axis_size("expert")
    batches = lax.axis_size("batch")
    experts = centroids.shape[0]
    capacity = tok_rows // experts
    hidden = up_weight.shape[3]
    chunks = 4
    total = groups * batches * capacity
    def flat(values):
        return values.reshape(values.shape[0], -1)

    vmem = pl.BlockSpec(memory_space=pltpu.VMEM)
    hbm = pl.BlockSpec(memory_space=pl.ANY)
    outs = pl.pallas_call(
        functools.partial(fused_kernel, groups, capacity, chunks),
        out_shape=[
            pltpu.VMEM((tok_rows, width), BF16),
            pltpu.VMEM((tok_rows, width), BF16),
            pltpu.VMEM((groups, 16, 128), F32),
            pltpu.VMEM((8, width), F32),
            pltpu.VMEM((8, hidden), F32),
            pltpu.VMEM(up_weight.shape, BF16),
            pltpu.VMEM(down_weight.shape, BF16),
        ],
        in_specs=[vmem] * 9 + [hbm] * 2,
        out_specs=[vmem] * 7,
        scratch_shapes=[
            pltpu.VMEM((2, width, hidden), BF16),
            pltpu.VMEM((2, hidden, width), BF16),
            pltpu.VMEM((tok_rows, tok_rows), BF16),
            pltpu.VMEM((tok_rows, width), BF16),
            pltpu.VMEM((tok_rows, width), BF16),
            pltpu.VMEM((total, width), BF16),
            pltpu.VMEM((total, width), BF16),
            pltpu.VMEM((total, width), BF16),
            pltpu.VMEM((total, width), BF16),
            pltpu.VMEM((2, total, width), BF16),
            pltpu.VMEM((2, total, hidden), BF16),
            pltpu.VMEM((2, total, hidden), BF16),
            pltpu.VMEM((2, total, width), BF16),
            pltpu.VMEM((2, total // 2, width), BF16),
            pltpu.VMEM((2, total // 2, width), BF16),
            pltpu.VMEM((2, total // 2, width), BF16),
            pltpu.VMEM((2, total // 4, width), BF16),
            pltpu.VMEM((2, total // 4, width), BF16),
            pltpu.VMEM((tok_rows, width), BF16),
            pltpu.VMEM((tok_rows, 128), F32),
            pltpu.VMEM((tok_rows, 128), F32),
            pltpu.VMEM((2, tok_rows, width), BF16),
            pltpu.VMEM((2, tok_rows, width), BF16),
            pltpu.VMEM((8, width), F32),
            pltpu.VMEM((8, width), F32),
            pltpu.VMEM((2, 3, 8, width), F32),
            pltpu.VMEM((groups, 16, 128), F32),
            pltpu.SemaphoreType.DMA((4,)),
            pltpu.SemaphoreType.DMA((len(ROUTE_KINDS), groups)),
            pltpu.SemaphoreType.DMA((len(ROUTE_KINDS), groups)),
            pltpu.SemaphoreType.DMA((len(LINK_KINDS), groups)),
            pltpu.SemaphoreType.DMA((len(LINK_KINDS), groups)),
            pltpu.SemaphoreType.DMA((len(CORE_KINDS), chunks)),
            pltpu.SemaphoreType.DMA((len(CORE_KINDS), chunks)),
            pltpu.SemaphoreType.DMA((2, 2)),
            pltpu.SemaphoreType.DMA((2, 2)),
        ],
        compiler_params=pltpu.CompilerParams(
            collective_id=0, has_side_effects=True, vmem_limit_bytes=52 << 20
        ),
        cost_estimate=pl.CostEstimate(
            flops=24 * total * width * hidden, bytes_accessed=40 << 20, transcendentals=0
        ),
    )(
        expert_ids.reshape(1, tok_rows),
        slots.reshape(1, tok_rows),
        tokens,
        cotangent,
        centroids,
        flat(sublayer_norm_gain),
        flat(sublayer_norm_bias),
        flat(up_bias),
        flat(down_bias),
        up_weight,
        down_weight,
    )
    layers = up_weight.shape[0]
    tiles = 4
    row = jax.ShapeDtypeStruct((layers, 1, width), F32)
    return pl.pallas_call(
        functools.partial(widen_kernel, capacity * groups * batches),
        out_shape=[
            jax.ShapeDtypeStruct(tokens.shape, BF16),
            jax.ShapeDtypeStruct(tokens.shape, BF16),
            jax.ShapeDtypeStruct((experts, width), F32),
            row,
            row,
            jax.ShapeDtypeStruct(up_weight.shape, F32),
            jax.ShapeDtypeStruct((layers, 1, hidden), F32),
            jax.ShapeDtypeStruct(down_weight.shape, F32),
            row,
            jax.ShapeDtypeStruct((experts,), F32),
            jax.ShapeDtypeStruct((experts,), F32),
        ],
        in_specs=[vmem] * 7,
        out_specs=[hbm, hbm, vmem, vmem, vmem, hbm, vmem, hbm, vmem, vmem, vmem],
        scratch_shapes=[
            pltpu.VMEM((layers, tiles, width // tiles, hidden), F32),
            pltpu.VMEM((layers, tiles, hidden // tiles, width), F32),
            pltpu.SemaphoreType.DMA((2,)),
            pltpu.SemaphoreType.DMA((2, layers, tiles)),
        ],
        compiler_params=pltpu.CompilerParams(vmem_limit_bytes=24 << 20),
        cost_estimate=pl.CostEstimate(
            flops=0, bytes_accessed=12 * layers * width * hidden, transcendentals=0
        ),
    )(*(pltpu.with_memory_space_constraint(out, pltpu.VMEM) for out in outs))


def solution(mesh):
    in_specs = (
        P(("expert", "batch"), None),
        P(("expert", "batch")),
        P(("expert", "batch")),
        P(("expert", "batch")),
        P(),
        P(None, "expert", None),
        P(None, "expert", None),
        P(None, "expert", None, "batch"),
        P(None, "expert", "batch"),
        P(None, "expert", "batch", None),
        P(None, "expert", None),
        P(("expert", "batch"), None),
    )
    out_specs = (
        P(("expert", "batch"), None),
        P(("expert", "batch"), None),
        P(),
        P(None, "expert", None),
        P(None, "expert", None),
        P(None, "expert", None, "batch"),
        P(None, "expert", "batch"),
        P(None, "expert", "batch", None),
        P(None, "expert", None),
        P(),
        P(),
    )
    body = per_device_fused if fused_fits(mesh) else per_device
    return jax.shard_map(
        body, mesh=mesh, in_specs=in_specs, out_specs=out_specs, check_vma=False
    )
```

```python
import functools

import jax
import jax.numpy as jnp
from jax import lax
from jax.experimental import pallas as pl
from jax.experimental.pallas import tpu as pltpu
from jax.sharding import PartitionSpec as P


def gelu_exact(values):
    return jax.nn.gelu(values, approximate=False)


def apply_layer_norm(row_block):
    values = row_block.astype(jnp.float32)
    row_mean = jnp.mean(values, axis=-1, keepdims=True)
    centered = values - row_mean
    row_inverse_scale = lax.rsqrt(jnp.mean(centered * centered, axis=-1, keepdims=True) + 1e-05)
    return (centered * row_inverse_scale, row_inverse_scale)


def per_device(
    tokens,
    lengths,
    expert_ids,
    slots,
    centroids,
    sublayer_norm_gain,
    sublayer_norm_bias,
    up_weight,
    up_bias,
    down_weight,
    down_bias,
    cotangent,
):
    tok_rows, width = tokens.shape
    layers = sublayer_norm_gain.shape[0]
    local_count = up_weight.shape[1]
    expert_count = centroids.shape[0]
    capacity = tok_rows // expert_count
    groups = lax.axis_size("expert")
    batches = lax.axis_size("batch")
    position = jnp.arange(tok_rows, dtype=jnp.int32)
    live = (position < lengths[0]).astype(jnp.float32)[:, None]
    target = jnp.where(slots >= 0, expert_ids * capacity + slots, tok_rows)
    source = jnp.full((tok_rows + 1,), -1, jnp.int32).at[target].set(position)[:tok_rows]
    filled = (source >= 0)[:, None]
    safe_source = jnp.maximum(source, 0)
    safe_target = jnp.minimum(target, tok_rows - 1)

    def pack(values):
        return jnp.where(filled, values[safe_source], jnp.zeros((), values.dtype))

    onehot = (expert_ids[:, None] == jnp.arange(expert_count, dtype=jnp.int32)[None, :]).astype(
        jnp.float32
    )
    logits = jnp.einsum("td,ed->te", tokens, centroids, preferred_element_type=jnp.float32)
    gate = jax.nn.sigmoid(jnp.sum(logits * onehot, axis=1))[:, None]
    used = onehot * live
    usage_gate = jnp.sum(used * gate, axis=0)
    usage_count = jnp.sum(used, axis=0)
    gate_total, count_total = lax.psum((usage_gate, usage_count), ("expert", "batch"))

    def expand_hidden(values, expert_layer_step):
        return values[expert_layer_step].astype(jnp.float32)[None, :, None, :]

    arrived = lax.all_to_all(pack(tokens), "expert", split_axis=0, concat_axis=0, tiled=True)
    current = arrived
    inputs = []
    kept = []
    for expert_layer_step in range(layers):
        gathered = lax.all_gather(current, "batch", axis=0, tiled=True)
        row_layout_grid = gathered.reshape(-1, local_count, capacity, width)
        standardized_input, row_inverse_scale = apply_layer_norm(row_layout_grid)
        normalized_rows = (
            standardized_input * expand_hidden(sublayer_norm_gain, expert_layer_step)
            + expand_hidden(sublayer_norm_bias, expert_layer_step)
        ).astype(jnp.bfloat16)
        pre_rows = jnp.einsum(
            "nlcd,ldf->nlcf",
            normalized_rows,
            up_weight[expert_layer_step],
            preferred_element_type=jnp.float32,
        ) + expand_hidden(up_bias, expert_layer_step)
        hidden_parts = (normalized_rows, pre_rows, gelu_exact(pre_rows).astype(jnp.bfloat16))

        def down_part(start, count, activity=hidden_parts[2], expert_layer_step=expert_layer_step):
            return jnp.einsum(
                "nlcf,lfd->nlcd",
                activity,
                down_weight[expert_layer_step],
                preferred_element_type=jnp.float32,
            )

        mixed_part = lax.psum_scatter(
            down_part(jnp.int32(0), lax.axis_size("batch") * groups).astype(jnp.bfloat16),
            "batch",
            scatter_dimension=0,
            tiled=True,
        ).astype(jnp.float32)
        own_grid = current.reshape(groups, local_count, capacity, width).astype(jnp.float32)
        result = (own_grid + mixed_part + expand_hidden(down_bias, expert_layer_step)).astype(
            jnp.bfloat16
        )
        inputs.append(current)
        kept.append(hidden_parts)
        current = result.reshape(tok_rows, width)
    returned = lax.all_to_all(current, "expert", split_axis=0, concat_axis=0, tiled=True)
    expert_tok = returned[safe_target].astype(jnp.float32)
    mixed = (live * (tokens.astype(jnp.float32) + gate * expert_tok)).astype(jnp.bfloat16)
    upstream = cotangent.astype(jnp.float32) * live
    gate_grad = jnp.sum(upstream * expert_tok, axis=1, keepdims=True)
    logit_grad = (gate_grad * gate * (1.0 - gate)).astype(jnp.bfloat16)
    route_grad = (onehot * logit_grad.astype(jnp.float32)).astype(jnp.bfloat16)
    centroid_part = jnp.einsum("te,td->ed", route_grad, tokens, preferred_element_type=jnp.float32)
    gate_input = jnp.einsum("te,ed->td", route_grad, centroids, preferred_element_type=jnp.float32)
    expert_grad = (gate * upstream).astype(jnp.bfloat16)
    grad_rows = lax.all_to_all(pack(expert_grad), "expert", split_axis=0, concat_axis=0, tiled=True)
    gain_parts = [None] * layers
    shift_parts = [None] * layers
    down_bias_parts = [None] * layers
    up_weight_grads = [None] * layers
    up_bias_grads = [None] * layers
    down_weight_grads = [None] * layers
    for expert_layer_step in range(layers - 1, -1, -1):
        own_rows = inputs[expert_layer_step]
        grads_all = lax.all_gather(grad_rows, "batch", axis=0, tiled=True).reshape(
            -1, local_count, capacity, width
        )
        normed, pre_act, activity = kept[expert_layer_step]
        act_grad = jnp.einsum(
            "nlcd,lfd->nlcf",
            grads_all,
            down_weight[expert_layer_step],
            preferred_element_type=jnp.float32,
        )
        pre_grad = jax.vjp(gelu_exact, pre_act)[1](act_grad)[0].astype(jnp.bfloat16)
        down_weight_grads[expert_layer_step] = jnp.einsum(
            "nlcf,nlcd->lfd", activity, grads_all, preferred_element_type=jnp.float32
        )
        up_weight_grads[expert_layer_step] = jnp.einsum(
            "nlcd,nlcf->ldf", normed, pre_grad, preferred_element_type=jnp.float32
        )
        up_bias_grads[expert_layer_step] = jnp.sum(pre_grad.astype(jnp.float32), axis=(0, 2))

        def up_part(start, count, pre_grad=pre_grad, expert_layer_step=expert_layer_step):
            return jnp.einsum(
                "nlcf,ldf->nlcd",
                pre_grad,
                up_weight[expert_layer_step],
                preferred_element_type=jnp.float32,
            )

        normed_grad = lax.psum_scatter(
            up_part(jnp.int32(0), lax.axis_size("batch") * groups).astype(jnp.bfloat16),
            "batch",
            scatter_dimension=0,
            tiled=True,
        ).astype(jnp.float32)
        out_grad = grad_rows.reshape(groups, local_count, capacity, width).astype(jnp.float32)
        down_bias_parts[expert_layer_step] = jnp.sum(out_grad, axis=(0, 2))
        own_hat, own_scale = apply_layer_norm(
            own_rows.reshape(groups, local_count, capacity, width)
        )
        gain_parts[expert_layer_step] = jnp.sum(normed_grad * own_hat, axis=(0, 2))
        shift_parts[expert_layer_step] = jnp.sum(normed_grad, axis=(0, 2))
        hat_grad = normed_grad * expand_hidden(sublayer_norm_gain, expert_layer_step)
        row_grad = own_scale * (
            hat_grad
            - jnp.mean(hat_grad, axis=-1, keepdims=True)
            - own_hat * jnp.mean(hat_grad * own_hat, axis=-1, keepdims=True)
        )
        grad_rows = (out_grad + row_grad).astype(jnp.bfloat16).reshape(tok_rows, width)
    gain_grad, shift_grad, down_bias_grad = lax.psum(
        (jnp.stack(gain_parts), jnp.stack(shift_parts), jnp.stack(down_bias_parts)), "batch"
    )
    token_back = lax.all_to_all(grad_rows, "expert", split_axis=0, concat_axis=0, tiled=True)
    tokens_grad = (
        upstream + gate_input + live * token_back[safe_target].astype(jnp.float32)
    ).astype(jnp.bfloat16)
    centroid_grad = lax.psum(centroid_part, ("expert", "batch"))
    denominator = jnp.float32(capacity * groups * batches)
    gate_mass = gate_total / denominator
    load = count_total / denominator
    return (
        mixed,
        tokens_grad,
        centroid_grad,
        gain_grad,
        shift_grad,
        jnp.stack(up_weight_grads),
        jnp.stack(up_bias_grads),
        jnp.stack(down_weight_grads),
        down_bias_grad,
        gate_mass,
        load,
    )


MESH = pl.DeviceIdType.MESH
F32 = jnp.float32
BF16 = jnp.bfloat16
ROW_STEP = 64
COL_STEP = 256
EMPTY = 8.0
BLOCK_KINDS = ("x", "g", "ngrad0")
LINK_KINDS = BLOCK_KINDS + ("sum0", "out", "ngrad1")
CORE_KINDS = ("x", "g", "part0", "h", "part1", "ngrad1", "hgrad", "ngrad0")
SCHEDULE = (
    "SX.0 SG.0 SX.1 SX.2",
    "SX.3 SX.4 SX.5 SG.2",
    "SG.1 PX.0 U0.0 SX.6",
    "SG.3 D0.0 PX.1 S0.0",
    "U0.1 D0.1 PX.3 SX.7",
    "SG.5 S0.1 PX.2 H.0",
    "PG.3 U0.3 PG.0 SG.4",
    "U0.2 D0.2 SG.7 D0.3",
    "SG.6 PG.1 S0.2 U1.0",
    "PG.2 H.1 S0.3 U1.1",
    "B1.0 D1.1 H.2 S1.0",
    "B1.1 U1.2 S1.1 H.3",
    "SO.1 B1.2 U1.3 B1.3",
    "W1.2 S1.2 D1.0 HG.1",
    "HG.0 W1.0 SO.0 B0.1",
    "B0.0 MX.1 SQ.1 GS.1",
    "S1.3 HG.2 W1.3 B0.2",
    "D1.2 D1.3 SO.2 TG.5",
    "TG.4 MX.0 SQ.2 GS.2",
    "HG.3 SO.3 SQ.0 GS.0",
    "W1.1 MX.2 B0.3 TG.7",
    "TG.6 SQ.3 GS.3 R0.0",
    "MX.3 R1.0 R1.1 TG.3",
    "TG.2 TG.1 TG.0 R1.2",
    "UP.0 R0.1 R0.2 UP.1",
)
PART_SLOT = {"part0": 0, "part1": 0, "ngrad1": 1, "ngrad0": 1}
ROUTE_KINDS = ("x", "ct", "mixed", "tgrad", "totals")


def fused_fits(tokens, centroids, up_weight):
    tok_rows, width = tokens.shape
    groups, capacity = lax.axis_size("expert"), tok_rows // centroids.shape[0]
    return (
        lax.axis_size("batch") == 4
        and groups == 8
        and up_weight.shape[:2] == (2, 1)
        and centroids.shape[0] == groups
        and up_weight.shape[3] == width
        and width % (4 * COL_STEP) == 0
        and capacity % 32 == 0
    )


def rows_at(start, count, unit):
    return pl.ds(pl.multiple_of(start, unit), count)


def loop_rows(count, step, body):
    step = min(step, count)
    for start in range(0, count, step):
        body(start, step)


def loop_tiles(count, step, body):
    def one(i, carry):
        body(pl.multiple_of(i * step, step), step)
        return carry

    lax.fori_loop(0, count // step, one, 0)


def normalize(values):
    centered = values - jnp.mean(values, axis=-1, keepdims=True)
    scale = lax.rsqrt(jnp.mean(centered * centered, axis=-1, keepdims=True) + 1e-05)
    return centered * scale, scale


def dot(a, b, dims):
    return lax.dot_general(a, b, (dims, ((), ())), preferred_element_type=F32)


NN = ((1,), (0,))
NT = ((1,), (1,))
TN = ((0,), (0,))


def fused_kernel(
    groups,
    capacity,
    chunks,
    ids_ref,
    slots_ref,
    tok_ref,
    ct_ref,
    cent_ref,
    gain_ref,
    bias_ref,
    up_bias_ref,
    down_bias_ref,
    up_hbm,
    down_hbm,
    mixed_ref,
    tgrad_ref,
    totals_ref,
    small_ref,
    up_grad_ref,
    down_grad_ref,
    n_0,
    a_0,
    d_0,
    hg_0,
    up_w,
    down_w,
    perm,
    pack_x,
    pack_ct,
    xa,
    ga,
    ha,
    hga,
    n_1,
    a_1,
    d_1,
    part,
    part_in,
    half_out,
    half_in,
    own_out,
    own_in,
    ct_own,
    gate_s,
    lg_s,
    back_out,
    back_in,
    acc,
    acc_0,
    red,
    totals_in,
    w_sem,
    route_send,
    route_recv,
    link_send,
    link_recv,
    core_send,
    core_recv,
    red_send,
    red_recv,
):
    tok_rows, width = tok_ref.shape
    hidden = up_w.shape[2]
    n_s, a_s, d_s = (n_0, n_1), (a_0, a_1), (d_0, d_1)
    per = groups // chunks
    rows_m = per * 4 * capacity
    rows_h = rows_m // 2
    rows_o = rows_m // 4
    e = lax.axis_index("expert")
    b = lax.axis_index("batch")
    x = b // 2
    c = lax.rem(b, 2)
    sib = (e, x * 2 + (1 - c))
    far = (e, (1 - x) * 2 + c)

    def flipped(m):
        out = jnp.int32(0)
        bit = 1
        while bit < groups:
            digit = lax.rem(e // bit, 2)
            out = out + bit * ((1 - digit) if m & bit else digit)
            bit *= 2
        return out

    half = c * rows_h
    sib_half = (1 - c) * rows_h
    own = half + x * rows_o
    pairs = [tuple(range(j * per, (j + 1) * per)) for j in range(chunks)]
    order = pairs[1:] + pairs[:1]
    place = {m: (k, i) for k, ms in enumerate(order) for i, m in enumerate(ms)}
    others = range(1, groups)

    def at_half(k):
        return rows_at(k * rows_m + half, rows_h, rows_h)

    def at_own_block(m):
        k, i = place[m]
        return pl.ds(k * rows_o + i * capacity, capacity)

    def at_sib_half(k):
        return rows_at(k * rows_m + sib_half, rows_h, rows_h)

    def at_block(m):
        k, i = place[m]
        return rows_at(k * rows_m + own + i * capacity, capacity, capacity)

    def at_all(k):
        return pl.ds(k * rows_m, rows_m)

    def copy_to(device, src, dst, send, recv):
        return pltpu.make_async_remote_copy(
            src_ref=src,
            dst_ref=dst,
            send_sem=send,
            recv_sem=recv,
            device_id=device,
            device_id_type=MESH,
        )

    def route(kind, m):
        n = ROUTE_KINDS.index(kind)
        to = flipped(m)
        theirs = rows_at(to * capacity, capacity, capacity)
        mine = rows_at(e * capacity, capacity, capacity)
        if kind == "x":
            src = pack_x.at[theirs]
            dst = xa.at[at_block(m)]
        elif kind == "ct":
            src = pack_ct.at[theirs]
            dst = ct_own.at[at_own_block(m)]
        elif kind == "totals":
            src = dst = totals_in.at[e]
        else:
            s = 0 if kind == "mixed" else 1
            src = back_out.at[s, at_own_block(m)]
            dst = back_in.at[s, mine]
        return copy_to((to, b), src, dst, route_send.at[n, m], route_recv.at[n, m])

    def link(kind, k):
        n = LINK_KINDS.index(kind)
        if kind in ("x", "g"):
            src = dst = {"x": xa, "g": ga}[kind].at[at_block(k)]
        elif kind in ("sum0", "ngrad1"):
            s = 0 if kind == "sum0" else 1
            at = pl.ds(k * rows_h, rows_h)
            src, dst = half_out.at[s, at], half_in.at[s, at]
        elif kind == "out":
            at = pl.ds(k * rows_o, rows_o)
            src, dst = own_out.at[0, at], own_in.at[0, at]
        else:
            at = at_own_block(k)
            src, dst = own_out.at[1, at], own_in.at[1, at]
        return copy_to(far, src, dst, link_send.at[n, k], link_recv.at[n, k])

    def core(kind, k):
        n = CORE_KINDS.index(kind)
        whole = {"x": xa, "g": ga, "h": ha, "hgrad": hga}
        if kind in whole:
            src = dst = whole[kind].at[at_half(k)]
        else:
            s = PART_SLOT[kind]
            src = part.at[s, at_sib_half(k)]
            dst = part_in.at[s, pl.ds(k * rows_h, rows_h)]
        return copy_to(sib, src, dst, core_send.at[n, k], core_recv.at[n, k])

    barrier = pltpu.get_barrier_semaphore()
    peers = [sib, far] + [(flipped(m), b) for m in range(1, groups)]
    for peer in peers:
        pl.semaphore_signal(barrier, inc=1, device_id=peer, device_id_type=MESH)
    loads = []
    for j in range(2):
        loads.append(pltpu.make_async_copy(up_hbm.at[j, 0], up_w.at[j], w_sem.at[2 * j]))
        loads.append(pltpu.make_async_copy(down_hbm.at[j, 0], down_w.at[j], w_sem.at[2 * j + 1]))
    for load in loads:
        load.start()
    target = jnp.where(
        slots_ref[...] >= 0, ids_ref[...] * capacity + slots_ref[...], -1
    )
    slot = lax.broadcasted_iota(jnp.int32, (tok_rows, tok_rows), 0)
    onehot = jnp.where(slot == target, 1.0, 0.0)
    perm[...] = onehot.astype(BF16)
    empty = EMPTY * (1.0 - jnp.sum(onehot, axis=1, keepdims=True))

    def pack(start, step):
        cols = rows_at(start, step, step)
        pack_x[:, cols] = (dot(perm[...], tok_ref[:, cols], NN) + empty).astype(BF16)
        pack_ct[:, cols] = dot(perm[...], ct_ref[:, cols], NN).astype(BF16)

    loop_rows(width, COL_STEP, pack)
    acc[...] = jnp.zeros_like(acc)
    acc_0[...] = jnp.zeros_like(acc_0)
    red[...] = jnp.zeros_like(red)
    cent_rows = cent_ref[...].astype(F32)
    cent_at = lax.broadcasted_iota(jnp.int32, cent_rows.shape, 0)
    cent = jnp.sum(jnp.where(cent_at == e, cent_rows, 0.0), axis=0, keepdims=True)
    pl.semaphore_wait(barrier, len(peers))
    near = 2 * per
    for kind, masks in (
        ("x", range(1, near)),
        ("ct", range(1, per)),
        ("x", range(near, groups)),
        ("ct", range(per, groups)),
    ):
        for m in masks:
            route(kind, m).start()
    mine = rows_at(e * capacity, capacity, capacity)
    xa[at_block(0)] = pack_x[mine]
    ct_own[at_own_block(0)] = pack_ct[mine]

    def send_x(m):
        if m:
            route("x", m).wait_recv()
        link("x", m).start()

    def send_g(m):
        if m:
            route("ct", m).wait_recv()
        at_o = at_own_block(m)
        values = xa[at_block(m)].astype(F32)
        gate = jax.nn.sigmoid(jnp.sum(values * cent, axis=-1, keepdims=True))
        gate_s[at_o] = jnp.broadcast_to(gate, (capacity, 128))
        ga[at_block(m)] = (gate * ct_own[at_o].astype(F32)).astype(BF16)
        used = jnp.where(values[:, 0:1] < 7.0, 1.0, 0.0)
        acc[3:4] += jnp.broadcast_to(jnp.sum(used * gate, axis=0, keepdims=True), (1, width))
        acc[4:5] += jnp.broadcast_to(jnp.sum(used, axis=0, keepdims=True), (1, width))
        link("g", m).start()

    def spread(kind, k):
        for m in order[k]:
            link(kind, m).wait_recv()
        core(kind, k).start()

    def up_step(j, rows_ref, k):
        gain = gain_ref[j : j + 1].astype(F32)
        bias = bias_ref[j : j + 1].astype(F32)

        def norm(start, step):
            at = rows_at(k * rows_m + start, step, step)
            rhat, _ = normalize(rows_ref[at].astype(F32))
            n_s[j][at] = (rhat * gain + bias).astype(BF16)

        loop_tiles(rows_m, 2 * ROW_STEP, norm)

        def up(start, step):
            cols = rows_at(start, step, step)
            pre = dot(n_s[j][at_all(k)], up_w[j, :, cols], NN) + up_bias_ref[j : j + 1, cols].astype(
                F32
            )
            cdf = 0.5 * (1.0 + lax.erf(pre * (0.5**0.5)))
            pdf = jnp.exp(-0.5 * pre * pre) * 0.3989422804014327
            a_s[j][at_all(k), cols] = (pre * cdf).astype(BF16)
            d_s[j][at_all(k), cols] = (cdf + pre * pdf).astype(BF16)

        loop_rows(hidden, COL_STEP, up)

    def down_step(j, k):
        kind = "part%d" % j
        if j == 1:
            core("part0", k).wait_send()

        def down(start, step):
            cols = rows_at(start, step, step)
            part[0, at_all(k), cols] = dot(a_s[j][at_all(k)], down_w[j, :, cols], NN).astype(BF16)

        loop_tiles(width, 2 * COL_STEP, down)
        core(kind, k).start()

    def back_step(j, grads_ref, k):
        kind = "ngrad%d" % j
        if j == 0:
            core("ngrad1", k).wait_send()

        def act(start, step):
            cols = rows_at(start, step, step)
            grad = dot(grads_ref[at_all(k)], down_w[j, cols, :], NT)
            d_s[j][at_all(k), cols] = (grad * d_s[j][at_all(k), cols].astype(F32)).astype(BF16)

        loop_tiles(hidden, 2 * COL_STEP, act)

        def up_back(start, step):
            cols = rows_at(start, step, step)
            part[1, at_all(k), cols] = dot(d_s[j][at_all(k)], up_w[j, cols, :], NT).astype(BF16)

        loop_tiles(width, 2 * COL_STEP, up_back)
        core(kind, k).start()

    def sum_half(kind, link_kind, k):
        s = PART_SLOT[kind]
        o = ("sum0", "ngrad1").index(link_kind)
        core(kind, k).wait_recv()

        def add_half(start, step):
            at = rows_at(k * rows_m + half + start, step, step)
            at_h = rows_at(k * rows_h + start, step, step)
            total = part[s, at].astype(F32) + part_in[s, at_h].astype(F32)
            half_out[o, at_h] = total.astype(BF16)

        loop_rows(rows_h, ROW_STEP, add_half)
        link(link_kind, k).start()

    def sum_far(kind, link_kind, k):
        s = PART_SLOT[kind]
        o = ("out", "ngrad0").index(link_kind)
        core(kind, k).wait_recv()

        def add_far(start, step):
            at = rows_at(k * rows_m + half + (1 - x) * rows_o + start, step, step)
            at_h = rows_at(k * rows_h + (1 - x) * rows_o + start, step, step)
            at_o = rows_at(k * rows_o + start, step, step)
            total = part[s, at].astype(F32) + part_in[s, at_h].astype(F32)
            own_out[o, at_o] = total.astype(BF16)

        loop_rows(rows_o, ROW_STEP, add_far)
        if link_kind in BLOCK_KINDS:
            for m in reversed(order[k]):
                link(link_kind, m).start()
        else:
            link(link_kind, k).start()

    def sum_own(s, o, k, start, step):
        at = rows_at(k * rows_m + own + start, step, step)
        at_h = rows_at(k * rows_h + x * rows_o + start, step, step)
        at_o = rows_at(k * rows_o + start, step, step)
        mine = part[s, at].astype(F32) + part_in[s, at_h].astype(F32)
        return mine + own_in[o, at_o].astype(F32)

    def make_h(k):
        link("sum0", k).wait_recv()
        shift = down_bias_ref[0:1].astype(F32)

        def add_h(start, step):
            at = rows_at(k * rows_m + half + start, step, step)
            at_h = rows_at(k * rows_h + start, step, step)
            total = half_out[0, at_h].astype(F32) + half_in[0, at_h].astype(F32)
            ha[at] = (xa[at].astype(F32) + total + shift).astype(BF16)

        loop_rows(rows_h, ROW_STEP, add_h)
        core("h", k).start()

    def norm_back(rows, ngrad, gain):
        rhat, scale = normalize(rows)
        q = ngrad * gain
        back = scale * (
            q - jnp.mean(q, axis=-1, keepdims=True) - rhat * jnp.mean(q * rhat, axis=-1, keepdims=True)
        )
        return back, rhat

    def make_hgrad(k):
        link("ngrad1", k).wait_recv()
        gain = gain_ref[1:2].astype(F32)

        def grad_h(start, step):
            at = rows_at(k * rows_m + half + start, step, step)
            at_h = rows_at(k * rows_h + start, step, step)
            ngrad = half_out[1, at_h].astype(F32) + half_in[1, at_h].astype(F32)
            back, rhat = norm_back(ha[at].astype(F32), ngrad, gain)
            hga[at] = (ga[at].astype(F32) + back).astype(BF16)
            acc[0:1] += 0.5 * jnp.sum(ngrad * rhat, axis=0, keepdims=True)
            acc[1:2] += 0.5 * jnp.sum(ngrad, axis=0, keepdims=True)

        loop_tiles(rows_h, ROW_STEP, grad_h)
        core("hgrad", k).start()

    def give_back(kind, m):
        if m:
            route(kind, m).start()
        else:
            s = 0 if kind == "mixed" else 1
            back_in[s, mine] = back_out[s, at_own_block(0)]

    def make_mixed(k):
        link("out", k).wait_recv()
        shift = down_bias_ref[1:2].astype(F32)

        def mix(start, step):
            at = rows_at(k * rows_m + own + start, step, step)
            at_o = rows_at(k * rows_o + start, step, step)
            out = (ha[at].astype(F32) + sum_own(0, 0, k, start, step) + shift).astype(BF16).astype(F32)
            rows = xa[at].astype(F32)
            gate = gate_s[at_o][:, 0:1]
            back_out[0, at_o] = (rows + gate * out).astype(BF16)
            along = jnp.sum(ct_own[at_o].astype(F32) * out, axis=-1, keepdims=True)
            lgrad = (along * gate * (1.0 - gate)).astype(BF16).astype(F32)
            lg_s[at_o] = jnp.broadcast_to(lgrad, (step, 128))
            acc[2:3] += jnp.sum(lgrad * rows, axis=0, keepdims=True)

        loop_rows(rows_o, ROW_STEP, mix)
        for m in reversed(order[k]):
            give_back("mixed", m)

    def norm_sums(k):
        def sum_rows(start, step):
            at = rows_at(k * rows_m + half + start, step, step)
            at_h = rows_at(k * rows_h + start, step, step)
            ngrad = part[1, at].astype(F32) + part_in[1, at_h].astype(F32)
            rhat, _ = normalize(xa[at].astype(F32))
            acc_0[0:1] += jnp.sum(ngrad * rhat, axis=0, keepdims=True)
            acc_0[1:2] += jnp.sum(ngrad, axis=0, keepdims=True)

        loop_tiles(rows_h, ROW_STEP, sum_rows)

    def make_tgrad(m):
        link("ngrad0", m).wait_recv()
        k, i = place[m]
        at_o = at_own_block(m)
        at = at_block(m)
        ngrad = sum_own(1, 1, k, i * capacity, capacity)
        back, _ = norm_back(xa[at].astype(F32), ngrad, gain_ref[0:1].astype(F32))
        back = (hga[at].astype(F32) + back).astype(BF16).astype(F32)
        back_out[1, at_o] = (
            ct_own[at_o].astype(F32) + lg_s[at_o][:, 0:1] * cent + back
        ).astype(BF16)
        give_back("tgrad", m)

    def column_sums(rows_ref):
        def one(i, total):
            values = rows_ref[rows_at(i * ROW_STEP, ROW_STEP, ROW_STEP)].astype(F32)
            return total + jnp.sum(values, axis=0, keepdims=True)

        return lax.fori_loop(
            0, rows_ref.shape[0] // ROW_STEP, one, jnp.zeros((1, rows_ref.shape[1]), F32)
        )

    def weight_grad(q):
        into, left, right = ((down_grad_ref, a_1, ga), (up_grad_ref, n_1, d_1))[q // 2]
        if q == 0:
            small_ref[4:5] = column_sums(right)
        if q == 2:
            small_ref[5:6] = column_sums(right)
        count = left.shape[1] // 2

        def tile(start, step):
            at = rows_at(q % 2 * count + start, step, step)
            into[at] = dot(left[:, at], right[...], TN).astype(BF16)

        loop_tiles(count, COL_STEP, tile)

    lanes = width // 128
    red_rows = (3 * lanes + 8, 2 * lanes)

    def over(s):
        at = pl.ds(0, red_rows[s])
        return copy_to(
            sib, red.at[s, 0, at], red.at[s, 1, at], red_send.at[s, 0], red_recv.at[s, 0]
        )

    def across(s):
        at = pl.ds(0, red_rows[s])
        return copy_to(
            far, red.at[s, 0, at], red.at[s, 2, at], red_send.at[s, 1], red_recv.at[s, 1]
        )

    def total(s, step):
        rows_ref = (acc, acc_0)[s]
        if step == 0:
            for r in range(3 - s):
                for i in range(lanes):
                    red[s, 0, r * lanes + i : r * lanes + i + 1] = rows_ref[
                        r : r + 1, i * 128 : (i + 1) * 128
                    ]
            if s == 0:
                red[s, 0, 3 * lanes : 3 * lanes + 2] = rows_ref[3:5, 0:128]
            over(s).start()
        elif step == 1:
            over(s).wait()
            red[s, 0] = red[s, 0] + red[s, 1]
            across(s).start()
        else:
            across(s).wait()
            sums = red[s, 0] + red[s, 2]
            for r in range(2):
                for i in range(lanes):
                    small_ref[2 * r + 1 - s : 2 * r + 2 - s, i * 128 : (i + 1) * 128] = sums[
                        r * lanes + i : r * lanes + i + 1
                    ]
            if s == 0:
                totals_in[e, 0 : lanes + 2] = sums[2 * lanes : 3 * lanes + 2]
                for m in others:
                    route("totals", m).start()

    def unpack(s):
        kind, out_ref = (("mixed", mixed_ref), ("tgrad", tgrad_ref))[s]
        for m in others:
            route(kind, m).wait_recv()

        def place_tokens(start, step):
            cols = rows_at(start, step, step)
            out_ref[:, cols] = dot(perm[...], back_in[s, :, cols], TN).astype(BF16)

        loop_rows(width, COL_STEP, place_tokens)

    steps = range(chunks)

    def up_0(k):
        if k == first_use[0]:
            loads[0].wait()
        core("x", k).wait_recv()
        up_step(0, xa, k)

    def down_0(k):
        if k == first_use[2]:
            loads[1].wait()
        down_step(0, k)

    def up_1(k):
        if k == first_use[1]:
            loads[2].wait()
            loads[3].wait()
        core("h", k).wait_recv()
        up_step(1, ha, k)

    def back_1(k):
        core("g", k).wait_recv()
        back_step(1, ga, k)

    def back_0(k):
        core("hgrad", k).wait_recv()
        hg_0[at_all(k)] = hga[at_all(k)]
        back_step(0, hga, k)

    tasks = {
        "SX": send_x,
        "SG": send_g,
        "PX": functools.partial(spread, "x"),
        "PG": functools.partial(spread, "g"),
        "U0": up_0,
        "D0": down_0,
        "S0": functools.partial(sum_half, "part0", "sum0"),
        "H": make_h,
        "U1": up_1,
        "B1": back_1,
        "D1": functools.partial(down_step, 1),
        "S1": functools.partial(sum_half, "ngrad1", "ngrad1"),
        "SO": functools.partial(sum_far, "part1", "out"),
        "HG": make_hgrad,
        "MX": make_mixed,
        "B0": back_0,
        "SQ": functools.partial(sum_far, "ngrad0", "ngrad0"),
        "GS": norm_sums,
        "TG": make_tgrad,
        "W1": weight_grad,
        "R1": functools.partial(total, 0),
        "R0": functools.partial(total, 1),
        "UP": unpack,
    }
    plan = [word.split(".") for line in SCHEDULE for word in line.split()]
    first_use = [next(int(k) for name, k in plan if name == u) for u in ("U0", "U1", "D0")]
    for name, k in plan:
        tasks[name](int(k))

    for m in others:
        route("totals", m).wait_recv()
    totals_ref[...] = totals_in[...]
    for m in others:
        for kind in ROUTE_KINDS:
            route(kind, m).wait_send()
    for m in range(groups):
        for kind in BLOCK_KINDS:
            link(kind, m).wait_send()
    for k in steps:
        for kind in LINK_KINDS[len(BLOCK_KINDS) :]:
            link(kind, k).wait_send()
        for kind in CORE_KINDS:
            if kind not in ("part0", "ngrad1"):
                core(kind, k).wait_send()


def widen_kernel(
    denominator,
    mixed_ref,
    tgrad_ref,
    totals_ref,
    small_ref,
    up_ref,
    down_ref,
    n_0,
    a_0,
    d_0,
    hg_0,
    mixed_out,
    tgrad_out,
    cent_out,
    gain_out,
    shift_out,
    up_out,
    ub_out,
    down_out,
    db_out,
    mass_out,
    load_out,
    cent_s,
    rows_s,
    up_wide,
    down_wide,
    sem,
    up_sem,
    down_sem,
):
    leaving = []

    def leave(src, dst, semaphore):
        move = pltpu.make_async_copy(src, dst, semaphore)
        move.start()
        leaving.append(move)

    def widen(ref, wide, dst, semaphore, t):
        at = pl.ds(t * COL_STEP, COL_STEP)
        wide[1, at] = ref[at].astype(F32)
        leave(wide.at[1, at], dst.at[1, 0, at], semaphore.at[1, t])

    def multiply(left, right, wide, dst, semaphore, t):
        at = pl.ds(t * COL_STEP, COL_STEP)
        wide[0, at] = dot(left[:, at], right[...], TN)
        leave(wide.at[0, at], dst.at[0, 0, at], semaphore.at[0, t])

    leave(mixed_ref, mixed_out, sem.at[0])
    leave(tgrad_ref, tgrad_out, sem.at[1])
    for t in range(down_wide.shape[1] // COL_STEP):
        widen(down_ref, down_wide, down_out, down_sem, t)
        multiply(a_0, hg_0, down_wide, down_out, down_sem, t)
    for t in range(up_wide.shape[1] // COL_STEP):
        widen(up_ref, up_wide, up_out, up_sem, t)
        multiply(n_0, d_0, up_wide, up_out, up_sem, t)

    def column_sums(ref):
        return jnp.sum(ref[...].astype(F32), axis=0, keepdims=True)

    for i in range(cent_s.shape[1] // 128):
        cent_s[:, i * 128 : (i + 1) * 128] = totals_ref[:, i]
    leave(cent_s, cent_out, sem.at[2])
    for j in range(2):
        rows_s[0, j] = small_ref[j : j + 1]
        rows_s[1, j] = small_ref[2 + j : 3 + j]
    rows_s[2, 0] = column_sums(d_0)
    rows_s[2, 1] = small_ref[5:6]
    rows_s[3, 0] = column_sums(hg_0)
    rows_s[3, 1] = small_ref[4:5]
    for n, dst in enumerate((gain_out, shift_out, ub_out, db_out)):
        leave(rows_s.at[n], dst, sem.at[3 + n])
    experts = totals_ref.shape[0]
    diagonal = lax.broadcasted_iota(jnp.int32, (experts, 128), 0) == lax.broadcasted_iota(
        jnp.int32, (experts, 128), 1
    )
    for out, n in ((mass_out, 8), (load_out, 9)):
        values = jnp.sum(jnp.where(diagonal, totals_ref[:, n], 0.0), axis=0)
        out[...] = values[0:experts] / jnp.float32(denominator)
    for move in leaving:
        move.wait()


def per_device_fused(
    tokens,
    lengths,
    expert_ids,
    slots,
    centroids,
    sublayer_norm_gain,
    sublayer_norm_bias,
    up_weight,
    up_bias,
    down_weight,
    down_bias,
    cotangent,
):
    if not fused_fits(tokens, centroids, up_weight):
        return per_device(
            tokens,
            lengths,
            expert_ids,
            slots,
            centroids,
            sublayer_norm_gain,
            sublayer_norm_bias,
            up_weight,
            up_bias,
            down_weight,
            down_bias,
            cotangent,
        )
    tok_rows, width = tokens.shape
    groups = lax.axis_size("expert")
    batches = lax.axis_size("batch")
    experts = centroids.shape[0]
    capacity = tok_rows // experts
    hidden = up_weight.shape[3]
    chunks = 4
    total = groups * batches * capacity
    def flat(values):
        return values.reshape(values.shape[0], -1)

    vmem = pl.BlockSpec(memory_space=pltpu.VMEM)
    hbm = pl.BlockSpec(memory_space=pl.ANY)
    outs = pl.pallas_call(
        functools.partial(fused_kernel, groups, capacity, chunks),
        out_shape=[
            pltpu.VMEM((tok_rows, width), BF16),
            pltpu.VMEM((tok_rows, width), BF16),
            pltpu.VMEM((groups, 16, 128), F32),
            pltpu.VMEM((8, width), F32),
            pltpu.VMEM(up_weight.shape[2:], BF16),
            pltpu.VMEM(down_weight.shape[2:], BF16),
            pltpu.VMEM((total, width), BF16),
            pltpu.VMEM((total, hidden), BF16),
            pltpu.VMEM((total, hidden), BF16),
            pltpu.VMEM((total, width), BF16),
        ],
        in_specs=[vmem] * 9 + [hbm] * 2,
        out_specs=[vmem] * 10,
        scratch_shapes=[
            pltpu.VMEM((2, width, hidden), BF16),
            pltpu.VMEM((2, hidden, width), BF16),
            pltpu.VMEM((tok_rows, tok_rows), BF16),
            pltpu.VMEM((tok_rows, width), BF16),
            pltpu.VMEM((tok_rows, width), BF16),
            pltpu.VMEM((total, width), BF16),
            pltpu.VMEM((total, width), BF16),
            pltpu.VMEM((total, width), BF16),
            pltpu.VMEM((total, width), BF16),
            pltpu.VMEM((total, width), BF16),
            pltpu.VMEM((total, hidden), BF16),
            pltpu.VMEM((total, hidden), BF16),
            pltpu.VMEM((2, total, width), BF16),
            pltpu.VMEM((2, total // 2, width), BF16),
            pltpu.VMEM((2, total // 2, width), BF16),
            pltpu.VMEM((2, total // 2, width), BF16),
            pltpu.VMEM((2, total // 4, width), BF16),
            pltpu.VMEM((2, total // 4, width), BF16),
            pltpu.VMEM((tok_rows, width), BF16),
            pltpu.VMEM((tok_rows, 128), F32),
            pltpu.VMEM((tok_rows, 128), F32),
            pltpu.VMEM((2, tok_rows, width), BF16),
            pltpu.VMEM((2, tok_rows, width), BF16),
            pltpu.VMEM((8, width), F32),
            pltpu.VMEM((8, width), F32),
            pltpu.VMEM((2, 3, 3 * width // 128 + 8, 128), F32),
            pltpu.VMEM((groups, 16, 128), F32),
            pltpu.SemaphoreType.DMA((4,)),
            pltpu.SemaphoreType.DMA((len(ROUTE_KINDS), groups)),
            pltpu.SemaphoreType.DMA((len(ROUTE_KINDS), groups)),
            pltpu.SemaphoreType.DMA((len(LINK_KINDS), groups)),
            pltpu.SemaphoreType.DMA((len(LINK_KINDS), groups)),
            pltpu.SemaphoreType.DMA((len(CORE_KINDS), chunks)),
            pltpu.SemaphoreType.DMA((len(CORE_KINDS), chunks)),
            pltpu.SemaphoreType.DMA((2, 2)),
            pltpu.SemaphoreType.DMA((2, 2)),
        ],
        compiler_params=pltpu.CompilerParams(
            collective_id=0, has_side_effects=True, vmem_limit_bytes=46 << 20
        ),
        cost_estimate=pl.CostEstimate(
            flops=24 * total * width * hidden, bytes_accessed=40 << 20, transcendentals=0
        ),
    )(
        expert_ids.reshape(1, tok_rows),
        slots.reshape(1, tok_rows),
        tokens,
        cotangent,
        centroids,
        flat(sublayer_norm_gain),
        flat(sublayer_norm_bias),
        flat(up_bias),
        flat(down_bias),
        up_weight,
        down_weight,
    )
    layers = up_weight.shape[0]
    row = jax.ShapeDtypeStruct((layers, 1, width), F32)
    return pl.pallas_call(
        functools.partial(widen_kernel, capacity * groups * batches),
        out_shape=[
            jax.ShapeDtypeStruct(tokens.shape, BF16),
            jax.ShapeDtypeStruct(tokens.shape, BF16),
            jax.ShapeDtypeStruct((experts, width), F32),
            row,
            row,
            jax.ShapeDtypeStruct(up_weight.shape, F32),
            jax.ShapeDtypeStruct((layers, 1, hidden), F32),
            jax.ShapeDtypeStruct(down_weight.shape, F32),
            row,
            jax.ShapeDtypeStruct((experts,), F32),
            jax.ShapeDtypeStruct((experts,), F32),
        ],
        in_specs=[vmem] * 10,
        out_specs=[hbm] * 9 + [vmem] * 2,
        scratch_shapes=[
            pltpu.VMEM((experts, width), F32),
            pltpu.VMEM((4, layers, 1, width), F32),
            pltpu.VMEM((layers, width, hidden), F32),
            pltpu.VMEM((layers, hidden, width), F32),
            pltpu.SemaphoreType.DMA((7,)),
            pltpu.SemaphoreType.DMA((layers, width // COL_STEP)),
            pltpu.SemaphoreType.DMA((layers, hidden // COL_STEP)),
        ],
        compiler_params=pltpu.CompilerParams(vmem_limit_bytes=24 << 20),
        cost_estimate=pl.CostEstimate(
            flops=0, bytes_accessed=12 * layers * width * hidden, transcendentals=0
        ),
    )(*(pltpu.with_memory_space_constraint(out, pltpu.VMEM) for out in outs))


def solution(mesh):
    in_specs = (
        P(("expert", "batch"), None),
        P(("expert", "batch")),
        P(("expert", "batch")),
        P(("expert", "batch")),
        P(),
        P(None, "expert", None),
        P(None, "expert", None),
        P(None, "expert", None, "batch"),
        P(None, "expert", "batch"),
        P(None, "expert", "batch", None),
        P(None, "expert", None),
        P(("expert", "batch"), None),
    )
    out_specs = (
        P(("expert", "batch"), None),
        P(("expert", "batch"), None),
        P(),
        P(None, "expert", None),
        P(None, "expert", None),
        P(None, "expert", None, "batch"),
        P(None, "expert", "batch"),
        P(None, "expert", "batch", None),
        P(None, "expert", None),
        P(),
        P(),
    )
    return jax.shard_map(
        per_device_fused, mesh=mesh, in_specs=in_specs, out_specs=out_specs, check_vma=False
    )
```

```python
import functools

import jax
import jax.numpy as jnp
from jax import lax
from jax.experimental import pallas as pl
from jax.experimental.pallas import tpu as pltpu
from jax.sharding import PartitionSpec as P


def gelu_exact(values):
    return jax.nn.gelu(values, approximate=False)


def apply_layer_norm(row_block):
    values = row_block.astype(jnp.float32)
    row_mean = jnp.mean(values, axis=-1, keepdims=True)
    centered = values - row_mean
    row_inverse_scale = lax.rsqrt(jnp.mean(centered * centered, axis=-1, keepdims=True) + 1e-05)
    return (centered * row_inverse_scale, row_inverse_scale)


def per_device(
    tokens,
    lengths,
    expert_ids,
    slots,
    centroids,
    sublayer_norm_gain,
    sublayer_norm_bias,
    up_weight,
    up_bias,
    down_weight,
    down_bias,
    cotangent,
):
    tok_rows, width = tokens.shape
    layers = sublayer_norm_gain.shape[0]
    local_count = up_weight.shape[1]
    expert_count = centroids.shape[0]
    capacity = tok_rows // expert_count
    groups = lax.axis_size("expert")
    batches = lax.axis_size("batch")
    position = jnp.arange(tok_rows, dtype=jnp.int32)
    live = (position < lengths[0]).astype(jnp.float32)[:, None]
    target = jnp.where(slots >= 0, expert_ids * capacity + slots, tok_rows)
    source = jnp.full((tok_rows + 1,), -1, jnp.int32).at[target].set(position)[:tok_rows]
    filled = (source >= 0)[:, None]
    safe_source = jnp.maximum(source, 0)
    safe_target = jnp.minimum(target, tok_rows - 1)

    def pack(values):
        return jnp.where(filled, values[safe_source], jnp.zeros((), values.dtype))

    onehot = (expert_ids[:, None] == jnp.arange(expert_count, dtype=jnp.int32)[None, :]).astype(
        jnp.float32
    )
    logits = jnp.einsum("td,ed->te", tokens, centroids, preferred_element_type=jnp.float32)
    gate = jax.nn.sigmoid(jnp.sum(logits * onehot, axis=1))[:, None]
    used = onehot * live
    usage_gate = jnp.sum(used * gate, axis=0)
    usage_count = jnp.sum(used, axis=0)
    gate_total, count_total = lax.psum((usage_gate, usage_count), ("expert", "batch"))

    def expand_hidden(values, expert_layer_step):
        return values[expert_layer_step].astype(jnp.float32)[None, :, None, :]

    arrived = lax.all_to_all(pack(tokens), "expert", split_axis=0, concat_axis=0, tiled=True)
    current = arrived
    inputs = []
    kept = []
    for expert_layer_step in range(layers):
        gathered = lax.all_gather(current, "batch", axis=0, tiled=True)
        row_layout_grid = gathered.reshape(-1, local_count, capacity, width)
        standardized_input, row_inverse_scale = apply_layer_norm(row_layout_grid)
        normalized_rows = (
            standardized_input * expand_hidden(sublayer_norm_gain, expert_layer_step)
            + expand_hidden(sublayer_norm_bias, expert_layer_step)
        ).astype(jnp.bfloat16)
        pre_rows = jnp.einsum(
            "nlcd,ldf->nlcf",
            normalized_rows,
            up_weight[expert_layer_step],
            preferred_element_type=jnp.float32,
        ) + expand_hidden(up_bias, expert_layer_step)
        hidden_parts = (normalized_rows, pre_rows, gelu_exact(pre_rows).astype(jnp.bfloat16))

        def down_part(start, count, activity=hidden_parts[2], expert_layer_step=expert_layer_step):
            return jnp.einsum(
                "nlcf,lfd->nlcd",
                activity,
                down_weight[expert_layer_step],
                preferred_element_type=jnp.float32,
            )

        mixed_part = lax.psum_scatter(
            down_part(jnp.int32(0), lax.axis_size("batch") * groups).astype(jnp.bfloat16),
            "batch",
            scatter_dimension=0,
            tiled=True,
        ).astype(jnp.float32)
        own_grid = current.reshape(groups, local_count, capacity, width).astype(jnp.float32)
        result = (own_grid + mixed_part + expand_hidden(down_bias, expert_layer_step)).astype(
            jnp.bfloat16
        )
        inputs.append(current)
        kept.append(hidden_parts)
        current = result.reshape(tok_rows, width)
    returned = lax.all_to_all(current, "expert", split_axis=0, concat_axis=0, tiled=True)
    expert_tok = returned[safe_target].astype(jnp.float32)
    mixed = (live * (tokens.astype(jnp.float32) + gate * expert_tok)).astype(jnp.bfloat16)
    upstream = cotangent.astype(jnp.float32) * live
    gate_grad = jnp.sum(upstream * expert_tok, axis=1, keepdims=True)
    logit_grad = (gate_grad * gate * (1.0 - gate)).astype(jnp.bfloat16)
    route_grad = (onehot * logit_grad.astype(jnp.float32)).astype(jnp.bfloat16)
    centroid_part = jnp.einsum("te,td->ed", route_grad, tokens, preferred_element_type=jnp.float32)
    gate_input = jnp.einsum("te,ed->td", route_grad, centroids, preferred_element_type=jnp.float32)
    expert_grad = (gate * upstream).astype(jnp.bfloat16)
    grad_rows = lax.all_to_all(pack(expert_grad), "expert", split_axis=0, concat_axis=0, tiled=True)
    gain_parts = [None] * layers
    shift_parts = [None] * layers
    down_bias_parts = [None] * layers
    up_weight_grads = [None] * layers
    up_bias_grads = [None] * layers
    down_weight_grads = [None] * layers
    for expert_layer_step in range(layers - 1, -1, -1):
        own_rows = inputs[expert_layer_step]
        grads_all = lax.all_gather(grad_rows, "batch", axis=0, tiled=True).reshape(
            -1, local_count, capacity, width
        )
        normed, pre_act, activity = kept[expert_layer_step]
        act_grad = jnp.einsum(
            "nlcd,lfd->nlcf",
            grads_all,
            down_weight[expert_layer_step],
            preferred_element_type=jnp.float32,
        )
        pre_grad = jax.vjp(gelu_exact, pre_act)[1](act_grad)[0].astype(jnp.bfloat16)
        down_weight_grads[expert_layer_step] = jnp.einsum(
            "nlcf,nlcd->lfd", activity, grads_all, preferred_element_type=jnp.float32
        )
        up_weight_grads[expert_layer_step] = jnp.einsum(
            "nlcd,nlcf->ldf", normed, pre_grad, preferred_element_type=jnp.float32
        )
        up_bias_grads[expert_layer_step] = jnp.sum(pre_grad.astype(jnp.float32), axis=(0, 2))

        def up_part(start, count, pre_grad=pre_grad, expert_layer_step=expert_layer_step):
            return jnp.einsum(
                "nlcf,ldf->nlcd",
                pre_grad,
                up_weight[expert_layer_step],
                preferred_element_type=jnp.float32,
            )

        normed_grad = lax.psum_scatter(
            up_part(jnp.int32(0), lax.axis_size("batch") * groups).astype(jnp.bfloat16),
            "batch",
            scatter_dimension=0,
            tiled=True,
        ).astype(jnp.float32)
        out_grad = grad_rows.reshape(groups, local_count, capacity, width).astype(jnp.float32)
        down_bias_parts[expert_layer_step] = jnp.sum(out_grad, axis=(0, 2))
        own_hat, own_scale = apply_layer_norm(
            own_rows.reshape(groups, local_count, capacity, width)
        )
        gain_parts[expert_layer_step] = jnp.sum(normed_grad * own_hat, axis=(0, 2))
        shift_parts[expert_layer_step] = jnp.sum(normed_grad, axis=(0, 2))
        hat_grad = normed_grad * expand_hidden(sublayer_norm_gain, expert_layer_step)
        row_grad = own_scale * (
            hat_grad
            - jnp.mean(hat_grad, axis=-1, keepdims=True)
            - own_hat * jnp.mean(hat_grad * own_hat, axis=-1, keepdims=True)
        )
        grad_rows = (out_grad + row_grad).astype(jnp.bfloat16).reshape(tok_rows, width)
    gain_grad, shift_grad, down_bias_grad = lax.psum(
        (jnp.stack(gain_parts), jnp.stack(shift_parts), jnp.stack(down_bias_parts)), "batch"
    )
    token_back = lax.all_to_all(grad_rows, "expert", split_axis=0, concat_axis=0, tiled=True)
    tokens_grad = (
        upstream + gate_input + live * token_back[safe_target].astype(jnp.float32)
    ).astype(jnp.bfloat16)
    centroid_grad = lax.psum(centroid_part, ("expert", "batch"))
    denominator = jnp.float32(capacity * groups * batches)
    gate_mass = gate_total / denominator
    load = count_total / denominator
    return (
        mixed,
        tokens_grad,
        centroid_grad,
        gain_grad,
        shift_grad,
        jnp.stack(up_weight_grads),
        jnp.stack(up_bias_grads),
        jnp.stack(down_weight_grads),
        down_bias_grad,
        gate_mass,
        load,
    )


MESH = pl.DeviceIdType.MESH
F32 = jnp.float32
BF16 = jnp.bfloat16
ROW_STEP = 64
COL_STEP = 256
EMPTY = 8.0
BLOCK_KINDS = ("x", "g", "ngrad0")
LINK_KINDS = BLOCK_KINDS + ("sum0", "out", "ngrad1")
CORE_KINDS = ("x", "g", "part0", "h", "part1", "ngrad1", "hgrad", "ngrad0")
SCHEDULE = (
    "RX.1 RX.2 RX.3 RC.1",
    "RX.4 RX.5 RX.6 RX.7",
    "RC.2 RC.3 RC.4 RC.5",
    "RC.6 RC.7 SX.0 SG.0",
    "SX.1 SX.2 SX.3 SX.4",
    "SX.5 PX.3 PX.0 SG.2",
    "SX.6 SG.1 U0.0 PX.1",
    "D0.0 SX.7 SG.3 U0.1",
    "S0.0 U0.3 D0.1 PX.2",
    "S0.1 U0.2 SG.5 SG.4",
    "H.0 D0.2 D0.3 SG.7",
    "S0.3 H.1 S0.2 U1.1",
    "SG.6 PG.0 D1.1 U1.0",
    "SO.1 PG.1 H.3 B1.1",
    "D1.0 B1.0 H.2 S1.1",
    "U1.2 S1.0 PG.3 PG.2",
    "U1.3 D1.2 B1.2 HG.1",
    "S1.2 B1.3 MX.1 B0.1",
    "W1.3 SO.2 HG.0 SQ.1",
    "B0.0 S1.3 HG.2 D1.3",
    "SO.0 GS.1 TG.5 B0.2",
    "SO.3 TG.4 W1.0 MX.2",
    "SQ.2 GS.2 HG.3 W1.2",
    "SQ.0 B0.3 MX.0 MX.3",
    "R1.0 TG.7 GS.0 TG.6",
    "R1.1 SQ.3 GS.3 R0.0",
    "TG.3 R0.1 R1.2 TG.2",
    "TG.1 R0.2 TG.0 W1.1",
    "UP.0 UP.1",
)
PART_SLOT = {"part0": 0, "part1": 0, "ngrad1": 1, "ngrad0": 1}
ROUTE_KINDS = ("x", "ct", "mixed", "tgrad", "totals")


def fused_fits(tokens, centroids, up_weight):
    tok_rows, width = tokens.shape
    groups, capacity = lax.axis_size("expert"), tok_rows // centroids.shape[0]
    return (
        lax.axis_size("batch") == 4
        and groups == 8
        and up_weight.shape[:2] == (2, 1)
        and centroids.shape[0] == groups
        and up_weight.shape[3] == width
        and width % (4 * COL_STEP) == 0
        and capacity % 32 == 0
    )


def rows_at(start, count, unit):
    return pl.ds(pl.multiple_of(start, unit), count)


def loop_rows(count, step, body):
    step = min(step, count)
    for start in range(0, count, step):
        body(start, step)


def loop_tiles(count, step, body):
    def one(i, carry):
        body(pl.multiple_of(i * step, step), step)
        return carry

    lax.fori_loop(0, count // step, one, 0)


def normalize(values):
    centered = values - jnp.mean(values, axis=-1, keepdims=True)
    scale = lax.rsqrt(jnp.mean(centered * centered, axis=-1, keepdims=True) + 1e-05)
    return centered * scale, scale


def dot(a, b, dims):
    return lax.dot_general(a, b, (dims, ((), ())), preferred_element_type=F32)


NN = ((1,), (0,))
NT = ((1,), (1,))
TN = ((0,), (0,))


def fused_kernel(
    groups,
    capacity,
    chunks,
    ids_hbm,
    slots_hbm,
    tok_hbm,
    ct_hbm,
    cent_hbm,
    gain_hbm,
    bias_hbm,
    up_bias_hbm,
    down_bias_hbm,
    up_hbm,
    down_hbm,
    mixed_ref,
    tgrad_ref,
    totals_ref,
    small_ref,
    up_grad_ref,
    down_grad_ref,
    n_0,
    a_0,
    d_0,
    hg_0,
    ids_ref,
    slots_ref,
    tok_ref,
    ct_ref,
    cent_ref,
    gain_ref,
    bias_ref,
    up_bias_ref,
    down_bias_ref,
    up_w,
    down_w,
    perm,
    pack_x,
    pack_ct,
    xa,
    ga,
    ha,
    hga,
    n_1,
    a_1,
    d_1,
    part,
    part_in,
    half_out,
    half_in,
    own_out,
    own_in,
    ct_own,
    gate_s,
    lg_s,
    back_out,
    back_in,
    acc,
    acc_0,
    red,
    totals_in,
    in_sem,
    w_sem,
    route_send,
    route_recv,
    link_send,
    link_recv,
    core_send,
    core_recv,
    red_send,
    red_recv,
):
    tok_rows, width = tok_ref.shape
    hidden = up_w.shape[2]
    n_s, a_s, d_s = (n_0, n_1), (a_0, a_1), (d_0, d_1)
    per = groups // chunks
    rows_m = per * 4 * capacity
    rows_h = rows_m // 2
    rows_o = rows_m // 4
    e = lax.axis_index("expert")
    b = lax.axis_index("batch")
    x = b // 2
    c = lax.rem(b, 2)
    sib = (e, x * 2 + (1 - c))
    far = (e, (1 - x) * 2 + c)

    def flipped(m):
        out = jnp.int32(0)
        bit = 1
        while bit < groups:
            digit = lax.rem(e // bit, 2)
            out = out + bit * ((1 - digit) if m & bit else digit)
            bit *= 2
        return out

    half = c * rows_h
    sib_half = (1 - c) * rows_h
    own = half + x * rows_o
    pairs = [tuple(range(j * per, (j + 1) * per)) for j in range(chunks)]
    order = pairs[1:] + pairs[:1]
    place = {m: (k, i) for k, ms in enumerate(order) for i, m in enumerate(ms)}
    others = range(1, groups)

    def at_half(k):
        return rows_at(k * rows_m + half, rows_h, rows_h)

    def at_own_block(m):
        k, i = place[m]
        return pl.ds(k * rows_o + i * capacity, capacity)

    def at_sib_half(k):
        return rows_at(k * rows_m + sib_half, rows_h, rows_h)

    def at_block(m):
        k, i = place[m]
        return rows_at(k * rows_m + own + i * capacity, capacity, capacity)

    def at_all(k):
        return pl.ds(k * rows_m, rows_m)

    def copy_to(device, src, dst, send, recv):
        return pltpu.make_async_remote_copy(
            src_ref=src,
            dst_ref=dst,
            send_sem=send,
            recv_sem=recv,
            device_id=device,
            device_id_type=MESH,
        )

    def route(kind, m):
        n = ROUTE_KINDS.index(kind)
        to = flipped(m)
        theirs = rows_at(to * capacity, capacity, capacity)
        mine = rows_at(e * capacity, capacity, capacity)
        if kind == "x":
            src = pack_x.at[theirs]
            dst = xa.at[at_block(m)]
        elif kind == "ct":
            src = pack_ct.at[theirs]
            dst = ct_own.at[at_own_block(m)]
        elif kind == "totals":
            src = dst = totals_in.at[e]
        else:
            s = 0 if kind == "mixed" else 1
            src = back_out.at[s, at_own_block(m)]
            dst = back_in.at[s, mine]
        return copy_to((to, b), src, dst, route_send.at[n, m], route_recv.at[n, m])

    def link(kind, k):
        n = LINK_KINDS.index(kind)
        if kind in ("x", "g"):
            src = dst = {"x": xa, "g": ga}[kind].at[at_block(k)]
        elif kind in ("sum0", "ngrad1"):
            s = 0 if kind == "sum0" else 1
            at = pl.ds(k * rows_h, rows_h)
            src, dst = half_out.at[s, at], half_in.at[s, at]
        elif kind == "out":
            at = pl.ds(k * rows_o, rows_o)
            src, dst = own_out.at[0, at], own_in.at[0, at]
        else:
            at = at_own_block(k)
            src, dst = own_out.at[1, at], own_in.at[1, at]
        return copy_to(far, src, dst, link_send.at[n, k], link_recv.at[n, k])

    def core(kind, k):
        n = CORE_KINDS.index(kind)
        whole = {"x": xa, "g": ga, "h": ha, "hgrad": hga}
        if kind in whole:
            src = dst = whole[kind].at[at_half(k)]
        else:
            s = PART_SLOT[kind]
            src = part.at[s, at_sib_half(k)]
            dst = part_in.at[s, pl.ds(k * rows_h, rows_h)]
        return copy_to(sib, src, dst, core_send.at[n, k], core_recv.at[n, k])

    barrier = pltpu.get_barrier_semaphore()
    peers = [sib, far] + [(flipped(m), b) for m in range(1, groups)]
    for peer in peers:
        pl.semaphore_signal(barrier, inc=1, device_id=peer, device_id_type=MESH)
    arrivals = [
        pltpu.make_async_copy(src, dst, in_sem.at[n])
        for n, (src, dst) in enumerate(
            (
                (ids_hbm, ids_ref),
                (slots_hbm, slots_ref),
                (tok_hbm, tok_ref),
                (ct_hbm, ct_ref),
                (cent_hbm, cent_ref),
                (gain_hbm, gain_ref),
                (bias_hbm, bias_ref),
                (up_bias_hbm, up_bias_ref),
                (down_bias_hbm, down_bias_ref),
            )
        )
    ]
    loads = []
    for j in range(2):
        loads.append(pltpu.make_async_copy(up_hbm.at[j, 0], up_w.at[j], w_sem.at[2 * j]))
        loads.append(pltpu.make_async_copy(down_hbm.at[j, 0], down_w.at[j], w_sem.at[2 * j + 1]))
    for load in arrivals + loads:
        load.start()
    acc[...] = jnp.zeros_like(acc)
    acc_0[...] = jnp.zeros_like(acc_0)
    red[...] = jnp.zeros_like(red)
    arrivals[0].wait()
    arrivals[1].wait()
    target = jnp.where(
        slots_ref[...] >= 0, ids_ref[...] * capacity + slots_ref[...], -1
    )
    slot = lax.broadcasted_iota(jnp.int32, (tok_rows, tok_rows), 0)
    onehot = jnp.where(slot == target, 1.0, 0.0)
    perm[...] = onehot.astype(BF16)
    empty = EMPTY * (1.0 - jnp.sum(onehot, axis=1, keepdims=True))

    def pack_tokens(start, step):
        cols = rows_at(start, step, step)
        pack_x[:, cols] = (dot(perm[...], tok_ref[:, cols], NN) + empty).astype(BF16)

    def pack_cotangent(start, step):
        cols = rows_at(start, step, step)
        pack_ct[:, cols] = dot(perm[...], ct_ref[:, cols], NN).astype(BF16)

    arrivals[2].wait()
    loop_rows(width, COL_STEP, pack_tokens)
    arrivals[3].wait()
    loop_rows(width, COL_STEP, pack_cotangent)
    for arrival in arrivals[4:]:
        arrival.wait()
    cent_rows = cent_ref[...].astype(F32)
    cent_at = lax.broadcasted_iota(jnp.int32, cent_rows.shape, 0)
    cent = jnp.sum(jnp.where(cent_at == e, cent_rows, 0.0), axis=0, keepdims=True)
    pl.semaphore_wait(barrier, len(peers))
    mine = rows_at(e * capacity, capacity, capacity)
    xa[at_block(0)] = pack_x[mine]
    ct_own[at_own_block(0)] = pack_ct[mine]

    def send_x(m):
        if m:
            route("x", m).wait_recv()
        link("x", m).start()

    def send_g(m):
        if m:
            route("ct", m).wait_recv()
        at_o = at_own_block(m)
        values = xa[at_block(m)].astype(F32)
        gate = jax.nn.sigmoid(jnp.sum(values * cent, axis=-1, keepdims=True))
        gate_s[at_o] = jnp.broadcast_to(gate, (capacity, 128))
        ga[at_block(m)] = (gate * ct_own[at_o].astype(F32)).astype(BF16)
        used = jnp.where(values[:, 0:1] < 7.0, 1.0, 0.0)
        acc[3:4] += jnp.broadcast_to(jnp.sum(used * gate, axis=0, keepdims=True), (1, width))
        acc[4:5] += jnp.broadcast_to(jnp.sum(used, axis=0, keepdims=True), (1, width))
        link("g", m).start()

    def spread(kind, k):
        for m in order[k]:
            link(kind, m).wait_recv()
        core(kind, k).start()

    def up_step(j, rows_ref, k):
        gain = gain_ref[j : j + 1].astype(F32)
        bias = bias_ref[j : j + 1].astype(F32)

        def norm(start, step):
            at = rows_at(k * rows_m + start, step, step)
            rhat, _ = normalize(rows_ref[at].astype(F32))
            n_s[j][at] = (rhat * gain + bias).astype(BF16)

        loop_tiles(rows_m, 2 * ROW_STEP, norm)

        def up(start, step):
            cols = rows_at(start, step, step)
            pre = dot(n_s[j][at_all(k)], up_w[j, :, cols], NN) + up_bias_ref[j : j + 1, cols].astype(
                F32
            )
            cdf = 0.5 * (1.0 + lax.erf(pre * (0.5**0.5)))
            pdf = jnp.exp(-0.5 * pre * pre) * 0.3989422804014327
            a_s[j][at_all(k), cols] = (pre * cdf).astype(BF16)
            d_s[j][at_all(k), cols] = (cdf + pre * pdf).astype(BF16)

        loop_rows(hidden, COL_STEP, up)

    def down_step(j, k):
        kind = "part%d" % j
        if j == 1:
            core("part0", k).wait_send()

        def down(start, step):
            cols = rows_at(start, step, step)
            part[0, at_all(k), cols] = dot(a_s[j][at_all(k)], down_w[j, :, cols], NN).astype(BF16)

        loop_tiles(width, 2 * COL_STEP, down)
        core(kind, k).start()

    def back_step(j, grads_ref, k):
        kind = "ngrad%d" % j
        if j == 0:
            core("ngrad1", k).wait_send()

        def act(start, step):
            cols = rows_at(start, step, step)
            grad = dot(grads_ref[at_all(k)], down_w[j, cols, :], NT)
            d_s[j][at_all(k), cols] = (grad * d_s[j][at_all(k), cols].astype(F32)).astype(BF16)

        loop_tiles(hidden, 2 * COL_STEP, act)

        def up_back(start, step):
            cols = rows_at(start, step, step)
            part[1, at_all(k), cols] = dot(d_s[j][at_all(k)], up_w[j, cols, :], NT).astype(BF16)

        loop_tiles(width, 2 * COL_STEP, up_back)
        core(kind, k).start()

    def sum_half(kind, link_kind, k):
        s = PART_SLOT[kind]
        o = ("sum0", "ngrad1").index(link_kind)
        core(kind, k).wait_recv()

        def add_half(start, step):
            at = rows_at(k * rows_m + half + start, step, step)
            at_h = rows_at(k * rows_h + start, step, step)
            total = part[s, at].astype(F32) + part_in[s, at_h].astype(F32)
            half_out[o, at_h] = total.astype(BF16)

        loop_rows(rows_h, ROW_STEP, add_half)
        link(link_kind, k).start()

    def sum_far(kind, link_kind, k):
        s = PART_SLOT[kind]
        o = ("out", "ngrad0").index(link_kind)
        core(kind, k).wait_recv()

        def add_far(start, step):
            at = rows_at(k * rows_m + half + (1 - x) * rows_o + start, step, step)
            at_h = rows_at(k * rows_h + (1 - x) * rows_o + start, step, step)
            at_o = rows_at(k * rows_o + start, step, step)
            total = part[s, at].astype(F32) + part_in[s, at_h].astype(F32)
            own_out[o, at_o] = total.astype(BF16)

        loop_rows(rows_o, ROW_STEP, add_far)
        if link_kind in BLOCK_KINDS:
            for m in reversed(order[k]):
                link(link_kind, m).start()
        else:
            link(link_kind, k).start()

    def sum_own(s, o, k, start, step):
        at = rows_at(k * rows_m + own + start, step, step)
        at_h = rows_at(k * rows_h + x * rows_o + start, step, step)
        at_o = rows_at(k * rows_o + start, step, step)
        mine = part[s, at].astype(F32) + part_in[s, at_h].astype(F32)
        return mine + own_in[o, at_o].astype(F32)

    def make_h(k):
        link("sum0", k).wait_recv()
        shift = down_bias_ref[0:1].astype(F32)

        def add_h(start, step):
            at = rows_at(k * rows_m + half + start, step, step)
            at_h = rows_at(k * rows_h + start, step, step)
            total = half_out[0, at_h].astype(F32) + half_in[0, at_h].astype(F32)
            ha[at] = (xa[at].astype(F32) + total + shift).astype(BF16)

        loop_rows(rows_h, ROW_STEP, add_h)
        core("h", k).start()

    def norm_back(rows, ngrad, gain):
        rhat, scale = normalize(rows)
        q = ngrad * gain
        back = scale * (
            q - jnp.mean(q, axis=-1, keepdims=True) - rhat * jnp.mean(q * rhat, axis=-1, keepdims=True)
        )
        return back, rhat

    def make_hgrad(k):
        link("ngrad1", k).wait_recv()
        gain = gain_ref[1:2].astype(F32)

        def grad_h(start, step):
            at = rows_at(k * rows_m + half + start, step, step)
            at_h = rows_at(k * rows_h + start, step, step)
            ngrad = half_out[1, at_h].astype(F32) + half_in[1, at_h].astype(F32)
            back, rhat = norm_back(ha[at].astype(F32), ngrad, gain)
            hga[at] = (ga[at].astype(F32) + back).astype(BF16)
            acc[0:1] += 0.5 * jnp.sum(ngrad * rhat, axis=0, keepdims=True)
            acc[1:2] += 0.5 * jnp.sum(ngrad, axis=0, keepdims=True)

        loop_tiles(rows_h, ROW_STEP, grad_h)
        core("hgrad", k).start()

    def give_back(kind, m):
        if m:
            route(kind, m).start()
        else:
            s = 0 if kind == "mixed" else 1
            back_in[s, mine] = back_out[s, at_own_block(0)]

    def make_mixed(k):
        link("out", k).wait_recv()
        shift = down_bias_ref[1:2].astype(F32)

        def mix(start, step):
            at = rows_at(k * rows_m + own + start, step, step)
            at_o = rows_at(k * rows_o + start, step, step)
            out = (ha[at].astype(F32) + sum_own(0, 0, k, start, step) + shift).astype(BF16).astype(F32)
            rows = xa[at].astype(F32)
            gate = gate_s[at_o][:, 0:1]
            back_out[0, at_o] = (rows + gate * out).astype(BF16)
            along = jnp.sum(ct_own[at_o].astype(F32) * out, axis=-1, keepdims=True)
            lgrad = (along * gate * (1.0 - gate)).astype(BF16).astype(F32)
            lg_s[at_o] = jnp.broadcast_to(lgrad, (step, 128))
            acc[2:3] += jnp.sum(lgrad * rows, axis=0, keepdims=True)

        loop_rows(rows_o, ROW_STEP, mix)
        for m in reversed(order[k]):
            give_back("mixed", m)

    def norm_sums(k):
        def sum_rows(start, step):
            at = rows_at(k * rows_m + half + start, step, step)
            at_h = rows_at(k * rows_h + start, step, step)
            ngrad = part[1, at].astype(F32) + part_in[1, at_h].astype(F32)
            rhat, _ = normalize(xa[at].astype(F32))
            acc_0[0:1] += jnp.sum(ngrad * rhat, axis=0, keepdims=True)
            acc_0[1:2] += jnp.sum(ngrad, axis=0, keepdims=True)

        loop_tiles(rows_h, ROW_STEP, sum_rows)

    def make_tgrad(m):
        link("ngrad0", m).wait_recv()
        k, i = place[m]
        at_o = at_own_block(m)
        at = at_block(m)
        ngrad = sum_own(1, 1, k, i * capacity, capacity)
        back, _ = norm_back(xa[at].astype(F32), ngrad, gain_ref[0:1].astype(F32))
        back = (hga[at].astype(F32) + back).astype(BF16).astype(F32)
        back_out[1, at_o] = (
            ct_own[at_o].astype(F32) + lg_s[at_o][:, 0:1] * cent + back
        ).astype(BF16)
        give_back("tgrad", m)

    def column_sums(rows_ref):
        def one(i, total):
            values = rows_ref[rows_at(i * ROW_STEP, ROW_STEP, ROW_STEP)].astype(F32)
            return total + jnp.sum(values, axis=0, keepdims=True)

        return lax.fori_loop(
            0, rows_ref.shape[0] // ROW_STEP, one, jnp.zeros((1, rows_ref.shape[1]), F32)
        )

    def weight_grad(q):
        into, left, right = ((down_grad_ref, a_1, ga), (up_grad_ref, n_1, d_1))[q // 2]
        if q == 0:
            small_ref[4:5] = column_sums(right)
        if q == 2:
            small_ref[5:6] = column_sums(right)
        count = left.shape[1] // 2

        def tile(start, step):
            at = rows_at(q % 2 * count + start, step, step)
            into[at] = dot(left[:, at], right[...], TN).astype(BF16)

        loop_tiles(count, COL_STEP, tile)

    lanes = width // 128
    red_rows = (3 * lanes + 8, 2 * lanes)

    def over(s):
        at = pl.ds(0, red_rows[s])
        return copy_to(
            sib, red.at[s, 0, at], red.at[s, 1, at], red_send.at[s, 0], red_recv.at[s, 0]
        )

    def across(s):
        at = pl.ds(0, red_rows[s])
        return copy_to(
            far, red.at[s, 0, at], red.at[s, 2, at], red_send.at[s, 1], red_recv.at[s, 1]
        )

    def total(s, step):
        rows_ref = (acc, acc_0)[s]
        if step == 0:
            for r in range(3 - s):
                for i in range(lanes):
                    red[s, 0, r * lanes + i : r * lanes + i + 1] = rows_ref[
                        r : r + 1, i * 128 : (i + 1) * 128
                    ]
            if s == 0:
                red[s, 0, 3 * lanes : 3 * lanes + 2] = rows_ref[3:5, 0:128]
            over(s).start()
        elif step == 1:
            over(s).wait()
            red[s, 0] = red[s, 0] + red[s, 1]
            across(s).start()
        else:
            across(s).wait()
            sums = red[s, 0] + red[s, 2]
            for r in range(2):
                for i in range(lanes):
                    small_ref[2 * r + 1 - s : 2 * r + 2 - s, i * 128 : (i + 1) * 128] = sums[
                        r * lanes + i : r * lanes + i + 1
                    ]
            if s == 0:
                totals_in[e, 0 : lanes + 2] = sums[2 * lanes : 3 * lanes + 2]
                for m in others:
                    route("totals", m).start()

    def unpack(s):
        kind, out_ref = (("mixed", mixed_ref), ("tgrad", tgrad_ref))[s]
        for m in others:
            route(kind, m).wait_recv()

        def place_tokens(start, step):
            cols = rows_at(start, step, step)
            out_ref[:, cols] = dot(perm[...], back_in[s, :, cols], TN).astype(BF16)

        loop_rows(width, COL_STEP, place_tokens)

    steps = range(chunks)

    def up_0(k):
        if k == first_use[0]:
            loads[0].wait()
        core("x", k).wait_recv()
        up_step(0, xa, k)

    def down_0(k):
        if k == first_use[2]:
            loads[1].wait()
        down_step(0, k)

    def up_1(k):
        if k == first_use[1]:
            loads[2].wait()
            loads[3].wait()
        core("h", k).wait_recv()
        up_step(1, ha, k)

    def back_1(k):
        core("g", k).wait_recv()
        back_step(1, ga, k)

    def back_0(k):
        core("hgrad", k).wait_recv()
        hg_0[at_all(k)] = hga[at_all(k)]
        back_step(0, hga, k)

    tasks = {
        "RX": lambda m: route("x", m).start(),
        "RC": lambda m: route("ct", m).start(),
        "SX": send_x,
        "SG": send_g,
        "PX": functools.partial(spread, "x"),
        "PG": functools.partial(spread, "g"),
        "U0": up_0,
        "D0": down_0,
        "S0": functools.partial(sum_half, "part0", "sum0"),
        "H": make_h,
        "U1": up_1,
        "B1": back_1,
        "D1": functools.partial(down_step, 1),
        "S1": functools.partial(sum_half, "ngrad1", "ngrad1"),
        "SO": functools.partial(sum_far, "part1", "out"),
        "HG": make_hgrad,
        "MX": make_mixed,
        "B0": back_0,
        "SQ": functools.partial(sum_far, "ngrad0", "ngrad0"),
        "GS": norm_sums,
        "TG": make_tgrad,
        "W1": weight_grad,
        "R1": functools.partial(total, 0),
        "R0": functools.partial(total, 1),
        "UP": unpack,
    }
    plan = [word.split(".") for line in SCHEDULE for word in line.split()]
    first_use = [next(int(k) for name, k in plan if name == u) for u in ("U0", "U1", "D0")]
    for name, k in plan:
        tasks[name](int(k))

    for m in others:
        route("totals", m).wait_recv()
    totals_ref[...] = totals_in[...]
    for m in others:
        for kind in ROUTE_KINDS:
            route(kind, m).wait_send()
    for m in range(groups):
        for kind in BLOCK_KINDS:
            link(kind, m).wait_send()
    for k in steps:
        for kind in LINK_KINDS[len(BLOCK_KINDS) :]:
            link(kind, k).wait_send()
        for kind in CORE_KINDS:
            if kind not in ("part0", "ngrad1"):
                core(kind, k).wait_send()


def widen_kernel(
    denominator,
    mixed_ref,
    tgrad_ref,
    totals_ref,
    small_ref,
    up_ref,
    down_ref,
    n_0,
    a_0,
    d_0,
    hg_0,
    mixed_out,
    tgrad_out,
    cent_out,
    gain_out,
    shift_out,
    up_out,
    ub_out,
    down_out,
    db_out,
    mass_out,
    load_out,
    cent_s,
    rows_s,
    up_wide,
    down_wide,
    sem,
    up_sem,
    down_sem,
):
    leaving = []

    def leave(src, dst, semaphore):
        move = pltpu.make_async_copy(src, dst, semaphore)
        move.start()
        leaving.append(move)

    def widen(ref, wide, dst, semaphore, t):
        at = pl.ds(t * COL_STEP, COL_STEP)
        wide[1, at] = ref[at].astype(F32)
        leave(wide.at[1, at], dst.at[1, 0, at], semaphore.at[1, t])

    def multiply(left, right, wide, dst, semaphore, t):
        at = pl.ds(t * COL_STEP, COL_STEP)
        wide[0, at] = dot(left[:, at], right[...], TN)
        leave(wide.at[0, at], dst.at[0, 0, at], semaphore.at[0, t])

    leave(mixed_ref, mixed_out, sem.at[0])
    leave(tgrad_ref, tgrad_out, sem.at[1])
    for t in range(down_wide.shape[1] // COL_STEP):
        widen(down_ref, down_wide, down_out, down_sem, t)
        multiply(a_0, hg_0, down_wide, down_out, down_sem, t)
    for t in range(up_wide.shape[1] // COL_STEP):
        widen(up_ref, up_wide, up_out, up_sem, t)
        multiply(n_0, d_0, up_wide, up_out, up_sem, t)

    def column_sums(ref):
        return jnp.sum(ref[...].astype(F32), axis=0, keepdims=True)

    for i in range(cent_s.shape[1] // 128):
        cent_s[:, i * 128 : (i + 1) * 128] = totals_ref[:, i]
    leave(cent_s, cent_out, sem.at[2])
    for j in range(2):
        rows_s[0, j] = small_ref[j : j + 1]
        rows_s[1, j] = small_ref[2 + j : 3 + j]
    rows_s[2, 0] = column_sums(d_0)
    rows_s[2, 1] = small_ref[5:6]
    rows_s[3, 0] = column_sums(hg_0)
    rows_s[3, 1] = small_ref[4:5]
    for n, dst in enumerate((gain_out, shift_out, ub_out, db_out)):
        leave(rows_s.at[n], dst, sem.at[3 + n])
    experts = totals_ref.shape[0]
    diagonal = lax.broadcasted_iota(jnp.int32, (experts, 128), 0) == lax.broadcasted_iota(
        jnp.int32, (experts, 128), 1
    )
    for out, n in ((mass_out, 8), (load_out, 9)):
        values = jnp.sum(jnp.where(diagonal, totals_ref[:, n], 0.0), axis=0)
        out[...] = values[0:experts] / jnp.float32(denominator)
    for move in leaving:
        move.wait()


def per_device_fused(
    tokens,
    lengths,
    expert_ids,
    slots,
    centroids,
    sublayer_norm_gain,
    sublayer_norm_bias,
    up_weight,
    up_bias,
    down_weight,
    down_bias,
    cotangent,
):
    if not fused_fits(tokens, centroids, up_weight):
        return per_device(
            tokens,
            lengths,
            expert_ids,
            slots,
            centroids,
            sublayer_norm_gain,
            sublayer_norm_bias,
            up_weight,
            up_bias,
            down_weight,
            down_bias,
            cotangent,
        )
    tok_rows, width = tokens.shape
    groups = lax.axis_size("expert")
    batches = lax.axis_size("batch")
    experts = centroids.shape[0]
    capacity = tok_rows // experts
    hidden = up_weight.shape[3]
    chunks = 4
    total = groups * batches * capacity
    def flat(values):
        return values.reshape(values.shape[0], -1)

    vmem = pl.BlockSpec(memory_space=pltpu.VMEM)
    hbm = pl.BlockSpec(memory_space=pl.ANY)
    outs = pl.pallas_call(
        functools.partial(fused_kernel, groups, capacity, chunks),
        out_shape=[
            pltpu.VMEM((tok_rows, width), BF16),
            pltpu.VMEM((tok_rows, width), BF16),
            pltpu.VMEM((groups, 16, 128), F32),
            pltpu.VMEM((8, width), F32),
            pltpu.VMEM(up_weight.shape[2:], BF16),
            pltpu.VMEM(down_weight.shape[2:], BF16),
            pltpu.VMEM((total, width), BF16),
            pltpu.VMEM((total, hidden), BF16),
            pltpu.VMEM((total, hidden), BF16),
            pltpu.VMEM((total, width), BF16),
        ],
        in_specs=[pl.BlockSpec(memory_space=pltpu.HBM)] * 11,
        out_specs=[vmem] * 10,
        scratch_shapes=[
            pltpu.VMEM((1, tok_rows), jnp.int32),
            pltpu.VMEM((1, tok_rows), jnp.int32),
            pltpu.VMEM((tok_rows, width), BF16),
            pltpu.VMEM((tok_rows, width), BF16),
            pltpu.VMEM((experts, width), BF16),
            pltpu.VMEM((2, width), BF16),
            pltpu.VMEM((2, width), BF16),
            pltpu.VMEM((2, hidden), BF16),
            pltpu.VMEM((2, width), BF16),
            pltpu.VMEM((2, width, hidden), BF16),
            pltpu.VMEM((2, hidden, width), BF16),
            pltpu.VMEM((tok_rows, tok_rows), BF16),
            pltpu.VMEM((tok_rows, width), BF16),
            pltpu.VMEM((tok_rows, width), BF16),
            pltpu.VMEM((total, width), BF16),
            pltpu.VMEM((total, width), BF16),
            pltpu.VMEM((total, width), BF16),
            pltpu.VMEM((total, width), BF16),
            pltpu.VMEM((total, width), BF16),
            pltpu.VMEM((total, hidden), BF16),
            pltpu.VMEM((total, hidden), BF16),
            pltpu.VMEM((2, total, width), BF16),
            pltpu.VMEM((2, total // 2, width), BF16),
            pltpu.VMEM((2, total // 2, width), BF16),
            pltpu.VMEM((2, total // 2, width), BF16),
            pltpu.VMEM((2, total // 4, width), BF16),
            pltpu.VMEM((2, total // 4, width), BF16),
            pltpu.VMEM((tok_rows, width), BF16),
            pltpu.VMEM((tok_rows, 128), F32),
            pltpu.VMEM((tok_rows, 128), F32),
            pltpu.VMEM((2, tok_rows, width), BF16),
            pltpu.VMEM((2, tok_rows, width), BF16),
            pltpu.VMEM((8, width), F32),
            pltpu.VMEM((8, width), F32),
            pltpu.VMEM((2, 3, 3 * width // 128 + 8, 128), F32),
            pltpu.VMEM((groups, 16, 128), F32),
            pltpu.SemaphoreType.DMA((9,)),
            pltpu.SemaphoreType.DMA((4,)),
            pltpu.SemaphoreType.DMA((len(ROUTE_KINDS), groups)),
            pltpu.SemaphoreType.DMA((len(ROUTE_KINDS), groups)),
            pltpu.SemaphoreType.DMA((len(LINK_KINDS), groups)),
            pltpu.SemaphoreType.DMA((len(LINK_KINDS), groups)),
            pltpu.SemaphoreType.DMA((len(CORE_KINDS), chunks)),
            pltpu.SemaphoreType.DMA((len(CORE_KINDS), chunks)),
            pltpu.SemaphoreType.DMA((2, 2)),
            pltpu.SemaphoreType.DMA((2, 2)),
        ],
        compiler_params=pltpu.CompilerParams(
            collective_id=0, has_side_effects=True, vmem_limit_bytes=46 << 20
        ),
        cost_estimate=pl.CostEstimate(
            flops=24 * total * width * hidden, bytes_accessed=40 << 20, transcendentals=0
        ),
    )(
        expert_ids.reshape(1, tok_rows),
        slots.reshape(1, tok_rows),
        tokens,
        cotangent,
        centroids,
        flat(sublayer_norm_gain),
        flat(sublayer_norm_bias),
        flat(up_bias),
        flat(down_bias),
        up_weight,
        down_weight,
    )
    layers = up_weight.shape[0]
    row = jax.ShapeDtypeStruct((layers, 1, width), F32)
    return pl.pallas_call(
        functools.partial(widen_kernel, capacity * groups * batches),
        out_shape=[
            jax.ShapeDtypeStruct(tokens.shape, BF16),
            jax.ShapeDtypeStruct(tokens.shape, BF16),
            jax.ShapeDtypeStruct((experts, width), F32),
            row,
            row,
            jax.ShapeDtypeStruct(up_weight.shape, F32),
            jax.ShapeDtypeStruct((layers, 1, hidden), F32),
            jax.ShapeDtypeStruct(down_weight.shape, F32),
            row,
            jax.ShapeDtypeStruct((experts,), F32),
            jax.ShapeDtypeStruct((experts,), F32),
        ],
        in_specs=[vmem] * 10,
        out_specs=[hbm] * 9 + [vmem] * 2,
        scratch_shapes=[
            pltpu.VMEM((experts, width), F32),
            pltpu.VMEM((4, layers, 1, width), F32),
            pltpu.VMEM((layers, width, hidden), F32),
            pltpu.VMEM((layers, hidden, width), F32),
            pltpu.SemaphoreType.DMA((7,)),
            pltpu.SemaphoreType.DMA((layers, width // COL_STEP)),
            pltpu.SemaphoreType.DMA((layers, hidden // COL_STEP)),
        ],
        compiler_params=pltpu.CompilerParams(vmem_limit_bytes=24 << 20),
        cost_estimate=pl.CostEstimate(
            flops=0, bytes_accessed=12 * layers * width * hidden, transcendentals=0
        ),
    )(*(pltpu.with_memory_space_constraint(out, pltpu.VMEM) for out in outs))


def solution(mesh):
    in_specs = (
        P(("expert", "batch"), None),
        P(("expert", "batch")),
        P(("expert", "batch")),
        P(("expert", "batch")),
        P(),
        P(None, "expert", None),
        P(None, "expert", None),
        P(None, "expert", None, "batch"),
        P(None, "expert", "batch"),
        P(None, "expert", "batch", None),
        P(None, "expert", None),
        P(("expert", "batch"), None),
    )
    out_specs = (
        P(("expert", "batch"), None),
        P(("expert", "batch"), None),
        P(),
        P(None, "expert", None),
        P(None, "expert", None),
        P(None, "expert", None, "batch"),
        P(None, "expert", "batch"),
        P(None, "expert", "batch", None),
        P(None, "expert", None),
        P(),
        P(),
    )
    return jax.shard_map(
        per_device_fused, mesh=mesh, in_specs=in_specs, out_specs=out_specs, check_vma=False
    )
```

```python
import functools

import jax
import jax.numpy as jnp
from jax import lax
from jax.experimental import pallas as pl
from jax.experimental.pallas import tpu as pltpu
from jax.sharding import PartitionSpec as P


def gelu_exact(values):
    return jax.nn.gelu(values, approximate=False)


def apply_layer_norm(row_block):
    values = row_block.astype(jnp.float32)
    row_mean = jnp.mean(values, axis=-1, keepdims=True)
    centered = values - row_mean
    row_inverse_scale = lax.rsqrt(jnp.mean(centered * centered, axis=-1, keepdims=True) + 1e-05)
    return (centered * row_inverse_scale, row_inverse_scale)


def per_device(
    tokens,
    lengths,
    expert_ids,
    slots,
    centroids,
    sublayer_norm_gain,
    sublayer_norm_bias,
    up_weight,
    up_bias,
    down_weight,
    down_bias,
    cotangent,
):
    tok_rows, width = tokens.shape
    layers = sublayer_norm_gain.shape[0]
    local_count = up_weight.shape[1]
    expert_count = centroids.shape[0]
    capacity = tok_rows // expert_count
    groups = lax.axis_size("expert")
    batches = lax.axis_size("batch")
    position = jnp.arange(tok_rows, dtype=jnp.int32)
    live = (position < lengths[0]).astype(jnp.float32)[:, None]
    target = jnp.where(slots >= 0, expert_ids * capacity + slots, tok_rows)
    source = jnp.full((tok_rows + 1,), -1, jnp.int32).at[target].set(position)[:tok_rows]
    filled = (source >= 0)[:, None]
    safe_source = jnp.maximum(source, 0)
    safe_target = jnp.minimum(target, tok_rows - 1)

    def pack(values):
        return jnp.where(filled, values[safe_source], jnp.zeros((), values.dtype))

    onehot = (expert_ids[:, None] == jnp.arange(expert_count, dtype=jnp.int32)[None, :]).astype(
        jnp.float32
    )
    logits = jnp.einsum("td,ed->te", tokens, centroids, preferred_element_type=jnp.float32)
    gate = jax.nn.sigmoid(jnp.sum(logits * onehot, axis=1))[:, None]
    used = onehot * live
    usage_gate = jnp.sum(used * gate, axis=0)
    usage_count = jnp.sum(used, axis=0)
    gate_total, count_total = lax.psum((usage_gate, usage_count), ("expert", "batch"))

    def expand_hidden(values, expert_layer_step):
        return values[expert_layer_step].astype(jnp.float32)[None, :, None, :]

    arrived = lax.all_to_all(pack(tokens), "expert", split_axis=0, concat_axis=0, tiled=True)
    current = arrived
    inputs = []
    kept = []
    for expert_layer_step in range(layers):
        gathered = lax.all_gather(current, "batch", axis=0, tiled=True)
        row_layout_grid = gathered.reshape(-1, local_count, capacity, width)
        standardized_input, row_inverse_scale = apply_layer_norm(row_layout_grid)
        normalized_rows = (
            standardized_input * expand_hidden(sublayer_norm_gain, expert_layer_step)
            + expand_hidden(sublayer_norm_bias, expert_layer_step)
        ).astype(jnp.bfloat16)
        pre_rows = jnp.einsum(
            "nlcd,ldf->nlcf",
            normalized_rows,
            up_weight[expert_layer_step],
            preferred_element_type=jnp.float32,
        ) + expand_hidden(up_bias, expert_layer_step)
        hidden_parts = (normalized_rows, pre_rows, gelu_exact(pre_rows).astype(jnp.bfloat16))

        def down_part(start, count, activity=hidden_parts[2], expert_layer_step=expert_layer_step):
            return jnp.einsum(
                "nlcf,lfd->nlcd",
                activity,
                down_weight[expert_layer_step],
                preferred_element_type=jnp.float32,
            )

        mixed_part = lax.psum_scatter(
            down_part(jnp.int32(0), lax.axis_size("batch") * groups).astype(jnp.bfloat16),
            "batch",
            scatter_dimension=0,
            tiled=True,
        ).astype(jnp.float32)
        own_grid = current.reshape(groups, local_count, capacity, width).astype(jnp.float32)
        result = (own_grid + mixed_part + expand_hidden(down_bias, expert_layer_step)).astype(
            jnp.bfloat16
        )
        inputs.append(current)
        kept.append(hidden_parts)
        current = result.reshape(tok_rows, width)
    returned = lax.all_to_all(current, "expert", split_axis=0, concat_axis=0, tiled=True)
    expert_tok = returned[safe_target].astype(jnp.float32)
    mixed = (live * (tokens.astype(jnp.float32) + gate * expert_tok)).astype(jnp.bfloat16)
    upstream = cotangent.astype(jnp.float32) * live
    gate_grad = jnp.sum(upstream * expert_tok, axis=1, keepdims=True)
    logit_grad = (gate_grad * gate * (1.0 - gate)).astype(jnp.bfloat16)
    route_grad = (onehot * logit_grad.astype(jnp.float32)).astype(jnp.bfloat16)
    centroid_part = jnp.einsum("te,td->ed", route_grad, tokens, preferred_element_type=jnp.float32)
    gate_input = jnp.einsum("te,ed->td", route_grad, centroids, preferred_element_type=jnp.float32)
    expert_grad = (gate * upstream).astype(jnp.bfloat16)
    grad_rows = lax.all_to_all(pack(expert_grad), "expert", split_axis=0, concat_axis=0, tiled=True)
    gain_parts = [None] * layers
    shift_parts = [None] * layers
    down_bias_parts = [None] * layers
    up_weight_grads = [None] * layers
    up_bias_grads = [None] * layers
    down_weight_grads = [None] * layers
    for expert_layer_step in range(layers - 1, -1, -1):
        own_rows = inputs[expert_layer_step]
        grads_all = lax.all_gather(grad_rows, "batch", axis=0, tiled=True).reshape(
            -1, local_count, capacity, width
        )
        normed, pre_act, activity = kept[expert_layer_step]
        act_grad = jnp.einsum(
            "nlcd,lfd->nlcf",
            grads_all,
            down_weight[expert_layer_step],
            preferred_element_type=jnp.float32,
        )
        pre_grad = jax.vjp(gelu_exact, pre_act)[1](act_grad)[0].astype(jnp.bfloat16)
        down_weight_grads[expert_layer_step] = jnp.einsum(
            "nlcf,nlcd->lfd", activity, grads_all, preferred_element_type=jnp.float32
        )
        up_weight_grads[expert_layer_step] = jnp.einsum(
            "nlcd,nlcf->ldf", normed, pre_grad, preferred_element_type=jnp.float32
        )
        up_bias_grads[expert_layer_step] = jnp.sum(pre_grad.astype(jnp.float32), axis=(0, 2))

        def up_part(start, count, pre_grad=pre_grad, expert_layer_step=expert_layer_step):
            return jnp.einsum(
                "nlcf,ldf->nlcd",
                pre_grad,
                up_weight[expert_layer_step],
                preferred_element_type=jnp.float32,
            )

        normed_grad = lax.psum_scatter(
            up_part(jnp.int32(0), lax.axis_size("batch") * groups).astype(jnp.bfloat16),
            "batch",
            scatter_dimension=0,
            tiled=True,
        ).astype(jnp.float32)
        out_grad = grad_rows.reshape(groups, local_count, capacity, width).astype(jnp.float32)
        down_bias_parts[expert_layer_step] = jnp.sum(out_grad, axis=(0, 2))
        own_hat, own_scale = apply_layer_norm(
            own_rows.reshape(groups, local_count, capacity, width)
        )
        gain_parts[expert_layer_step] = jnp.sum(normed_grad * own_hat, axis=(0, 2))
        shift_parts[expert_layer_step] = jnp.sum(normed_grad, axis=(0, 2))
        hat_grad = normed_grad * expand_hidden(sublayer_norm_gain, expert_layer_step)
        row_grad = own_scale * (
            hat_grad
            - jnp.mean(hat_grad, axis=-1, keepdims=True)
            - own_hat * jnp.mean(hat_grad * own_hat, axis=-1, keepdims=True)
        )
        grad_rows = (out_grad + row_grad).astype(jnp.bfloat16).reshape(tok_rows, width)
    gain_grad, shift_grad, down_bias_grad = lax.psum(
        (jnp.stack(gain_parts), jnp.stack(shift_parts), jnp.stack(down_bias_parts)), "batch"
    )
    token_back = lax.all_to_all(grad_rows, "expert", split_axis=0, concat_axis=0, tiled=True)
    tokens_grad = (
        upstream + gate_input + live * token_back[safe_target].astype(jnp.float32)
    ).astype(jnp.bfloat16)
    centroid_grad = lax.psum(centroid_part, ("expert", "batch"))
    denominator = jnp.float32(capacity * groups * batches)
    gate_mass = gate_total / denominator
    load = count_total / denominator
    return (
        mixed,
        tokens_grad,
        centroid_grad,
        gain_grad,
        shift_grad,
        jnp.stack(up_weight_grads),
        jnp.stack(up_bias_grads),
        jnp.stack(down_weight_grads),
        down_bias_grad,
        gate_mass,
        load,
    )


MESH = pl.DeviceIdType.MESH
F32 = jnp.float32
BF16 = jnp.bfloat16
ROW_STEP = 64
COL_STEP = 256
EMPTY = 8.0
BLOCK_KINDS = ("x", "g", "ngrad0")
LINK_KINDS = BLOCK_KINDS + ("sum0", "out", "ngrad1")
CORE_KINDS = ("x", "g", "part0", "h", "part1", "ngrad1", "hgrad", "ngrad0")
SCHEDULE = (
    "RX.1 RX.2 RX.3 RX.4",
    "RX.5 RX.6 RX.7 SX.0",
    "PC.0 RC.1 RC.2 RC.3",
    "RC.4 RC.5 RC.6 RC.7",
    "SG.0 SX.1 SX.2 SX.3",
    "SX.4 SX.5 PX.3 PX.0",
    "SG.2 SX.6 SG.1 U0.0",
    "PX.1 D0.0 SX.7 SG.3",
    "U0.1 S0.0 U0.3 D0.1",
    "PX.2 S0.1 U0.2 SG.5",
    "SG.4 H.0 D0.2 D0.3",
    "SG.7 S0.3 H.1 S0.2",
    "U1.1 SG.6 PG.0 D1.1",
    "U1.0 SO.1 PG.1 H.3",
    "B1.1 D1.0 B1.0 H.2",
    "S1.1 U1.2 S1.0 PG.3",
    "PG.2 U1.3 D1.2 B1.2",
    "HG.1 S1.2 B1.3 MX.1",
    "B0.1 W1.3 SO.2 HG.0",
    "SQ.1 B0.0 S1.3 HG.2",
    "D1.3 SO.0 GS.1 TG.5",
    "B0.2 SO.3 TG.4 W1.0",
    "MX.2 SQ.2 GS.2 HG.3",
    "W1.2 SQ.0 B0.3 MX.0",
    "MX.3 R1.0 TG.7 GS.0",
    "TG.6 R1.1 SQ.3 GS.3",
    "R0.0 TG.3 R0.1 R1.2",
    "TG.2 TG.1 R0.2 TG.0",
    "W1.1 UP.0 UP.1",
)
PART_SLOT = {"part0": 0, "part1": 0, "ngrad1": 1, "ngrad0": 1}
ROUTE_KINDS = ("x", "ct", "mixed", "tgrad", "totals")


def fused_fits(tokens, centroids, up_weight):
    tok_rows, width = tokens.shape
    groups, capacity = lax.axis_size("expert"), tok_rows // centroids.shape[0]
    return (
        lax.axis_size("batch") == 4
        and groups == 8
        and up_weight.shape[:2] == (2, 1)
        and centroids.shape[0] == groups
        and up_weight.shape[3] == width
        and width % (4 * COL_STEP) == 0
        and capacity % 32 == 0
    )


def rows_at(start, count, unit):
    return pl.ds(pl.multiple_of(start, unit), count)


def loop_rows(count, step, body):
    step = min(step, count)
    for start in range(0, count, step):
        body(start, step)


def loop_tiles(count, step, body):
    def one(i, carry):
        body(pl.multiple_of(i * step, step), step)
        return carry

    lax.fori_loop(0, count // step, one, 0)


def normalize(values):
    centered = values - jnp.mean(values, axis=-1, keepdims=True)
    scale = lax.rsqrt(jnp.mean(centered * centered, axis=-1, keepdims=True) + 1e-05)
    return centered * scale, scale


def dot(a, b, dims):
    return lax.dot_general(a, b, (dims, ((), ())), preferred_element_type=F32)


NN = ((1,), (0,))
NT = ((1,), (1,))
TN = ((0,), (0,))


def fused_kernel(
    groups,
    capacity,
    chunks,
    ids_hbm,
    slots_hbm,
    tok_hbm,
    ct_hbm,
    cent_hbm,
    gain_hbm,
    bias_hbm,
    up_bias_hbm,
    down_bias_hbm,
    up_hbm,
    down_hbm,
    mixed_ref,
    tgrad_ref,
    totals_ref,
    small_ref,
    up_grad_ref,
    down_grad_ref,
    n_0,
    a_0,
    d_0,
    hg_0,
    ids_ref,
    slots_ref,
    tok_ref,
    ct_ref,
    cent_ref,
    gain_ref,
    bias_ref,
    up_bias_ref,
    down_bias_ref,
    up_w,
    down_w,
    perm,
    pack_x,
    pack_ct,
    xa,
    ga,
    ha,
    hga,
    n_1,
    a_1,
    d_1,
    part,
    part_in,
    half_out,
    half_in,
    own_out,
    own_in,
    ct_own,
    gate_s,
    lg_s,
    back_out,
    back_in,
    acc,
    acc_0,
    cent_s,
    red,
    totals_in,
    in_sem,
    w_sem,
    route_send,
    route_recv,
    link_send,
    link_recv,
    core_send,
    core_recv,
    red_send,
    red_recv,
):
    tok_rows, width = tok_ref.shape
    hidden = up_w.shape[2]
    n_s, a_s, d_s = (n_0, n_1), (a_0, a_1), (d_0, d_1)
    per = groups // chunks
    rows_m = per * 4 * capacity
    rows_h = rows_m // 2
    rows_o = rows_m // 4
    e = lax.axis_index("expert")
    b = lax.axis_index("batch")
    x = b // 2
    c = lax.rem(b, 2)
    sib = (e, x * 2 + (1 - c))
    far = (e, (1 - x) * 2 + c)

    def flipped(m):
        out = jnp.int32(0)
        bit = 1
        while bit < groups:
            digit = lax.rem(e // bit, 2)
            out = out + bit * ((1 - digit) if m & bit else digit)
            bit *= 2
        return out

    half = c * rows_h
    sib_half = (1 - c) * rows_h
    own = half + x * rows_o
    pairs = [tuple(range(j * per, (j + 1) * per)) for j in range(chunks)]
    order = pairs[1:] + pairs[:1]
    place = {m: (k, i) for k, ms in enumerate(order) for i, m in enumerate(ms)}
    others = range(1, groups)

    def at_half(k):
        return rows_at(k * rows_m + half, rows_h, rows_h)

    def at_own_block(m):
        k, i = place[m]
        return pl.ds(k * rows_o + i * capacity, capacity)

    def at_sib_half(k):
        return rows_at(k * rows_m + sib_half, rows_h, rows_h)

    def at_block(m):
        k, i = place[m]
        return rows_at(k * rows_m + own + i * capacity, capacity, capacity)

    def at_all(k):
        return pl.ds(k * rows_m, rows_m)

    def copy_to(device, src, dst, send, recv):
        return pltpu.make_async_remote_copy(
            src_ref=src,
            dst_ref=dst,
            send_sem=send,
            recv_sem=recv,
            device_id=device,
            device_id_type=MESH,
        )

    def route(kind, m):
        n = ROUTE_KINDS.index(kind)
        to = flipped(m)
        theirs = rows_at(to * capacity, capacity, capacity)
        mine = rows_at(e * capacity, capacity, capacity)
        if kind == "x":
            src = pack_x.at[theirs]
            dst = xa.at[at_block(m)]
        elif kind == "ct":
            src = pack_ct.at[theirs]
            dst = ct_own.at[at_own_block(m)]
        elif kind == "totals":
            src = dst = totals_in.at[e]
        else:
            s = 0 if kind == "mixed" else 1
            src = back_out.at[s, at_own_block(m)]
            dst = back_in.at[s, mine]
        return copy_to((to, b), src, dst, route_send.at[n, m], route_recv.at[n, m])

    def link(kind, k):
        n = LINK_KINDS.index(kind)
        if kind in ("x", "g"):
            src = dst = {"x": xa, "g": ga}[kind].at[at_block(k)]
        elif kind in ("sum0", "ngrad1"):
            s = 0 if kind == "sum0" else 1
            at = pl.ds(k * rows_h, rows_h)
            src, dst = half_out.at[s, at], half_in.at[s, at]
        elif kind == "out":
            at = pl.ds(k * rows_o, rows_o)
            src, dst = own_out.at[0, at], own_in.at[0, at]
        else:
            at = at_own_block(k)
            src, dst = own_out.at[1, at], own_in.at[1, at]
        return copy_to(far, src, dst, link_send.at[n, k], link_recv.at[n, k])

    def core(kind, k):
        n = CORE_KINDS.index(kind)
        whole = {"x": xa, "g": ga, "h": ha, "hgrad": hga}
        if kind in whole:
            src = dst = whole[kind].at[at_half(k)]
        else:
            s = PART_SLOT[kind]
            src = part.at[s, at_sib_half(k)]
            dst = part_in.at[s, pl.ds(k * rows_h, rows_h)]
        return copy_to(sib, src, dst, core_send.at[n, k], core_recv.at[n, k])

    barrier = pltpu.get_barrier_semaphore()
    peers = [sib, far] + [(flipped(m), b) for m in range(1, groups)]
    for peer in peers:
        pl.semaphore_signal(barrier, inc=1, device_id=peer, device_id_type=MESH)
    arrivals = [
        pltpu.make_async_copy(src, dst, in_sem.at[n])
        for n, (src, dst) in enumerate(
            (
                (ids_hbm, ids_ref),
                (slots_hbm, slots_ref),
                (tok_hbm, tok_ref),
                (ct_hbm, ct_ref),
                (cent_hbm, cent_ref),
                (gain_hbm, gain_ref),
                (bias_hbm, bias_ref),
                (up_bias_hbm, up_bias_ref),
                (down_bias_hbm, down_bias_ref),
            )
        )
    ]
    loads = []
    for j in range(2):
        loads.append(pltpu.make_async_copy(up_hbm.at[j, 0], up_w.at[j], w_sem.at[2 * j]))
        loads.append(pltpu.make_async_copy(down_hbm.at[j, 0], down_w.at[j], w_sem.at[2 * j + 1]))
    for load in arrivals + loads:
        load.start()
    acc[...] = jnp.zeros_like(acc)
    acc_0[...] = jnp.zeros_like(acc_0)
    red[...] = jnp.zeros_like(red)
    arrivals[0].wait()
    arrivals[1].wait()
    target = jnp.where(
        slots_ref[...] >= 0, ids_ref[...] * capacity + slots_ref[...], -1
    )
    slot = lax.broadcasted_iota(jnp.int32, (tok_rows, tok_rows), 0)
    onehot = jnp.where(slot == target, 1.0, 0.0)
    perm[...] = onehot.astype(BF16)
    empty = EMPTY * (1.0 - jnp.sum(onehot, axis=1, keepdims=True))

    def pack_tokens(start, step):
        cols = rows_at(start, step, step)
        pack_x[:, cols] = (dot(perm[...], tok_ref[:, cols], NN) + empty).astype(BF16)

    def pack_cotangent(start, step):
        cols = rows_at(start, step, step)
        pack_ct[:, cols] = dot(perm[...], ct_ref[:, cols], NN).astype(BF16)

    arrivals[2].wait()
    loop_rows(width, COL_STEP, pack_tokens)
    pl.semaphore_wait(barrier, len(peers))
    mine = rows_at(e * capacity, capacity, capacity)
    xa[at_block(0)] = pack_x[mine]

    def prepare_cotangent(_):
        arrivals[3].wait()
        loop_rows(width, COL_STEP, pack_cotangent)
        ct_own[at_own_block(0)] = pack_ct[mine]
        for arrival in arrivals[4:]:
            arrival.wait()
        cent_rows = cent_ref[...].astype(F32)
        cent_at = lax.broadcasted_iota(jnp.int32, cent_rows.shape, 0)
        cent_s[0:1] = jnp.sum(jnp.where(cent_at == e, cent_rows, 0.0), axis=0, keepdims=True)

    def send_x(m):
        if m:
            route("x", m).wait_recv()
        link("x", m).start()

    def send_g(m):
        if m:
            route("ct", m).wait_recv()
        at_o = at_own_block(m)
        values = xa[at_block(m)].astype(F32)
        gate = jax.nn.sigmoid(jnp.sum(values * cent_s[0:1], axis=-1, keepdims=True))
        gate_s[at_o] = jnp.broadcast_to(gate, (capacity, 128))
        ga[at_block(m)] = (gate * ct_own[at_o].astype(F32)).astype(BF16)
        used = jnp.where(values[:, 0:1] < 7.0, 1.0, 0.0)
        acc[3:4] += jnp.broadcast_to(jnp.sum(used * gate, axis=0, keepdims=True), (1, width))
        acc[4:5] += jnp.broadcast_to(jnp.sum(used, axis=0, keepdims=True), (1, width))
        link("g", m).start()

    def spread(kind, k):
        for m in order[k]:
            link(kind, m).wait_recv()
        core(kind, k).start()

    def up_step(j, rows_ref, k):
        gain = gain_ref[j : j + 1].astype(F32)
        bias = bias_ref[j : j + 1].astype(F32)

        def norm(start, step):
            at = rows_at(k * rows_m + start, step, step)
            rhat, _ = normalize(rows_ref[at].astype(F32))
            n_s[j][at] = (rhat * gain + bias).astype(BF16)

        loop_tiles(rows_m, 2 * ROW_STEP, norm)

        def up(start, step):
            cols = rows_at(start, step, step)
            pre = dot(n_s[j][at_all(k)], up_w[j, :, cols], NN) + up_bias_ref[j : j + 1, cols].astype(
                F32
            )
            cdf = 0.5 * (1.0 + lax.erf(pre * (0.5**0.5)))
            pdf = jnp.exp(-0.5 * pre * pre) * 0.3989422804014327
            a_s[j][at_all(k), cols] = (pre * cdf).astype(BF16)
            d_s[j][at_all(k), cols] = (cdf + pre * pdf).astype(BF16)

        loop_rows(hidden, COL_STEP, up)

    def down_step(j, k):
        kind = "part%d" % j
        if j == 1:
            core("part0", k).wait_send()

        def down(start, step):
            cols = rows_at(start, step, step)
            part[0, at_all(k), cols] = dot(a_s[j][at_all(k)], down_w[j, :, cols], NN).astype(BF16)

        loop_tiles(width, 2 * COL_STEP, down)
        core(kind, k).start()

    def back_step(j, grads_ref, k):
        kind = "ngrad%d" % j
        if j == 0:
            core("ngrad1", k).wait_send()

        def act(start, step):
            cols = rows_at(start, step, step)
            grad = dot(grads_ref[at_all(k)], down_w[j, cols, :], NT)
            d_s[j][at_all(k), cols] = (grad * d_s[j][at_all(k), cols].astype(F32)).astype(BF16)

        loop_tiles(hidden, 2 * COL_STEP, act)

        def up_back(start, step):
            cols = rows_at(start, step, step)
            part[1, at_all(k), cols] = dot(d_s[j][at_all(k)], up_w[j, cols, :], NT).astype(BF16)

        loop_tiles(width, 2 * COL_STEP, up_back)
        core(kind, k).start()

    def sum_half(kind, link_kind, k):
        s = PART_SLOT[kind]
        o = ("sum0", "ngrad1").index(link_kind)
        core(kind, k).wait_recv()

        def add_half(start, step):
            at = rows_at(k * rows_m + half + start, step, step)
            at_h = rows_at(k * rows_h + start, step, step)
            total = part[s, at].astype(F32) + part_in[s, at_h].astype(F32)
            half_out[o, at_h] = total.astype(BF16)

        loop_rows(rows_h, ROW_STEP, add_half)
        link(link_kind, k).start()

    def sum_far(kind, link_kind, k):
        s = PART_SLOT[kind]
        o = ("out", "ngrad0").index(link_kind)
        core(kind, k).wait_recv()

        def add_far(start, step):
            at = rows_at(k * rows_m + half + (1 - x) * rows_o + start, step, step)
            at_h = rows_at(k * rows_h + (1 - x) * rows_o + start, step, step)
            at_o = rows_at(k * rows_o + start, step, step)
            total = part[s, at].astype(F32) + part_in[s, at_h].astype(F32)
            own_out[o, at_o] = total.astype(BF16)

        loop_rows(rows_o, ROW_STEP, add_far)
        if link_kind in BLOCK_KINDS:
            for m in reversed(order[k]):
                link(link_kind, m).start()
        else:
            link(link_kind, k).start()

    def sum_own(s, o, k, start, step):
        at = rows_at(k * rows_m + own + start, step, step)
        at_h = rows_at(k * rows_h + x * rows_o + start, step, step)
        at_o = rows_at(k * rows_o + start, step, step)
        mine = part[s, at].astype(F32) + part_in[s, at_h].astype(F32)
        return mine + own_in[o, at_o].astype(F32)

    def make_h(k):
        link("sum0", k).wait_recv()
        shift = down_bias_ref[0:1].astype(F32)

        def add_h(start, step):
            at = rows_at(k * rows_m + half + start, step, step)
            at_h = rows_at(k * rows_h + start, step, step)
            total = half_out[0, at_h].astype(F32) + half_in[0, at_h].astype(F32)
            ha[at] = (xa[at].astype(F32) + total + shift).astype(BF16)

        loop_rows(rows_h, ROW_STEP, add_h)
        core("h", k).start()

    def norm_back(rows, ngrad, gain):
        rhat, scale = normalize(rows)
        q = ngrad * gain
        back = scale * (
            q - jnp.mean(q, axis=-1, keepdims=True) - rhat * jnp.mean(q * rhat, axis=-1, keepdims=True)
        )
        return back, rhat

    def make_hgrad(k):
        link("ngrad1", k).wait_recv()
        gain = gain_ref[1:2].astype(F32)

        def grad_h(start, step):
            at = rows_at(k * rows_m + half + start, step, step)
            at_h = rows_at(k * rows_h + start, step, step)
            ngrad = half_out[1, at_h].astype(F32) + half_in[1, at_h].astype(F32)
            back, rhat = norm_back(ha[at].astype(F32), ngrad, gain)
            hga[at] = (ga[at].astype(F32) + back).astype(BF16)
            acc[0:1] += 0.5 * jnp.sum(ngrad * rhat, axis=0, keepdims=True)
            acc[1:2] += 0.5 * jnp.sum(ngrad, axis=0, keepdims=True)

        loop_tiles(rows_h, ROW_STEP, grad_h)
        core("hgrad", k).start()

    def give_back(kind, m):
        if m:
            route(kind, m).start()
        else:
            s = 0 if kind == "mixed" else 1
            back_in[s, mine] = back_out[s, at_own_block(0)]

    def make_mixed(k):
        link("out", k).wait_recv()
        shift = down_bias_ref[1:2].astype(F32)

        def mix(start, step):
            at = rows_at(k * rows_m + own + start, step, step)
            at_o = rows_at(k * rows_o + start, step, step)
            out = (ha[at].astype(F32) + sum_own(0, 0, k, start, step) + shift).astype(BF16).astype(F32)
            rows = xa[at].astype(F32)
            gate = gate_s[at_o][:, 0:1]
            back_out[0, at_o] = (rows + gate * out).astype(BF16)
            along = jnp.sum(ct_own[at_o].astype(F32) * out, axis=-1, keepdims=True)
            lgrad = (along * gate * (1.0 - gate)).astype(BF16).astype(F32)
            lg_s[at_o] = jnp.broadcast_to(lgrad, (step, 128))
            acc[2:3] += jnp.sum(lgrad * rows, axis=0, keepdims=True)

        loop_rows(rows_o, ROW_STEP, mix)
        for m in reversed(order[k]):
            give_back("mixed", m)

    def norm_sums(k):
        def sum_rows(start, step):
            at = rows_at(k * rows_m + half + start, step, step)
            at_h = rows_at(k * rows_h + start, step, step)
            ngrad = part[1, at].astype(F32) + part_in[1, at_h].astype(F32)
            rhat, _ = normalize(xa[at].astype(F32))
            acc_0[0:1] += jnp.sum(ngrad * rhat, axis=0, keepdims=True)
            acc_0[1:2] += jnp.sum(ngrad, axis=0, keepdims=True)

        loop_tiles(rows_h, ROW_STEP, sum_rows)

    def make_tgrad(m):
        link("ngrad0", m).wait_recv()
        k, i = place[m]
        at_o = at_own_block(m)
        at = at_block(m)
        ngrad = sum_own(1, 1, k, i * capacity, capacity)
        back, _ = norm_back(xa[at].astype(F32), ngrad, gain_ref[0:1].astype(F32))
        back = (hga[at].astype(F32) + back).astype(BF16).astype(F32)
        back_out[1, at_o] = (
            ct_own[at_o].astype(F32) + lg_s[at_o][:, 0:1] * cent_s[0:1] + back
        ).astype(BF16)
        give_back("tgrad", m)

    def column_sums(rows_ref):
        def one(i, total):
            values = rows_ref[rows_at(i * ROW_STEP, ROW_STEP, ROW_STEP)].astype(F32)
            return total + jnp.sum(values, axis=0, keepdims=True)

        return lax.fori_loop(
            0, rows_ref.shape[0] // ROW_STEP, one, jnp.zeros((1, rows_ref.shape[1]), F32)
        )

    def weight_grad(q):
        into, left, right = ((down_grad_ref, a_1, ga), (up_grad_ref, n_1, d_1))[q // 2]
        if q == 0:
            small_ref[4:5] = column_sums(right)
        if q == 2:
            small_ref[5:6] = column_sums(right)
        count = left.shape[1] // 2

        def tile(start, step):
            at = rows_at(q % 2 * count + start, step, step)
            into[at] = dot(left[:, at], right[...], TN).astype(BF16)

        loop_tiles(count, COL_STEP, tile)

    lanes = width // 128
    red_rows = (3 * lanes + 8, 2 * lanes)

    def over(s):
        at = pl.ds(0, red_rows[s])
        return copy_to(
            sib, red.at[s, 0, at], red.at[s, 1, at], red_send.at[s, 0], red_recv.at[s, 0]
        )

    def across(s):
        at = pl.ds(0, red_rows[s])
        return copy_to(
            far, red.at[s, 0, at], red.at[s, 2, at], red_send.at[s, 1], red_recv.at[s, 1]
        )

    def total(s, step):
        rows_ref = (acc, acc_0)[s]
        if step == 0:
            for r in range(3 - s):
                for i in range(lanes):
                    red[s, 0, r * lanes + i : r * lanes + i + 1] = rows_ref[
                        r : r + 1, i * 128 : (i + 1) * 128
                    ]
            if s == 0:
                red[s, 0, 3 * lanes : 3 * lanes + 2] = rows_ref[3:5, 0:128]
            over(s).start()
        elif step == 1:
            over(s).wait()
            red[s, 0] = red[s, 0] + red[s, 1]
            across(s).start()
        else:
            across(s).wait()
            sums = red[s, 0] + red[s, 2]
            for r in range(2):
                for i in range(lanes):
                    small_ref[2 * r + 1 - s : 2 * r + 2 - s, i * 128 : (i + 1) * 128] = sums[
                        r * lanes + i : r * lanes + i + 1
                    ]
            if s == 0:
                totals_in[e, 0 : lanes + 2] = sums[2 * lanes : 3 * lanes + 2]
                for m in others:
                    route("totals", m).start()

    def unpack(s):
        kind, out_ref = (("mixed", mixed_ref), ("tgrad", tgrad_ref))[s]
        for m in others:
            route(kind, m).wait_recv()

        def place_tokens(start, step):
            cols = rows_at(start, step, step)
            out_ref[:, cols] = dot(perm[...], back_in[s, :, cols], TN).astype(BF16)

        loop_rows(width, COL_STEP, place_tokens)

    steps = range(chunks)

    def up_0(k):
        if k == first_use[0]:
            loads[0].wait()
        core("x", k).wait_recv()
        up_step(0, xa, k)

    def down_0(k):
        if k == first_use[2]:
            loads[1].wait()
        down_step(0, k)

    def up_1(k):
        if k == first_use[1]:
            loads[2].wait()
            loads[3].wait()
        core("h", k).wait_recv()
        up_step(1, ha, k)

    def back_1(k):
        core("g", k).wait_recv()
        back_step(1, ga, k)

    def back_0(k):
        core("hgrad", k).wait_recv()
        hg_0[at_all(k)] = hga[at_all(k)]
        back_step(0, hga, k)

    tasks = {
        "RX": lambda m: route("x", m).start(),
        "PC": prepare_cotangent,
        "RC": lambda m: route("ct", m).start(),
        "SX": send_x,
        "SG": send_g,
        "PX": functools.partial(spread, "x"),
        "PG": functools.partial(spread, "g"),
        "U0": up_0,
        "D0": down_0,
        "S0": functools.partial(sum_half, "part0", "sum0"),
        "H": make_h,
        "U1": up_1,
        "B1": back_1,
        "D1": functools.partial(down_step, 1),
        "S1": functools.partial(sum_half, "ngrad1", "ngrad1"),
        "SO": functools.partial(sum_far, "part1", "out"),
        "HG": make_hgrad,
        "MX": make_mixed,
        "B0": back_0,
        "SQ": functools.partial(sum_far, "ngrad0", "ngrad0"),
        "GS": norm_sums,
        "TG": make_tgrad,
        "W1": weight_grad,
        "R1": functools.partial(total, 0),
        "R0": functools.partial(total, 1),
        "UP": unpack,
    }
    plan = [word.split(".") for line in SCHEDULE for word in line.split()]
    first_use = [next(int(k) for name, k in plan if name == u) for u in ("U0", "U1", "D0")]
    for name, k in plan:
        tasks[name](int(k))

    for m in others:
        route("totals", m).wait_recv()
    totals_ref[...] = totals_in[...]
    for m in others:
        for kind in ROUTE_KINDS:
            route(kind, m).wait_send()
    for m in range(groups):
        for kind in BLOCK_KINDS:
            link(kind, m).wait_send()
    for k in steps:
        for kind in LINK_KINDS[len(BLOCK_KINDS) :]:
            link(kind, k).wait_send()
        for kind in CORE_KINDS:
            if kind not in ("part0", "ngrad1"):
                core(kind, k).wait_send()


def widen_kernel(
    denominator,
    mixed_ref,
    tgrad_ref,
    totals_ref,
    small_ref,
    up_ref,
    down_ref,
    n_0,
    a_0,
    d_0,
    hg_0,
    mixed_out,
    tgrad_out,
    cent_out,
    gain_out,
    shift_out,
    up_out,
    ub_out,
    down_out,
    db_out,
    mass_out,
    load_out,
    cent_s,
    rows_s,
    vec_s,
    up_wide,
    down_wide,
    sem,
    up_sem,
    down_sem,
):
    leaving = []

    def leave(src, dst, semaphore):
        move = pltpu.make_async_copy(src, dst, semaphore)
        move.start()
        leaving.append(move)

    def widen(ref, wide, dst, semaphore, t):
        at = pl.ds(t * COL_STEP, COL_STEP)
        wide[1, at] = ref[at].astype(F32)
        leave(wide.at[1, at], dst.at[1, 0, at], semaphore.at[1, t])

    def multiply(left, right, wide, dst, semaphore, t):
        at = pl.ds(t * COL_STEP, COL_STEP)
        wide[0, at] = dot(left[:, at], right[...], TN)
        leave(wide.at[0, at], dst.at[0, 0, at], semaphore.at[0, t])

    leave(mixed_ref, mixed_out, sem.at[0])
    leave(tgrad_ref, tgrad_out, sem.at[1])
    for t in range(down_wide.shape[1] // COL_STEP):
        widen(down_ref, down_wide, down_out, down_sem, t)
        multiply(a_0, hg_0, down_wide, down_out, down_sem, t)
    for t in range(up_wide.shape[1] // COL_STEP):
        widen(up_ref, up_wide, up_out, up_sem, t)
        multiply(n_0, d_0, up_wide, up_out, up_sem, t)

    def column_sums(ref):
        return jnp.sum(ref[...].astype(F32), axis=0, keepdims=True)

    for i in range(cent_s.shape[1] // 128):
        cent_s[:, i * 128 : (i + 1) * 128] = totals_ref[:, i]
    leave(cent_s, cent_out, sem.at[2])
    for j in range(2):
        rows_s[0, j] = small_ref[j : j + 1]
        rows_s[1, j] = small_ref[2 + j : 3 + j]
    rows_s[2, 0] = column_sums(d_0)
    rows_s[2, 1] = small_ref[5:6]
    rows_s[3, 0] = column_sums(hg_0)
    rows_s[3, 1] = small_ref[4:5]
    for n, dst in enumerate((gain_out, shift_out, ub_out, db_out)):
        leave(rows_s.at[n], dst, sem.at[3 + n])
    experts = totals_ref.shape[0]
    diagonal = lax.broadcasted_iota(jnp.int32, (experts, 128), 0) == lax.broadcasted_iota(
        jnp.int32, (experts, 128), 1
    )
    for i, (dst, n) in enumerate(((mass_out, 8), (load_out, 9))):
        values = jnp.sum(jnp.where(diagonal, totals_ref[:, n], 0.0), axis=0)
        vec_s[i, 0:experts] = values[0:experts] / jnp.float32(denominator)
        leave(vec_s.at[i], dst, sem.at[7 + i])
    for move in leaving:
        move.wait()


def per_device_fused(
    tokens,
    lengths,
    expert_ids,
    slots,
    centroids,
    sublayer_norm_gain,
    sublayer_norm_bias,
    up_weight,
    up_bias,
    down_weight,
    down_bias,
    cotangent,
):
    if not fused_fits(tokens, centroids, up_weight):
        return per_device(
            tokens,
            lengths,
            expert_ids,
            slots,
            centroids,
            sublayer_norm_gain,
            sublayer_norm_bias,
            up_weight,
            up_bias,
            down_weight,
            down_bias,
            cotangent,
        )
    tok_rows, width = tokens.shape
    groups = lax.axis_size("expert")
    batches = lax.axis_size("batch")
    experts = centroids.shape[0]
    capacity = tok_rows // experts
    hidden = up_weight.shape[3]
    chunks = 4
    total = groups * batches * capacity
    def flat(values):
        return values.reshape(values.shape[0], -1)

    vmem = pl.BlockSpec(memory_space=pltpu.VMEM)
    hbm = pl.BlockSpec(memory_space=pl.ANY)
    outs = pl.pallas_call(
        functools.partial(fused_kernel, groups, capacity, chunks),
        out_shape=[
            pltpu.VMEM((tok_rows, width), BF16),
            pltpu.VMEM((tok_rows, width), BF16),
            pltpu.VMEM((groups, 16, 128), F32),
            pltpu.VMEM((8, width), F32),
            pltpu.VMEM(up_weight.shape[2:], BF16),
            pltpu.VMEM(down_weight.shape[2:], BF16),
            pltpu.VMEM((total, width), BF16),
            pltpu.VMEM((total, hidden), BF16),
            pltpu.VMEM((total, hidden), BF16),
            pltpu.VMEM((total, width), BF16),
        ],
        in_specs=[pl.BlockSpec(memory_space=pltpu.HBM)] * 11,
        out_specs=[vmem] * 10,
        scratch_shapes=[
            pltpu.VMEM((1, tok_rows), jnp.int32),
            pltpu.VMEM((1, tok_rows), jnp.int32),
            pltpu.VMEM((tok_rows, width), BF16),
            pltpu.VMEM((tok_rows, width), BF16),
            pltpu.VMEM((experts, width), BF16),
            pltpu.VMEM((2, width), BF16),
            pltpu.VMEM((2, width), BF16),
            pltpu.VMEM((2, hidden), BF16),
            pltpu.VMEM((2, width), BF16),
            pltpu.VMEM((2, width, hidden), BF16),
            pltpu.VMEM((2, hidden, width), BF16),
            pltpu.VMEM((tok_rows, tok_rows), BF16),
            pltpu.VMEM((tok_rows, width), BF16),
            pltpu.VMEM((tok_rows, width), BF16),
            pltpu.VMEM((total, width), BF16),
            pltpu.VMEM((total, width), BF16),
            pltpu.VMEM((total, width), BF16),
            pltpu.VMEM((total, width), BF16),
            pltpu.VMEM((total, width), BF16),
            pltpu.VMEM((total, hidden), BF16),
            pltpu.VMEM((total, hidden), BF16),
            pltpu.VMEM((2, total, width), BF16),
            pltpu.VMEM((2, total // 2, width), BF16),
            pltpu.VMEM((2, total // 2, width), BF16),
            pltpu.VMEM((2, total // 2, width), BF16),
            pltpu.VMEM((2, total // 4, width), BF16),
            pltpu.VMEM((2, total // 4, width), BF16),
            pltpu.VMEM((tok_rows, width), BF16),
            pltpu.VMEM((tok_rows, 128), F32),
            pltpu.VMEM((tok_rows, 128), F32),
            pltpu.VMEM((2, tok_rows, width), BF16),
            pltpu.VMEM((2, tok_rows, width), BF16),
            pltpu.VMEM((8, width), F32),
            pltpu.VMEM((8, width), F32),
            pltpu.VMEM((8, width), F32),
            pltpu.VMEM((2, 3, 3 * width // 128 + 8, 128), F32),
            pltpu.VMEM((groups, 16, 128), F32),
            pltpu.SemaphoreType.DMA((9,)),
            pltpu.SemaphoreType.DMA((4,)),
            pltpu.SemaphoreType.DMA((len(ROUTE_KINDS), groups)),
            pltpu.SemaphoreType.DMA((len(ROUTE_KINDS), groups)),
            pltpu.SemaphoreType.DMA((len(LINK_KINDS), groups)),
            pltpu.SemaphoreType.DMA((len(LINK_KINDS), groups)),
            pltpu.SemaphoreType.DMA((len(CORE_KINDS), chunks)),
            pltpu.SemaphoreType.DMA((len(CORE_KINDS), chunks)),
            pltpu.SemaphoreType.DMA((2, 2)),
            pltpu.SemaphoreType.DMA((2, 2)),
        ],
        compiler_params=pltpu.CompilerParams(
            collective_id=0, has_side_effects=True, vmem_limit_bytes=46 << 20
        ),
        cost_estimate=pl.CostEstimate(
            flops=24 * total * width * hidden, bytes_accessed=40 << 20, transcendentals=0
        ),
    )(
        expert_ids.reshape(1, tok_rows),
        slots.reshape(1, tok_rows),
        tokens,
        cotangent,
        centroids,
        flat(sublayer_norm_gain),
        flat(sublayer_norm_bias),
        flat(up_bias),
        flat(down_bias),
        up_weight,
        down_weight,
    )
    layers = up_weight.shape[0]
    row = jax.ShapeDtypeStruct((layers, 1, width), F32)
    return pl.pallas_call(
        functools.partial(widen_kernel, capacity * groups * batches),
        out_shape=[
            jax.ShapeDtypeStruct(tokens.shape, BF16),
            jax.ShapeDtypeStruct(tokens.shape, BF16),
            jax.ShapeDtypeStruct((experts, width), F32),
            row,
            row,
            jax.ShapeDtypeStruct(up_weight.shape, F32),
            jax.ShapeDtypeStruct((layers, 1, hidden), F32),
            jax.ShapeDtypeStruct(down_weight.shape, F32),
            row,
            jax.ShapeDtypeStruct((experts,), F32),
            jax.ShapeDtypeStruct((experts,), F32),
        ],
        in_specs=[vmem] * 10,
        out_specs=[hbm] * 11,
        scratch_shapes=[
            pltpu.VMEM((experts, width), F32),
            pltpu.VMEM((4, layers, 1, width), F32),
            pltpu.VMEM((2, experts), F32),
            pltpu.VMEM((layers, width, hidden), F32),
            pltpu.VMEM((layers, hidden, width), F32),
            pltpu.SemaphoreType.DMA((9,)),
            pltpu.SemaphoreType.DMA((layers, width // COL_STEP)),
            pltpu.SemaphoreType.DMA((layers, hidden // COL_STEP)),
        ],
        compiler_params=pltpu.CompilerParams(vmem_limit_bytes=24 << 20),
        cost_estimate=pl.CostEstimate(
            flops=0, bytes_accessed=12 * layers * width * hidden, transcendentals=0
        ),
    )(*(pltpu.with_memory_space_constraint(out, pltpu.VMEM) for out in outs))


def solution(mesh):
    in_specs = (
        P(("expert", "batch"), None),
        P(("expert", "batch")),
        P(("expert", "batch")),
        P(("expert", "batch")),
        P(),
        P(None, "expert", None),
        P(None, "expert", None),
        P(None, "expert", None, "batch"),
        P(None, "expert", "batch"),
        P(None, "expert", "batch", None),
        P(None, "expert", None),
        P(("expert", "batch"), None),
    )
    out_specs = (
        P(("expert", "batch"), None),
        P(("expert", "batch"), None),
        P(),
        P(None, "expert", None),
        P(None, "expert", None),
        P(None, "expert", None, "batch"),
        P(None, "expert", "batch"),
        P(None, "expert", "batch", None),
        P(None, "expert", None),
        P(),
        P(),
    )
    return jax.shard_map(
        per_device_fused, mesh=mesh, in_specs=in_specs, out_specs=out_specs, check_vma=False
    )
```

```python
import functools

import jax
import jax.numpy as jnp
from jax import lax
from jax.experimental import pallas as pl
from jax.experimental.pallas import tpu as pltpu
from jax.sharding import PartitionSpec as P


def gelu_exact(values):
    return jax.nn.gelu(values, approximate=False)


def apply_layer_norm(row_block):
    values = row_block.astype(jnp.float32)
    row_mean = jnp.mean(values, axis=-1, keepdims=True)
    centered = values - row_mean
    row_inverse_scale = lax.rsqrt(jnp.mean(centered * centered, axis=-1, keepdims=True) + 1e-05)
    return (centered * row_inverse_scale, row_inverse_scale)


def per_device(
    tokens,
    lengths,
    expert_ids,
    slots,
    centroids,
    sublayer_norm_gain,
    sublayer_norm_bias,
    up_weight,
    up_bias,
    down_weight,
    down_bias,
    cotangent,
):
    tok_rows, width = tokens.shape
    layers = sublayer_norm_gain.shape[0]
    local_count = up_weight.shape[1]
    expert_count = centroids.shape[0]
    capacity = tok_rows // expert_count
    groups = lax.axis_size("expert")
    batches = lax.axis_size("batch")
    position = jnp.arange(tok_rows, dtype=jnp.int32)
    live = (position < lengths[0]).astype(jnp.float32)[:, None]
    target = jnp.where(slots >= 0, expert_ids * capacity + slots, tok_rows)
    source = jnp.full((tok_rows + 1,), -1, jnp.int32).at[target].set(position)[:tok_rows]
    filled = (source >= 0)[:, None]
    safe_source = jnp.maximum(source, 0)
    safe_target = jnp.minimum(target, tok_rows - 1)

    def pack(values):
        return jnp.where(filled, values[safe_source], jnp.zeros((), values.dtype))

    onehot = (expert_ids[:, None] == jnp.arange(expert_count, dtype=jnp.int32)[None, :]).astype(
        jnp.float32
    )
    logits = jnp.einsum("td,ed->te", tokens, centroids, preferred_element_type=jnp.float32)
    gate = jax.nn.sigmoid(jnp.sum(logits * onehot, axis=1))[:, None]
    used = onehot * live
    usage_gate = jnp.sum(used * gate, axis=0)
    usage_count = jnp.sum(used, axis=0)
    gate_total, count_total = lax.psum((usage_gate, usage_count), ("expert", "batch"))

    def expand_hidden(values, expert_layer_step):
        return values[expert_layer_step].astype(jnp.float32)[None, :, None, :]

    arrived = lax.all_to_all(pack(tokens), "expert", split_axis=0, concat_axis=0, tiled=True)
    current = arrived
    inputs = []
    kept = []
    for expert_layer_step in range(layers):
        gathered = lax.all_gather(current, "batch", axis=0, tiled=True)
        row_layout_grid = gathered.reshape(-1, local_count, capacity, width)
        standardized_input, row_inverse_scale = apply_layer_norm(row_layout_grid)
        normalized_rows = (
            standardized_input * expand_hidden(sublayer_norm_gain, expert_layer_step)
            + expand_hidden(sublayer_norm_bias, expert_layer_step)
        ).astype(jnp.bfloat16)
        pre_rows = jnp.einsum(
            "nlcd,ldf->nlcf",
            normalized_rows,
            up_weight[expert_layer_step],
            preferred_element_type=jnp.float32,
        ) + expand_hidden(up_bias, expert_layer_step)
        hidden_parts = (normalized_rows, pre_rows, gelu_exact(pre_rows).astype(jnp.bfloat16))

        def down_part(start, count, activity=hidden_parts[2], expert_layer_step=expert_layer_step):
            return jnp.einsum(
                "nlcf,lfd->nlcd",
                activity,
                down_weight[expert_layer_step],
                preferred_element_type=jnp.float32,
            )

        mixed_part = lax.psum_scatter(
            down_part(jnp.int32(0), lax.axis_size("batch") * groups).astype(jnp.bfloat16),
            "batch",
            scatter_dimension=0,
            tiled=True,
        ).astype(jnp.float32)
        own_grid = current.reshape(groups, local_count, capacity, width).astype(jnp.float32)
        result = (own_grid + mixed_part + expand_hidden(down_bias, expert_layer_step)).astype(
            jnp.bfloat16
        )
        inputs.append(current)
        kept.append(hidden_parts)
        current = result.reshape(tok_rows, width)
    returned = lax.all_to_all(current, "expert", split_axis=0, concat_axis=0, tiled=True)
    expert_tok = returned[safe_target].astype(jnp.float32)
    mixed = (live * (tokens.astype(jnp.float32) + gate * expert_tok)).astype(jnp.bfloat16)
    upstream = cotangent.astype(jnp.float32) * live
    gate_grad = jnp.sum(upstream * expert_tok, axis=1, keepdims=True)
    logit_grad = (gate_grad * gate * (1.0 - gate)).astype(jnp.bfloat16)
    route_grad = (onehot * logit_grad.astype(jnp.float32)).astype(jnp.bfloat16)
    centroid_part = jnp.einsum("te,td->ed", route_grad, tokens, preferred_element_type=jnp.float32)
    gate_input = jnp.einsum("te,ed->td", route_grad, centroids, preferred_element_type=jnp.float32)
    expert_grad = (gate * upstream).astype(jnp.bfloat16)
    grad_rows = lax.all_to_all(pack(expert_grad), "expert", split_axis=0, concat_axis=0, tiled=True)
    gain_parts = [None] * layers
    shift_parts = [None] * layers
    down_bias_parts = [None] * layers
    up_weight_grads = [None] * layers
    up_bias_grads = [None] * layers
    down_weight_grads = [None] * layers
    for expert_layer_step in range(layers - 1, -1, -1):
        own_rows = inputs[expert_layer_step]
        grads_all = lax.all_gather(grad_rows, "batch", axis=0, tiled=True).reshape(
            -1, local_count, capacity, width
        )
        normed, pre_act, activity = kept[expert_layer_step]
        act_grad = jnp.einsum(
            "nlcd,lfd->nlcf",
            grads_all,
            down_weight[expert_layer_step],
            preferred_element_type=jnp.float32,
        )
        pre_grad = jax.vjp(gelu_exact, pre_act)[1](act_grad)[0].astype(jnp.bfloat16)
        down_weight_grads[expert_layer_step] = jnp.einsum(
            "nlcf,nlcd->lfd", activity, grads_all, preferred_element_type=jnp.float32
        )
        up_weight_grads[expert_layer_step] = jnp.einsum(
            "nlcd,nlcf->ldf", normed, pre_grad, preferred_element_type=jnp.float32
        )
        up_bias_grads[expert_layer_step] = jnp.sum(pre_grad.astype(jnp.float32), axis=(0, 2))

        def up_part(start, count, pre_grad=pre_grad, expert_layer_step=expert_layer_step):
            return jnp.einsum(
                "nlcf,ldf->nlcd",
                pre_grad,
                up_weight[expert_layer_step],
                preferred_element_type=jnp.float32,
            )

        normed_grad = lax.psum_scatter(
            up_part(jnp.int32(0), lax.axis_size("batch") * groups).astype(jnp.bfloat16),
            "batch",
            scatter_dimension=0,
            tiled=True,
        ).astype(jnp.float32)
        out_grad = grad_rows.reshape(groups, local_count, capacity, width).astype(jnp.float32)
        down_bias_parts[expert_layer_step] = jnp.sum(out_grad, axis=(0, 2))
        own_hat, own_scale = apply_layer_norm(
            own_rows.reshape(groups, local_count, capacity, width)
        )
        gain_parts[expert_layer_step] = jnp.sum(normed_grad * own_hat, axis=(0, 2))
        shift_parts[expert_layer_step] = jnp.sum(normed_grad, axis=(0, 2))
        hat_grad = normed_grad * expand_hidden(sublayer_norm_gain, expert_layer_step)
        row_grad = own_scale * (
            hat_grad
            - jnp.mean(hat_grad, axis=-1, keepdims=True)
            - own_hat * jnp.mean(hat_grad * own_hat, axis=-1, keepdims=True)
        )
        grad_rows = (out_grad + row_grad).astype(jnp.bfloat16).reshape(tok_rows, width)
    gain_grad, shift_grad, down_bias_grad = lax.psum(
        (jnp.stack(gain_parts), jnp.stack(shift_parts), jnp.stack(down_bias_parts)), "batch"
    )
    token_back = lax.all_to_all(grad_rows, "expert", split_axis=0, concat_axis=0, tiled=True)
    tokens_grad = (
        upstream + gate_input + live * token_back[safe_target].astype(jnp.float32)
    ).astype(jnp.bfloat16)
    centroid_grad = lax.psum(centroid_part, ("expert", "batch"))
    denominator = jnp.float32(capacity * groups * batches)
    gate_mass = gate_total / denominator
    load = count_total / denominator
    return (
        mixed,
        tokens_grad,
        centroid_grad,
        gain_grad,
        shift_grad,
        jnp.stack(up_weight_grads),
        jnp.stack(up_bias_grads),
        jnp.stack(down_weight_grads),
        down_bias_grad,
        gate_mass,
        load,
    )


MESH = pl.DeviceIdType.MESH
F32 = jnp.float32
BF16 = jnp.bfloat16
ROW_STEP = 64
COL_STEP = 256
EMPTY = 8.0
BLOCK_KINDS = ("x", "g", "ngrad0")
LINK_KINDS = BLOCK_KINDS + ("sum0", "out", "ngrad1")
CORE_KINDS = ("x", "g", "part0", "h", "part1", "ngrad1", "hgrad", "ngrad0")
SCHEDULE = (
    "RX.1 RX.2 RX.3 RX.4",
    "RX.5 RX.6 RX.7 SX.0",
    "PC.0 RC.1 RC.2 RC.3",
    "RC.4 RC.5 RC.6 RC.7",
    "SG.0 SX.1 SX.2 SX.3",
    "SX.4 SX.5 PX.3 PX.0",
    "SG.2 SX.6 SG.1 U0.0",
    "PX.1 D0.0 SX.7 SG.3",
    "U0.1 S0.0 U0.3 D0.1",
    "PX.2 S0.1 U0.2 SG.5",
    "SG.4 H.0 D0.2 D0.3",
    "SG.7 S0.3 H.1 S0.2",
    "U1.1 SG.6 PG.0 D1.1",
    "U1.0 SO.1 PG.1 H.3",
    "B1.1 D1.0 B1.0 H.2",
    "S1.1 U1.2 S1.0 PG.3",
    "PG.2 U1.3 D1.2 B1.2",
    "HG.1 S1.2 B1.3 MX.1",
    "B0.1 W1.3 SO.2 HG.0",
    "SQ.1 B0.0 S1.3 HG.2",
    "D1.3 SO.0 GS.1 TG.5",
    "B0.2 SO.3 TG.4 W1.0",
    "MX.2 SQ.2 GS.2 HG.3",
    "W1.2 SQ.0 B0.3 MX.0",
    "MX.3 R1.0 TG.7 GS.0",
    "TG.6 R1.1 SQ.3 GS.3",
    "R0.0 TG.3 R0.1 R1.2",
    "TG.2 TG.1 W1.1 TG.0",
    "UP.0 R0.2 UP.1",
)
PART_SLOT = {"part0": 0, "part1": 0, "ngrad1": 1, "ngrad0": 1}
ROUTE_KINDS = ("x", "ct", "mixed", "tgrad", "totals")


def fused_fits(tokens, centroids, up_weight):
    tok_rows, width = tokens.shape
    groups, capacity = lax.axis_size("expert"), tok_rows // centroids.shape[0]
    return (
        lax.axis_size("batch") == 4
        and groups == 8
        and up_weight.shape[:2] == (2, 1)
        and centroids.shape[0] == groups
        and up_weight.shape[3] == width
        and width % (4 * COL_STEP) == 0
        and capacity % 32 == 0
    )


def rows_at(start, count, unit):
    return pl.ds(pl.multiple_of(start, unit), count)


def loop_rows(count, step, body):
    step = min(step, count)
    for start in range(0, count, step):
        body(start, step)


def loop_tiles(count, step, body):
    def one(i, carry):
        body(pl.multiple_of(i * step, step), step)
        return carry

    lax.fori_loop(0, count // step, one, 0)


def normalize(values):
    centered = values - jnp.mean(values, axis=-1, keepdims=True)
    scale = lax.rsqrt(jnp.mean(centered * centered, axis=-1, keepdims=True) + 1e-05)
    return centered * scale, scale


def dot(a, b, dims):
    return lax.dot_general(a, b, (dims, ((), ())), preferred_element_type=F32)


NN = ((1,), (0,))
NT = ((1,), (1,))
TN = ((0,), (0,))


def fused_kernel(
    groups,
    capacity,
    chunks,
    ids_hbm,
    slots_hbm,
    tok_hbm,
    ct_hbm,
    cent_hbm,
    gain_hbm,
    bias_hbm,
    up_bias_hbm,
    down_bias_hbm,
    up_hbm,
    down_hbm,
    mixed_ref,
    tgrad_ref,
    totals_ref,
    small_ref,
    up_grad_ref,
    down_grad_ref,
    n_0,
    a_0,
    d_0,
    hg_0,
    ids_ref,
    slots_ref,
    tok_ref,
    ct_ref,
    cent_ref,
    gain_ref,
    bias_ref,
    up_bias_ref,
    down_bias_ref,
    up_w,
    down_w,
    perm,
    pack_x,
    pack_ct,
    xa,
    ga,
    ha,
    hga,
    n_1,
    a_1,
    d_1,
    part,
    part_in,
    half_out,
    half_in,
    own_out,
    own_in,
    ct_own,
    gate_s,
    lg_s,
    back_out,
    back_in,
    acc,
    acc_0,
    cent_s,
    red,
    totals_in,
    in_sem,
    w_sem,
    route_send,
    route_recv,
    link_send,
    link_recv,
    core_send,
    core_recv,
    red_send,
    red_recv,
):
    tok_rows, width = tok_ref.shape
    hidden = up_w.shape[2]
    n_s, a_s, d_s = (n_0, n_1), (a_0, a_1), (d_0, d_1)
    per = groups // chunks
    rows_m = per * 4 * capacity
    rows_h = rows_m // 2
    rows_o = rows_m // 4
    e = lax.axis_index("expert")
    b = lax.axis_index("batch")
    x = b // 2
    c = lax.rem(b, 2)
    sib = (e, x * 2 + (1 - c))
    far = (e, (1 - x) * 2 + c)

    def flipped(m):
        out = jnp.int32(0)
        bit = 1
        while bit < groups:
            digit = lax.rem(e // bit, 2)
            out = out + bit * ((1 - digit) if m & bit else digit)
            bit *= 2
        return out

    half = c * rows_h
    sib_half = (1 - c) * rows_h
    own = half + x * rows_o
    pairs = [tuple(range(j * per, (j + 1) * per)) for j in range(chunks)]
    order = pairs[1:] + pairs[:1]
    place = {m: (k, i) for k, ms in enumerate(order) for i, m in enumerate(ms)}
    others = range(1, groups)

    def at_half(k):
        return rows_at(k * rows_m + half, rows_h, rows_h)

    def at_own_block(m):
        k, i = place[m]
        return pl.ds(k * rows_o + i * capacity, capacity)

    def at_sib_half(k):
        return rows_at(k * rows_m + sib_half, rows_h, rows_h)

    def at_block(m):
        k, i = place[m]
        return rows_at(k * rows_m + own + i * capacity, capacity, capacity)

    def at_all(k):
        return pl.ds(k * rows_m, rows_m)

    def copy_to(device, src, dst, send, recv):
        return pltpu.make_async_remote_copy(
            src_ref=src,
            dst_ref=dst,
            send_sem=send,
            recv_sem=recv,
            device_id=device,
            device_id_type=MESH,
        )

    def route(kind, m):
        n = ROUTE_KINDS.index(kind)
        to = flipped(m)
        theirs = rows_at(to * capacity, capacity, capacity)
        mine = rows_at(e * capacity, capacity, capacity)
        if kind == "x":
            src = pack_x.at[theirs]
            dst = xa.at[at_block(m)]
        elif kind == "ct":
            src = pack_ct.at[theirs]
            dst = ct_own.at[at_own_block(m)]
        elif kind == "totals":
            src = dst = totals_in.at[e]
        else:
            s = 0 if kind == "mixed" else 1
            src = back_out.at[s, at_own_block(m)]
            dst = back_in.at[s, mine]
        return copy_to((to, b), src, dst, route_send.at[n, m], route_recv.at[n, m])

    def link(kind, k):
        n = LINK_KINDS.index(kind)
        if kind in ("x", "g"):
            src = dst = {"x": xa, "g": ga}[kind].at[at_block(k)]
        elif kind in ("sum0", "ngrad1"):
            s = 0 if kind == "sum0" else 1
            at = pl.ds(k * rows_h, rows_h)
            src, dst = half_out.at[s, at], half_in.at[s, at]
        elif kind == "out":
            at = pl.ds(k * rows_o, rows_o)
            src, dst = own_out.at[0, at], own_in.at[0, at]
        else:
            at = at_own_block(k)
            src, dst = own_out.at[1, at], own_in.at[1, at]
        return copy_to(far, src, dst, link_send.at[n, k], link_recv.at[n, k])

    def core(kind, k):
        n = CORE_KINDS.index(kind)
        whole = {"x": xa, "g": ga, "h": ha, "hgrad": hga}
        if kind in whole:
            src = dst = whole[kind].at[at_half(k)]
        else:
            s = PART_SLOT[kind]
            src = part.at[s, at_sib_half(k)]
            dst = part_in.at[s, pl.ds(k * rows_h, rows_h)]
        return copy_to(sib, src, dst, core_send.at[n, k], core_recv.at[n, k])

    barrier = pltpu.get_barrier_semaphore()
    peers = [sib, far] + [(flipped(m), b) for m in range(1, groups)]
    for peer in peers:
        pl.semaphore_signal(barrier, inc=1, device_id=peer, device_id_type=MESH)
    arrivals = [
        pltpu.make_async_copy(src, dst, in_sem.at[n])
        for n, (src, dst) in enumerate(
            (
                (ids_hbm, ids_ref),
                (slots_hbm, slots_ref),
                (tok_hbm, tok_ref),
                (ct_hbm, ct_ref),
                (cent_hbm, cent_ref),
                (gain_hbm, gain_ref),
                (bias_hbm, bias_ref),
                (up_bias_hbm, up_bias_ref),
                (down_bias_hbm, down_bias_ref),
            )
        )
    ]
    loads = []
    for j in range(2):
        loads.append(pltpu.make_async_copy(up_hbm.at[j, 0], up_w.at[j], w_sem.at[2 * j]))
        loads.append(pltpu.make_async_copy(down_hbm.at[j, 0], down_w.at[j], w_sem.at[2 * j + 1]))
    for load in arrivals + loads:
        load.start()
    acc[...] = jnp.zeros_like(acc)
    acc_0[...] = jnp.zeros_like(acc_0)
    red[...] = jnp.zeros_like(red)
    arrivals[0].wait()
    arrivals[1].wait()
    target = jnp.where(
        slots_ref[...] >= 0, ids_ref[...] * capacity + slots_ref[...], -1
    )
    slot = lax.broadcasted_iota(jnp.int32, (tok_rows, tok_rows), 0)
    onehot = jnp.where(slot == target, 1.0, 0.0)
    perm[...] = onehot.astype(BF16)
    empty = EMPTY * (1.0 - jnp.sum(onehot, axis=1, keepdims=True))

    def pack_tokens(start, step):
        cols = rows_at(start, step, step)
        pack_x[:, cols] = (dot(perm[...], tok_ref[:, cols], NN) + empty).astype(BF16)

    def pack_cotangent(start, step):
        cols = rows_at(start, step, step)
        pack_ct[:, cols] = dot(perm[...], ct_ref[:, cols], NN).astype(BF16)

    arrivals[2].wait()
    loop_rows(width, COL_STEP, pack_tokens)
    pl.semaphore_wait(barrier, len(peers))
    mine = rows_at(e * capacity, capacity, capacity)
    xa[at_block(0)] = pack_x[mine]

    def prepare_cotangent(_):
        arrivals[3].wait()
        loop_rows(width, COL_STEP, pack_cotangent)
        ct_own[at_own_block(0)] = pack_ct[mine]
        for arrival in arrivals[4:]:
            arrival.wait()
        cent_rows = cent_ref[...].astype(F32)
        cent_at = lax.broadcasted_iota(jnp.int32, cent_rows.shape, 0)
        cent_s[0:1] = jnp.sum(jnp.where(cent_at == e, cent_rows, 0.0), axis=0, keepdims=True)

    def send_x(m):
        if m:
            route("x", m).wait_recv()
        link("x", m).start()

    def send_g(m):
        if m:
            route("ct", m).wait_recv()
        at_o = at_own_block(m)
        values = xa[at_block(m)].astype(F32)
        gate = jax.nn.sigmoid(jnp.sum(values * cent_s[0:1], axis=-1, keepdims=True))
        gate_s[at_o] = jnp.broadcast_to(gate, (capacity, 128))
        ga[at_block(m)] = (gate * ct_own[at_o].astype(F32)).astype(BF16)
        used = jnp.where(values[:, 0:1] < 7.0, 1.0, 0.0)
        acc[3:4] += jnp.broadcast_to(jnp.sum(used * gate, axis=0, keepdims=True), (1, width))
        acc[4:5] += jnp.broadcast_to(jnp.sum(used, axis=0, keepdims=True), (1, width))
        link("g", m).start()

    def spread(kind, k):
        for m in order[k]:
            link(kind, m).wait_recv()
        core(kind, k).start()

    def up_step(j, rows_ref, k):
        gain = gain_ref[j : j + 1].astype(F32)
        bias = bias_ref[j : j + 1].astype(F32)

        def norm(start, step):
            at = rows_at(k * rows_m + start, step, step)
            rhat, _ = normalize(rows_ref[at].astype(F32))
            n_s[j][at] = (rhat * gain + bias).astype(BF16)

        loop_tiles(rows_m, 2 * ROW_STEP, norm)

        def up(start, step):
            cols = rows_at(start, step, step)
            pre = dot(n_s[j][at_all(k)], up_w[j, :, cols], NN) + up_bias_ref[j : j + 1, cols].astype(
                F32
            )
            cdf = 0.5 * (1.0 + lax.erf(pre * (0.5**0.5)))
            pdf = jnp.exp(-0.5 * pre * pre) * 0.3989422804014327
            a_s[j][at_all(k), cols] = (pre * cdf).astype(BF16)
            d_s[j][at_all(k), cols] = (cdf + pre * pdf).astype(BF16)

        loop_rows(hidden, COL_STEP, up)

    def down_step(j, k):
        kind = "part%d" % j
        if j == 1:
            core("part0", k).wait_send()

        def down(start, step):
            cols = rows_at(start, step, step)
            part[0, at_all(k), cols] = dot(a_s[j][at_all(k)], down_w[j, :, cols], NN).astype(BF16)

        loop_tiles(width, 2 * COL_STEP, down)
        core(kind, k).start()

    def back_step(j, grads_ref, k):
        kind = "ngrad%d" % j
        if j == 0:
            core("ngrad1", k).wait_send()

        def act(start, step):
            cols = rows_at(start, step, step)
            grad = dot(grads_ref[at_all(k)], down_w[j, cols, :], NT)
            d_s[j][at_all(k), cols] = (grad * d_s[j][at_all(k), cols].astype(F32)).astype(BF16)

        loop_tiles(hidden, 2 * COL_STEP, act)

        def up_back(start, step):
            cols = rows_at(start, step, step)
            part[1, at_all(k), cols] = dot(d_s[j][at_all(k)], up_w[j, cols, :], NT).astype(BF16)

        loop_tiles(width, 2 * COL_STEP, up_back)
        core(kind, k).start()

    def sum_half(kind, link_kind, k):
        s = PART_SLOT[kind]
        o = ("sum0", "ngrad1").index(link_kind)
        core(kind, k).wait_recv()

        def add_half(start, step):
            at = rows_at(k * rows_m + half + start, step, step)
            at_h = rows_at(k * rows_h + start, step, step)
            total = part[s, at].astype(F32) + part_in[s, at_h].astype(F32)
            half_out[o, at_h] = total.astype(BF16)

        loop_rows(rows_h, ROW_STEP, add_half)
        link(link_kind, k).start()

    def sum_far(kind, link_kind, k):
        s = PART_SLOT[kind]
        o = ("out", "ngrad0").index(link_kind)
        core(kind, k).wait_recv()

        def add_far(start, step):
            at = rows_at(k * rows_m + half + (1 - x) * rows_o + start, step, step)
            at_h = rows_at(k * rows_h + (1 - x) * rows_o + start, step, step)
            at_o = rows_at(k * rows_o + start, step, step)
            total = part[s, at].astype(F32) + part_in[s, at_h].astype(F32)
            own_out[o, at_o] = total.astype(BF16)

        loop_rows(rows_o, ROW_STEP, add_far)
        if link_kind in BLOCK_KINDS:
            for m in reversed(order[k]):
                link(link_kind, m).start()
        else:
            link(link_kind, k).start()

    def sum_own(s, o, k, start, step):
        at = rows_at(k * rows_m + own + start, step, step)
        at_h = rows_at(k * rows_h + x * rows_o + start, step, step)
        at_o = rows_at(k * rows_o + start, step, step)
        mine = part[s, at].astype(F32) + part_in[s, at_h].astype(F32)
        return mine + own_in[o, at_o].astype(F32)

    def make_h(k):
        link("sum0", k).wait_recv()
        shift = down_bias_ref[0:1].astype(F32)

        def add_h(start, step):
            at = rows_at(k * rows_m + half + start, step, step)
            at_h = rows_at(k * rows_h + start, step, step)
            total = half_out[0, at_h].astype(F32) + half_in[0, at_h].astype(F32)
            ha[at] = (xa[at].astype(F32) + total + shift).astype(BF16)

        loop_rows(rows_h, ROW_STEP, add_h)
        core("h", k).start()

    def norm_back(rows, ngrad, gain):
        rhat, scale = normalize(rows)
        q = ngrad * gain
        back = scale * (
            q - jnp.mean(q, axis=-1, keepdims=True) - rhat * jnp.mean(q * rhat, axis=-1, keepdims=True)
        )
        return back, rhat

    def make_hgrad(k):
        link("ngrad1", k).wait_recv()
        gain = gain_ref[1:2].astype(F32)

        def grad_h(start, step):
            at = rows_at(k * rows_m + half + start, step, step)
            at_h = rows_at(k * rows_h + start, step, step)
            ngrad = half_out[1, at_h].astype(F32) + half_in[1, at_h].astype(F32)
            back, rhat = norm_back(ha[at].astype(F32), ngrad, gain)
            hga[at] = (ga[at].astype(F32) + back).astype(BF16)
            acc[0:1] += 0.5 * jnp.sum(ngrad * rhat, axis=0, keepdims=True)
            acc[1:2] += 0.5 * jnp.sum(ngrad, axis=0, keepdims=True)

        loop_tiles(rows_h, ROW_STEP, grad_h)
        core("hgrad", k).start()

    def give_back(kind, m):
        if m:
            route(kind, m).start()
        else:
            s = 0 if kind == "mixed" else 1
            back_in[s, mine] = back_out[s, at_own_block(0)]

    def make_mixed(k):
        link("out", k).wait_recv()
        shift = down_bias_ref[1:2].astype(F32)

        def mix(start, step):
            at = rows_at(k * rows_m + own + start, step, step)
            at_o = rows_at(k * rows_o + start, step, step)
            out = (ha[at].astype(F32) + sum_own(0, 0, k, start, step) + shift).astype(BF16).astype(F32)
            rows = xa[at].astype(F32)
            gate = gate_s[at_o][:, 0:1]
            back_out[0, at_o] = (rows + gate * out).astype(BF16)
            along = jnp.sum(ct_own[at_o].astype(F32) * out, axis=-1, keepdims=True)
            lgrad = (along * gate * (1.0 - gate)).astype(BF16).astype(F32)
            lg_s[at_o] = jnp.broadcast_to(lgrad, (step, 128))
            acc[2:3] += jnp.sum(lgrad * rows, axis=0, keepdims=True)

        loop_rows(rows_o, ROW_STEP, mix)
        for m in reversed(order[k]):
            give_back("mixed", m)

    def norm_sums(k):
        def sum_rows(start, step):
            at = rows_at(k * rows_m + half + start, step, step)
            at_h = rows_at(k * rows_h + start, step, step)
            ngrad = part[1, at].astype(F32) + part_in[1, at_h].astype(F32)
            rhat, _ = normalize(xa[at].astype(F32))
            acc_0[0:1] += jnp.sum(ngrad * rhat, axis=0, keepdims=True)
            acc_0[1:2] += jnp.sum(ngrad, axis=0, keepdims=True)

        loop_tiles(rows_h, ROW_STEP, sum_rows)

    def make_tgrad(m):
        link("ngrad0", m).wait_recv()
        k, i = place[m]
        at_o = at_own_block(m)
        at = at_block(m)
        ngrad = sum_own(1, 1, k, i * capacity, capacity)
        back, _ = norm_back(xa[at].astype(F32), ngrad, gain_ref[0:1].astype(F32))
        back = (hga[at].astype(F32) + back).astype(BF16).astype(F32)
        back_out[1, at_o] = (
            ct_own[at_o].astype(F32) + lg_s[at_o][:, 0:1] * cent_s[0:1] + back
        ).astype(BF16)
        give_back("tgrad", m)

    def column_sums(rows_ref):
        def one(i, total):
            values = rows_ref[rows_at(i * ROW_STEP, ROW_STEP, ROW_STEP)].astype(F32)
            return total + jnp.sum(values, axis=0, keepdims=True)

        return lax.fori_loop(
            0, rows_ref.shape[0] // ROW_STEP, one, jnp.zeros((1, rows_ref.shape[1]), F32)
        )

    def weight_grad(q):
        into, left, right = ((down_grad_ref, a_1, ga), (up_grad_ref, n_1, d_1))[q // 2]
        if q == 0:
            small_ref[4:5] = column_sums(right)
        if q == 2:
            small_ref[5:6] = column_sums(right)
        count = left.shape[1] // 2

        def tile(start, step):
            at = rows_at(q % 2 * count + start, step, step)
            into[at] = dot(left[:, at], right[...], TN).astype(BF16)

        loop_tiles(count, COL_STEP, tile)

    lanes = width // 128
    red_rows = (3 * lanes + 8, 2 * lanes)

    def over(s):
        at = pl.ds(0, red_rows[s])
        return copy_to(
            sib, red.at[s, 0, at], red.at[s, 1, at], red_send.at[s, 0], red_recv.at[s, 0]
        )

    def across(s):
        at = pl.ds(0, red_rows[s])
        return copy_to(
            far, red.at[s, 0, at], red.at[s, 2, at], red_send.at[s, 1], red_recv.at[s, 1]
        )

    def total(s, step):
        rows_ref = (acc, acc_0)[s]
        if step == 0:
            for r in range(3 - s):
                for i in range(lanes):
                    red[s, 0, r * lanes + i : r * lanes + i + 1] = rows_ref[
                        r : r + 1, i * 128 : (i + 1) * 128
                    ]
            if s == 0:
                red[s, 0, 3 * lanes : 3 * lanes + 2] = rows_ref[3:5, 0:128]
            over(s).start()
        elif step == 1:
            over(s).wait()
            red[s, 0] = red[s, 0] + red[s, 1]
            across(s).start()
        else:
            across(s).wait()
            sums = red[s, 0] + red[s, 2]
            for r in range(2):
                for i in range(lanes):
                    small_ref[2 * r + 1 - s : 2 * r + 2 - s, i * 128 : (i + 1) * 128] = sums[
                        r * lanes + i : r * lanes + i + 1
                    ]
            if s == 0:
                totals_in[e, 0 : lanes + 2] = sums[2 * lanes : 3 * lanes + 2]
                for m in others:
                    route("totals", m).start()

    def unpack(s):
        kind, out_ref = (("mixed", mixed_ref), ("tgrad", tgrad_ref))[s]
        for m in others:
            route(kind, m).wait_recv()

        def place_tokens(start, step):
            cols = rows_at(start, step, step)
            out_ref[:, cols] = dot(perm[...], back_in[s, :, cols], TN).astype(BF16)

        loop_rows(width, COL_STEP, place_tokens)

    steps = range(chunks)

    def up_0(k):
        if k == first_use[0]:
            loads[0].wait()
        core("x", k).wait_recv()
        up_step(0, xa, k)

    def down_0(k):
        if k == first_use[2]:
            loads[1].wait()
        down_step(0, k)

    def up_1(k):
        if k == first_use[1]:
            loads[2].wait()
            loads[3].wait()
        core("h", k).wait_recv()
        up_step(1, ha, k)

    def back_1(k):
        core("g", k).wait_recv()
        back_step(1, ga, k)

    def back_0(k):
        core("hgrad", k).wait_recv()
        hg_0[at_all(k)] = hga[at_all(k)]
        back_step(0, hga, k)

    tasks = {
        "RX": lambda m: route("x", m).start(),
        "PC": prepare_cotangent,
        "RC": lambda m: route("ct", m).start(),
        "SX": send_x,
        "SG": send_g,
        "PX": functools.partial(spread, "x"),
        "PG": functools.partial(spread, "g"),
        "U0": up_0,
        "D0": down_0,
        "S0": functools.partial(sum_half, "part0", "sum0"),
        "H": make_h,
        "U1": up_1,
        "B1": back_1,
        "D1": functools.partial(down_step, 1),
        "S1": functools.partial(sum_half, "ngrad1", "ngrad1"),
        "SO": functools.partial(sum_far, "part1", "out"),
        "HG": make_hgrad,
        "MX": make_mixed,
        "B0": back_0,
        "SQ": functools.partial(sum_far, "ngrad0", "ngrad0"),
        "GS": norm_sums,
        "TG": make_tgrad,
        "W1": weight_grad,
        "R1": functools.partial(total, 0),
        "R0": functools.partial(total, 1),
        "UP": unpack,
    }
    plan = [word.split(".") for line in SCHEDULE for word in line.split()]
    first_use = [next(int(k) for name, k in plan if name == u) for u in ("U0", "U1", "D0")]
    for name, k in plan:
        tasks[name](int(k))

    for m in others:
        route("totals", m).wait_recv()
    totals_ref[...] = totals_in[...]
    for m in others:
        for kind in ROUTE_KINDS:
            route(kind, m).wait_send()
    for m in range(groups):
        for kind in BLOCK_KINDS:
            link(kind, m).wait_send()
    for k in steps:
        for kind in LINK_KINDS[len(BLOCK_KINDS) :]:
            link(kind, k).wait_send()
        for kind in CORE_KINDS:
            if kind not in ("part0", "ngrad1"):
                core(kind, k).wait_send()


def widen_kernel(
    denominator,
    mixed_ref,
    tgrad_ref,
    totals_ref,
    small_ref,
    up_ref,
    down_ref,
    n_0,
    a_0,
    d_0,
    hg_0,
    mixed_out,
    tgrad_out,
    cent_out,
    gain_out,
    shift_out,
    up_out,
    ub_out,
    down_out,
    db_out,
    mass_out,
    load_out,
    cent_s,
    rows_s,
    vec_s,
    up_wide,
    down_wide,
    sem,
    up_sem,
    down_sem,
):
    leaving = []

    def leave(src, dst, semaphore):
        move = pltpu.make_async_copy(src, dst, semaphore)
        move.start()
        leaving.append(move)

    def widen(ref, wide, dst, semaphore, t):
        at = pl.ds(t * COL_STEP, COL_STEP)
        wide[1, at] = ref[at].astype(F32)
        leave(wide.at[1, at], dst.at[1, 0, at], semaphore.at[1, t])

    def multiply(left, right, wide, dst, semaphore, t):
        at = pl.ds(t * COL_STEP, COL_STEP)
        wide[0, at] = dot(left[:, at], right[...], TN)
        leave(wide.at[0, at], dst.at[0, 0, at], semaphore.at[0, t])

    leave(mixed_ref, mixed_out, sem.at[0])
    leave(tgrad_ref, tgrad_out, sem.at[1])
    for t in range(down_wide.shape[1] // COL_STEP):
        widen(down_ref, down_wide, down_out, down_sem, t)
        multiply(a_0, hg_0, down_wide, down_out, down_sem, t)
    for t in range(up_wide.shape[1] // COL_STEP):
        widen(up_ref, up_wide, up_out, up_sem, t)
        multiply(n_0, d_0, up_wide, up_out, up_sem, t)

    def column_sums(ref):
        return jnp.sum(ref[...].astype(F32), axis=0, keepdims=True)

    for i in range(cent_s.shape[1] // 128):
        cent_s[:, i * 128 : (i + 1) * 128] = totals_ref[:, i]
    leave(cent_s, cent_out, sem.at[2])
    for j in range(2):
        rows_s[0, j] = small_ref[j : j + 1]
        rows_s[1, j] = small_ref[2 + j : 3 + j]
    rows_s[2, 0] = column_sums(d_0)
    rows_s[2, 1] = small_ref[5:6]
    rows_s[3, 0] = column_sums(hg_0)
    rows_s[3, 1] = small_ref[4:5]
    for n, dst in enumerate((gain_out, shift_out, ub_out, db_out)):
        leave(rows_s.at[n], dst, sem.at[3 + n])
    experts = totals_ref.shape[0]
    diagonal = lax.broadcasted_iota(jnp.int32, (experts, 128), 0) == lax.broadcasted_iota(
        jnp.int32, (experts, 128), 1
    )
    for i, (dst, n) in enumerate(((mass_out, 8), (load_out, 9))):
        values = jnp.sum(jnp.where(diagonal, totals_ref[:, n], 0.0), axis=0)
        vec_s[i, 0:experts] = values[0:experts] / jnp.float32(denominator)
        leave(vec_s.at[i], dst, sem.at[7 + i])
    for move in leaving:
        move.wait()


def per_device_fused(
    tokens,
    lengths,
    expert_ids,
    slots,
    centroids,
    sublayer_norm_gain,
    sublayer_norm_bias,
    up_weight,
    up_bias,
    down_weight,
    down_bias,
    cotangent,
):
    if not fused_fits(tokens, centroids, up_weight):
        return per_device(
            tokens,
            lengths,
            expert_ids,
            slots,
            centroids,
            sublayer_norm_gain,
            sublayer_norm_bias,
            up_weight,
            up_bias,
            down_weight,
            down_bias,
            cotangent,
        )
    tok_rows, width = tokens.shape
    groups = lax.axis_size("expert")
    batches = lax.axis_size("batch")
    experts = centroids.shape[0]
    capacity = tok_rows // experts
    hidden = up_weight.shape[3]
    chunks = 4
    total = groups * batches * capacity
    def flat(values):
        return values.reshape(values.shape[0], -1)

    vmem = pl.BlockSpec(memory_space=pltpu.VMEM)
    hbm = pl.BlockSpec(memory_space=pl.ANY)
    outs = pl.pallas_call(
        functools.partial(fused_kernel, groups, capacity, chunks),
        out_shape=[
            pltpu.VMEM((tok_rows, width), BF16),
            pltpu.VMEM((tok_rows, width), BF16),
            pltpu.VMEM((groups, 16, 128), F32),
            pltpu.VMEM((8, width), F32),
            pltpu.VMEM(up_weight.shape[2:], BF16),
            pltpu.VMEM(down_weight.shape[2:], BF16),
            pltpu.VMEM((total, width), BF16),
            pltpu.VMEM((total, hidden), BF16),
            pltpu.VMEM((total, hidden), BF16),
            pltpu.VMEM((total, width), BF16),
        ],
        in_specs=[pl.BlockSpec(memory_space=pltpu.HBM)] * 11,
        out_specs=[vmem] * 10,
        scratch_shapes=[
            pltpu.VMEM((1, tok_rows), jnp.int32),
            pltpu.VMEM((1, tok_rows), jnp.int32),
            pltpu.VMEM((tok_rows, width), BF16),
            pltpu.VMEM((tok_rows, width), BF16),
            pltpu.VMEM((experts, width), BF16),
            pltpu.VMEM((2, width), BF16),
            pltpu.VMEM((2, width), BF16),
            pltpu.VMEM((2, hidden), BF16),
            pltpu.VMEM((2, width), BF16),
            pltpu.VMEM((2, width, hidden), BF16),
            pltpu.VMEM((2, hidden, width), BF16),
            pltpu.VMEM((tok_rows, tok_rows), BF16),
            pltpu.VMEM((tok_rows, width), BF16),
            pltpu.VMEM((tok_rows, width), BF16),
            pltpu.VMEM((total, width), BF16),
            pltpu.VMEM((total, width), BF16),
            pltpu.VMEM((total, width), BF16),
            pltpu.VMEM((total, width), BF16),
            pltpu.VMEM((total, width), BF16),
            pltpu.VMEM((total, hidden), BF16),
            pltpu.VMEM((total, hidden), BF16),
            pltpu.VMEM((2, total, width), BF16),
            pltpu.VMEM((2, total // 2, width), BF16),
            pltpu.VMEM((2, total // 2, width), BF16),
            pltpu.VMEM((2, total // 2, width), BF16),
            pltpu.VMEM((2, total // 4, width), BF16),
            pltpu.VMEM((2, total // 4, width), BF16),
            pltpu.VMEM((tok_rows, width), BF16),
            pltpu.VMEM((tok_rows, 128), F32),
            pltpu.VMEM((tok_rows, 128), F32),
            pltpu.VMEM((2, tok_rows, width), BF16),
            pltpu.VMEM((2, tok_rows, width), BF16),
            pltpu.VMEM((8, width), F32),
            pltpu.VMEM((8, width), F32),
            pltpu.VMEM((8, width), F32),
            pltpu.VMEM((2, 3, 3 * width // 128 + 8, 128), F32),
            pltpu.VMEM((groups, 16, 128), F32),
            pltpu.SemaphoreType.DMA((9,)),
            pltpu.SemaphoreType.DMA((4,)),
            pltpu.SemaphoreType.DMA((len(ROUTE_KINDS), groups)),
            pltpu.SemaphoreType.DMA((len(ROUTE_KINDS), groups)),
            pltpu.SemaphoreType.DMA((len(LINK_KINDS), groups)),
            pltpu.SemaphoreType.DMA((len(LINK_KINDS), groups)),
            pltpu.SemaphoreType.DMA((len(CORE_KINDS), chunks)),
            pltpu.SemaphoreType.DMA((len(CORE_KINDS), chunks)),
            pltpu.SemaphoreType.DMA((2, 2)),
            pltpu.SemaphoreType.DMA((2, 2)),
        ],
        compiler_params=pltpu.CompilerParams(
            collective_id=0, has_side_effects=True, vmem_limit_bytes=46 << 20
        ),
        cost_estimate=pl.CostEstimate(
            flops=24 * total * width * hidden, bytes_accessed=40 << 20, transcendentals=0
        ),
    )(
        expert_ids.reshape(1, tok_rows),
        slots.reshape(1, tok_rows),
        tokens,
        cotangent,
        centroids,
        flat(sublayer_norm_gain),
        flat(sublayer_norm_bias),
        flat(up_bias),
        flat(down_bias),
        up_weight,
        down_weight,
    )
    layers = up_weight.shape[0]
    row = jax.ShapeDtypeStruct((layers, 1, width), F32)
    return pl.pallas_call(
        functools.partial(widen_kernel, capacity * groups * batches),
        out_shape=[
            jax.ShapeDtypeStruct(tokens.shape, BF16),
            jax.ShapeDtypeStruct(tokens.shape, BF16),
            jax.ShapeDtypeStruct((experts, width), F32),
            row,
            row,
            jax.ShapeDtypeStruct(up_weight.shape, F32),
            jax.ShapeDtypeStruct((layers, 1, hidden), F32),
            jax.ShapeDtypeStruct(down_weight.shape, F32),
            row,
            jax.ShapeDtypeStruct((experts,), F32),
            jax.ShapeDtypeStruct((experts,), F32),
        ],
        in_specs=[vmem] * 10,
        out_specs=[hbm] * 11,
        scratch_shapes=[
            pltpu.VMEM((experts, width), F32),
            pltpu.VMEM((4, layers, 1, width), F32),
            pltpu.VMEM((2, experts), F32),
            pltpu.VMEM((layers, width, hidden), F32),
            pltpu.VMEM((layers, hidden, width), F32),
            pltpu.SemaphoreType.DMA((9,)),
            pltpu.SemaphoreType.DMA((layers, width // COL_STEP)),
            pltpu.SemaphoreType.DMA((layers, hidden // COL_STEP)),
        ],
        compiler_params=pltpu.CompilerParams(vmem_limit_bytes=24 << 20),
        cost_estimate=pl.CostEstimate(
            flops=0, bytes_accessed=12 * layers * width * hidden, transcendentals=0
        ),
    )(*(pltpu.with_memory_space_constraint(out, pltpu.VMEM) for out in outs))


def solution(mesh):
    in_specs = (
        P(("expert", "batch"), None),
        P(("expert", "batch")),
        P(("expert", "batch")),
        P(("expert", "batch")),
        P(),
        P(None, "expert", None),
        P(None, "expert", None),
        P(None, "expert", None, "batch"),
        P(None, "expert", "batch"),
        P(None, "expert", "batch", None),
        P(None, "expert", None),
        P(("expert", "batch"), None),
    )
    out_specs = (
        P(("expert", "batch"), None),
        P(("expert", "batch"), None),
        P(),
        P(None, "expert", None),
        P(None, "expert", None),
        P(None, "expert", None, "batch"),
        P(None, "expert", "batch"),
        P(None, "expert", "batch", None),
        P(None, "expert", None),
        P(),
        P(),
    )
    return jax.shard_map(
        per_device_fused, mesh=mesh, in_specs=in_specs, out_specs=out_specs, check_vma=False
    )
```
